32 devices in a mesh: pair: 2 (over x), dp: 16 (over z, y, core).
Axes of the slice: x: 2, y: 2, z: 4, core: 2. Of those that a mesh axis runs over, the one named last changes fastest.
Arguments:
- states: bfloat16 [2, 18944, 512], P('pair', 'dp'), may hold values from -6 to 6
- norm_gains: bfloat16 [2, 512, 2], P('pair'), may hold values from 0.5 to 1.5
- w_qkv: bfloat16 [2, 512, 1536], P('pair'), may hold values from -0.25 to 0.25
- w_out: bfloat16 [2, 512, 512], P('pair'), may hold values from -2 to 2
- w_up: bfloat16 [2, 512, 2048], P('pair'), may hold values from -0.25 to 0.25
- w_down: bfloat16 [2, 2048, 512], P('pair'), may hold values from -0.125 to 0.125
- w_head: bfloat16 [2, 512, 256], P('pair'), may hold values from -0.25 to 0.25
- task_ids: int32 [64], P('dp'), may hold values from 0 to 31
- chosen: int32 [18944], P('dp'), may hold values from 0 to 255
- reward: int32 [18944], P('dp'), may hold values 0 or 1
- finished: int32 [18944], P('dp'), may hold values 0 or 1
Outputs:
- q_values: bfloat16 [18944, 256], P('dp', 'pair')
- grad_states: bfloat16 [18944, 512], P('dp', 'pair')
- grad_gains: float32 [512, 2], P('dp', 'pair')
- grad_qkv: float32 [512, 1536], P('dp', 'pair')
- grad_out: float32 [512, 512], P('dp', 'pair')
- grad_up: float32 [512, 2048], P('dp', 'pair')
- grad_down: float32 [2048, 512], P('dp', 'pair')
- grad_head: float32 [512, 256], P('dp', 'pair')
- new_gains: float32 [512, 2], P('dp', 'pair')
- new_qkv: float32 [512, 1536], P('dp', 'pair')
- new_out: float32 [512, 512], P('dp', 'pair')
- new_up: float32 [512, 2048], P('dp', 'pair')
- new_down: float32 [2048, 512], P('dp', 'pair')
- new_head: float32 [512, 256], P('dp', 'pair')
- stats: float32 [5], replicated
The draws below stay inside these ranges and needn't reach their ends.
All inputs are finite; a program needn't handle non-finite values. No bound on the sum of `reward` or of `finished` on one device may be relied on, other than what follows from the above.
Results may differ from the reference program's by a relative error of at most 0.012.
Values may be sent and summed in bfloat16 or wider, within the bound.
A program may use at most 192 MiB of HBM per device.

```python
import math
import jax
import jax.numpy as jnp
import numpy as np
from jax import lax

D = 512
HEAD_DIM = 64
FF = 2048
BINS = 256
L = 296
TASKS = 32
SEQ_DEV = 4
SEQS = 64
TOKENS = 18944
N_DP = 16


def touch_ends(entries, rng, smallest, top_value):
    index_at = [jax.random.randint(jax.random.fold_in(rng, axis), (), 0, length) for axis, length in enumerate(entries.shape)]
    longest = entries.shape.index(max(entries.shape))
    beside = index_at[:longest] + [(index_at[longest] + 1) % entries.shape[longest]] + index_at[longest + 1:]
    return entries.at[tuple(index_at)].set(smallest).at[tuple(beside)].set(top_value)


def levels(stream_key, shape, cuts, least, largest):
    gain, own = 1.0, jax.random.fold_in(stream_key, 6)
    for axis_at, blocks in cuts:
        heights = jnp.exp(jax.random.uniform(jax.random.fold_in(own, axis_at), (blocks,), jnp.float32, least / len(cuts), largest / len(cuts)))
        gain = gain * jnp.repeat(heights, shape[axis_at] // blocks).reshape([-1 if axis == axis_at else 1 for axis in range(len(shape))])
    return gain


def cumulative_ranks(number_of, skew):
    weights = [(1 << 20) // math.isqrt(standing ** skew) + 1 for standing in range(1, number_of + 1)]
    deviation = 1 + sum(weights) // (1 << 30)
    return np.cumsum(np.array([max(1, weight // deviation) for weight in weights]))


def ranked_ids(own_key, dims, count, skew):
    listing = cumulative_ranks(count, skew)
    pick = jax.random.randint(jax.random.fold_in(own_key, 1), dims, 0, int(listing[count - 1]))
    standing = jnp.searchsorted(jnp.asarray(listing, jnp.int32), pick, side="right")
    return jax.random.permutation(jax.random.fold_in(own_key, 2), count)[standing].astype(jnp.int32)


def bell_draw(key, shape, width, limit, split=(), kind=jnp.bfloat16):
    gain = levels(key, shape, split, -0.22, 0.18) if split else 1.0
    values = jax.random.normal(key, shape, jnp.float32) * width * gain
    return jnp.minimum(jnp.maximum(values, -limit), limit).astype(kind)


def setup_inputs(seed: int = 0) -> dict:
    key_list = jax.random.split(jax.random.key(seed), 12)
    return {
        "states": bell_draw(key_list[0], (2, TOKENS, D), 1.0, 6.0, ((0, 2), (1, 16))),
        "norm_gains": jnp.clip(1.0 + 0.1 * jax.random.normal(key_list[1], (2, D, 2), jnp.float32), 0.5, 1.5).astype(jnp.bfloat16),
        "w_qkv": bell_draw(key_list[2], (2, D, 3 * D), D ** -0.5, 0.25, ((0, 2),)),
        "w_out": bell_draw(key_list[3], (2, D, D), (D // 64) ** -0.5, 2.0, ((0, 2),)),
        "w_up": bell_draw(key_list[4], (2, D, FF), D ** -0.5, 0.25, ((0, 2),)),
        "w_down": bell_draw(key_list[5], (2, FF, D), FF ** -0.5, 0.125, ((0, 2),)),
        "w_head": bell_draw(key_list[6], (2, D, BINS), D ** -0.5, 0.25, ((0, 2),)),
        "task_ids": touch_ends(ranked_ids(key_list[7], (SEQS,), TASKS, 2), jax.random.fold_in(key_list[7], 3), 0, TASKS - 1).astype(jnp.int32),
        "chosen": touch_ends(jax.random.randint(key_list[8], (TOKENS,), 0, BINS), jax.random.fold_in(key_list[8], 1), 0, BINS - 1).astype(jnp.int32),
        "reward": touch_ends((jax.random.randint(key_list[9], (TOKENS,), 0, 4) < 1).astype(jnp.int32), jax.random.fold_in(key_list[9], 1), 0, 1),
        "finished": touch_ends((jax.random.randint(key_list[10], (TOKENS,), 0, 8) < 1).astype(jnp.int32), jax.random.fold_in(key_list[10], 1), 0, 1),
    }


EPSILON = 1e-06
DISCOUNT = 0.98
SOFT_RATE = 0.2
SCORE_SCALE = 0.125
NEG_LARGE = -1000000000.0
HIGHEST = lax.Precision.HIGHEST

@jax.custom_vjp
def low(v):
    return lax.optimization_barrier(v.astype(jnp.bfloat16)).astype(jnp.float32)

@jax.custom_vjp
def low_back(v):
    return v

def low_keep(v):
    return (low(v), None)

def low_pass(kept, grad):
    return (grad,)

def back_keep(v):
    return (v, None)

def back_low(kept, grad):
    return (low(grad),)
low.defvjp(low_keep, low_pass)
low_back.defvjp(back_keep, back_low)

def matmul(left, right):
    return jnp.dot(left, right, precision=HIGHEST)

def normalize(values, gain_row):
    return values * lax.rsqrt(lax.optimization_barrier(jnp.mean(values * values, axis=-1, keepdims=True)) + EPSILON) * gain_row

def attention(qkv_rows, seq_count):
    heads_here = qkv_rows.shape[1] // (3 * HEAD_DIM)
    shaped = qkv_rows.reshape(seq_count, L, 3, heads_here, HEAD_DIM)
    queries = shaped[:, :, 0]
    key_rows = shaped[:, :, 1]
    value_rows = shaped[:, :, 2]
    scores = low_back(jnp.einsum('sqhd,skhd->shqk', queries, key_rows, precision=HIGHEST) * SCORE_SCALE)
    causal = lax.broadcasted_iota(jnp.int32, (L, L), 0) >= lax.broadcasted_iota(jnp.int32, (L, L), 1)
    probs = low(jax.nn.softmax(jnp.where(causal, scores, NEG_LARGE), axis=-1))
    mixed = jnp.einsum('shqk,skhd->sqhd', probs, value_rows, precision=HIGHEST)
    return mixed.reshape(seq_count * L, heads_here * HEAD_DIM)

def layer(params, tokens):
    gain_pair, w_qkv, w_out, w_up, w_down, w_head = params
    seq_count = tokens.shape[0] // L
    normed_one = low(normalize(tokens, gain_pair[:, 0]))
    qkv_rows = low_back(low(matmul(normed_one, w_qkv)))
    attended = low_back(low(attention(qkv_rows, seq_count)))
    middle = tokens + low_back(matmul(attended, w_out))
    normed_two = low(normalize(middle, gain_pair[:, 1]))
    upper = low_back(matmul(normed_two, w_up))
    active = low(jax.nn.gelu(upper))
    final_rows = middle + low_back(matmul(active, w_down))
    return low_back(matmul(low(final_rows), w_head))

def reference(states, norm_gains, w_qkv, w_out, w_up, w_down, w_head, task_ids, chosen, reward, finished):
    stacked = tuple((weight.astype(jnp.float32) for weight in (norm_gains, w_qkv, w_out, w_up, w_down, w_head)))
    online = tuple((weight[0] for weight in stacked))
    target = tuple((weight[1] for weight in stacked))
    block_rows = SEQ_DEV * L
    current = states[0].astype(jnp.float32).reshape(N_DP, block_rows, D)
    following = states[1].astype(jnp.float32).reshape(N_DP, block_rows, D)

    def target_block(block):
        return lax.optimization_barrier(jnp.max(layer(target, block), axis=1))
    next_max = lax.map(target_block, following).reshape(TOKENS)
    bootstrap = reward.astype(jnp.float32) + DISCOUNT * (1.0 - finished.astype(jnp.float32)) * next_max
    table = (task_ids[:, None] == jnp.arange(TASKS, dtype=jnp.int32)[None, :]).astype(jnp.float32)
    counts = lax.optimization_barrier(jnp.sum(table, axis=0))
    seq_weight = SEQS / (TASKS * lax.optimization_barrier(jnp.sum(table * counts[None, :], axis=1)))
    row_weight = jnp.broadcast_to(seq_weight[:, None], (SEQS, L)).reshape(N_DP, block_rows)
    bins_iota = jnp.arange(BINS, dtype=jnp.int32)
    picks = chosen.reshape(N_DP, block_rows)
    aims = bootstrap.reshape(N_DP, block_rows)

    def online_block(carry, block):
        grad_sums, loss_sum, max_sum, max_top = carry
        tokens, aim_rows, weight_rows, pick_rows = block

        def objective(params, inputs):
            qvals = layer(params, inputs)
            picked = lax.optimization_barrier(jnp.sum(jnp.where(pick_rows[:, None] == bins_iota[None, :], qvals, 0.0), axis=1))
            differ = picked - aim_rows
            return (jnp.sum(weight_rows * 0.5 * differ * differ), qvals)
        loss, back_fn, qvals = jax.vjp(objective, online, tokens, has_aux=True)
        grad_params, grad_tokens = back_fn(jnp.ones_like(loss))
        row_top = lax.optimization_barrier(jnp.max(qvals, axis=1))
        grad_sums = jax.tree.map(jnp.add, grad_sums, grad_params)
        carry = (grad_sums, loss_sum + loss, max_sum + jnp.sum(row_top), jnp.maximum(max_top, jnp.max(row_top)))
        return (carry, (qvals.astype(jnp.bfloat16), grad_tokens.astype(jnp.bfloat16)))
    start = (tuple((jnp.zeros(weight.shape, jnp.float32) for weight in online)), jnp.zeros((), jnp.float32), jnp.zeros((), jnp.float32), jnp.full((), -1e+30, jnp.float32))
    final_carry, outputs = lax.scan(online_block, start, (current, aims, row_weight, picks))
    grad_sums, loss_sum, max_sum, max_top = final_carry
    q_values = outputs[0].reshape(TOKENS, BINS)
    grad_states = outputs[1].reshape(TOKENS, D)
    averaged = tuple((target_w + SOFT_RATE * (online_w - target_w) for online_w, target_w in zip(online, target)))
    stats = jnp.stack([loss_sum / TOKENS, max_sum / TOKENS, max_top, jnp.sum(next_max) / TOKENS, jnp.max(next_max)])
    return (q_values, grad_states, grad_sums[0], grad_sums[1], grad_sums[2], grad_sums[3], grad_sums[4], grad_sums[5], averaged[0], averaged[1], averaged[2], averaged[3], averaged[4], averaged[5], stats)
```

```python
import functools

import jax
import jax.numpy as jnp
from jax import lax
from jax.experimental import pallas as pl
from jax.experimental.pallas import tpu as pltpu
from jax.sharding import PartitionSpec as P

F32 = jnp.float32
BF16 = jnp.bfloat16
MESH = pl.DeviceIdType.MESH

HEAD_DIM = 64
L = 296
LP = 304
TASKS = 32
EPSILON = 1e-06
DISCOUNT = 0.98
SOFT_RATE = 0.2
SCORE_SCALE = 0.125
NEG_LARGE = -1000000000.0
LOWEST = -1e30

BLOCKS = ((0, 128, 128), (128, 128, 256), (256, 48, 304))


def dot_nn(a, b):
    return lax.dot_general(a, b, (((1,), (0,)), ((), ())), preferred_element_type=F32)


def dot_nt(a, b):
    return lax.dot_general(a, b, (((1,), (1,)), ((), ())), preferred_element_type=F32)


def dot_tn(a, b):
    return lax.dot_general(a, b, (((0,), (0,)), ((), ())), preferred_element_type=F32)


def dot_tt(a, b):
    return lax.dot_general(a, b, (((0,), (1,)), ((), ())), preferred_element_type=F32)


def inverse_rms(values):
    return lax.rsqrt(jnp.mean(values * values, axis=-1, keepdims=True) + EPSILON)


def gelu_and_slope(u):
    c = 0.7978845608028654
    square = u * u
    t = jnp.tanh(u * (c + (c * 0.044715) * square))
    half = 0.5 * t + 0.5
    slope = half + (u * (0.5 - 0.5 * t * t)) * (c + (3 * c * 0.044715) * square)
    return u * half, slope


def lane_halves(a):
    lane = lax.broadcasted_iota(jnp.int32, (1, 2 * HEAD_DIM), 1)
    zero = jnp.zeros((), a.dtype)
    return jnp.where(lane < HEAD_DIM, a, zero), jnp.where(lane >= HEAD_DIM, a, zero)


def rows_of(ref, first, width):
    value = ref[:, :, first : first + width]
    return value.reshape(value.shape[0] * value.shape[1], width)


class Names:
    pass


def forward_sequence(n, s, d):
    x = n.x[s].astype(F32)
    normed = (x * inverse_rms(x) * n.gains[0:1, :]).astype(BF16)
    n.normed_one[s] = normed
    for first in range(0, 3 * d, 256):
        n.qkv[s, :, first : first + 256] = dot_nn(
            normed, n.w_qkv[:, first : first + 256]
        ).astype(BF16)
    corner = lax.broadcasted_iota(jnp.int32, (128, 128), 0) >= lax.broadcasted_iota(
        jnp.int32, (128, 128), 1
    )
    for pair in range(d // 128):
        at = 128 * pair
        queries = lane_halves(n.qkv[s, :, at : at + 128] * jnp.array(SCORE_SCALE, BF16))
        keys = n.qkv[s, :, d + at : d + at + 128]
        values = lane_halves(n.qkv[s, :, 2 * d + at : 2 * d + at + 128])
        for block, (first, rows, seen) in enumerate(BLOCKS):
            mixed = None
            for head in range(2):
                raw = dot_nt(queries[head][first : first + rows], keys[:seen])
                diagonal = jnp.where(corner[:rows, :rows], raw[:, first:], NEG_LARGE)
                scores = jnp.concatenate([raw[:, :first], diagonal], axis=1) if first else diagonal
                largest = jnp.max(scores, axis=-1, keepdims=True)
                raised = jnp.exp(scores - largest)
                totals = jnp.sum(raised, axis=-1, keepdims=True)
                probs = (raised * (1.0 / totals)).astype(BF16)
                n.probs[block][s, 2 * pair + head] = probs
                part = dot_nn(probs, values[head][:seen])
                mixed = part if mixed is None else mixed + part
            n.attended[s, first : first + rows, at : at + 128] = mixed.astype(BF16)
    middle = x + dot_nn(n.attended[s], n.w_out[...])
    n.middle[s] = middle
    normed = (middle * inverse_rms(middle) * n.gains[1:2, :]).astype(BF16)
    n.normed_two[s] = normed
    ff = n.w_up.shape[1]
    for first in range(0, ff, 256):
        active, slope = gelu_and_slope(dot_nn(normed, n.w_up[:, first : first + 256]))
        n.active[s, :, first : first + 256] = active.astype(BF16)
        n.slope[s, :, first : first + 256] = slope.astype(BF16)
    final_low = (n.middle[s] + dot_nn(n.active[s], n.w_down[...])).astype(BF16)
    n.final_low[s] = final_low
    n.q_rows[s] = dot_nn(final_low, n.w_head[...]).astype(BF16)
    q_columns = dot_tt(n.w_head[...], final_low)
    bins = lax.broadcasted_iota(jnp.int32, q_columns.shape, 0)
    chosen = n.aux[s, 0:1, :].astype(jnp.int32)
    n.picked[pl.ds(s, 1), :] = jnp.sum(
        jnp.where(bins == chosen, q_columns, 0.0), axis=0, keepdims=True
    )
    n.tops[pl.ds(s, 1), :] = jnp.max(q_columns, axis=0, keepdims=True)


def backward_ffn(n, s):
    bins = lax.broadcasted_iota(jnp.int32, (n.w_head.shape[1], LP), 0)
    chosen = n.aux[s, 0:1, :].astype(jnp.int32)
    grad_q = jnp.where(bins == chosen, n.coef[pl.ds(s, 1), :], 0.0).astype(BF16)
    n.grad_q[s] = grad_q
    grad_final = dot_tt(grad_q, n.w_head[...])
    grad_ffn = grad_final.astype(BF16)
    n.grad_ffn[s] = grad_ffn
    ff = n.w_up.shape[1]
    for first in range(0, ff, 256):
        grad_active = dot_nt(grad_ffn, n.w_down[first : first + 256, :])
        n.slope[s, :, first : first + 256] = (
            grad_active * n.slope[s, :, first : first + 256].astype(F32)
        ).astype(BF16)
    grad_two = dot_nt(n.slope[s], n.w_up[...])
    middle = n.middle[s]
    inverse = inverse_rms(middle)
    normal = middle * inverse
    n.gain_sums[1] += jnp.sum((grad_two * normal).reshape(LP // 8, 8, -1), axis=0)
    inner = grad_two * n.gains[1:2, :]
    grad_middle = grad_final + inverse * (
        inner - normal * jnp.mean(inner * normal, axis=-1, keepdims=True)
    )
    n.middle[s] = grad_middle
    grad_branch = grad_middle.astype(BF16)
    n.grad_branch[s] = grad_branch
    n.grad_mixed[s] = dot_nt(grad_branch, n.w_out[...]).astype(BF16)


def backward_attention(n, s, d):
    lane = lax.broadcasted_iota(jnp.int32, (1, 128), 1)
    for pair in range(d // 128):
        at = 128 * pair
        values = n.qkv[s, :, 2 * d + at : 2 * d + at + 128]
        grad_mixed = n.grad_mixed[s, :, at : at + 128]
        product = n.attended[s, :, at : at + 128].astype(F32) * grad_mixed.astype(F32)
        centres = (
            jnp.sum(jnp.where(lane < HEAD_DIM, product, 0.0), axis=-1, keepdims=True),
            jnp.sum(jnp.where(lane >= HEAD_DIM, product, 0.0), axis=-1, keepdims=True),
        )
        queries = lane_halves(n.qkv[s, :, at : at + 128])
        keys = lane_halves(n.qkv[s, :, d + at : d + at + 128])
        grads = lane_halves(grad_mixed)
        grad_keys = [None] * 3
        grad_values = [None] * 3
        for block, (first, rows, seen) in enumerate(BLOCKS):
            grad_queries = None
            for head in range(2):
                probs = n.probs[block][s, 2 * pair + head]
                here = grads[head][first : first + rows]
                grad_probs = dot_nt(here, values[:seen])
                grad_scores = (
                    probs.astype(F32) * (grad_probs - centres[head][first : first + rows])
                ).astype(BF16)
                part = dot_nn(grad_scores, keys[head][:seen])
                grad_queries = part if grad_queries is None else grad_queries + part
                of_values = dot_tn(probs, here)
                of_keys = dot_tn(grad_scores, queries[head][first : first + rows])
                for i, start in enumerate((0, 128, 256)):
                    if start < seen:
                        end = min(start + 128, seen)
                        piece = of_values[start:end]
                        grad_values[i] = piece if grad_values[i] is None else grad_values[i] + piece
                        piece = of_keys[start:end]
                        grad_keys[i] = piece if grad_keys[i] is None else grad_keys[i] + piece
            n.qkv[s, first : first + rows, at : at + 128] = (grad_queries * SCORE_SCALE).astype(
                BF16
            )
        for i, (first, rows, _) in enumerate(BLOCKS):
            n.qkv[s, first : first + rows, d + at : d + at + 128] = (
                grad_keys[i] * SCORE_SCALE
            ).astype(BF16)
            n.qkv[s, first : first + rows, 2 * d + at : 2 * d + at + 128] = grad_values[i].astype(
                BF16
            )
    grad_one = dot_nt(n.qkv[s], n.w_qkv[...])
    x = n.x[s].astype(F32)
    inverse = inverse_rms(x)
    normal = x * inverse
    n.gain_sums[0] += jnp.sum((grad_one * normal).reshape(LP // 8, 8, -1), axis=0)
    inner = grad_one * n.gains[0:1, :]
    n.grad_states[s] = (
        n.middle[s]
        + inverse * (inner - normal * jnp.mean(inner * normal, axis=-1, keepdims=True))
    ).astype(BF16)


TENSORS = ("down", "up", "out", "head", "qkv")
SEMAPHORES = 96


def layer_kernel(names, data_count, inside, *refs):
    n = Names()
    for name, ref in zip(names, refs):
        setattr(n, name, ref)
    n.probs = (n.probs_0, n.probs_1, n.probs_2)
    d = n.x.shape[2]
    ff = n.w_up.shape[1]
    seq_count = n.x.shape[0]

    me_pair = lax.axis_index("pair")
    me = lax.axis_index("dp")
    other = 1 - me_pair
    core = me % 2
    row = (me // 2) % 2
    low = (me // 4) % 2
    high = me // 8
    sibling = (me_pair, me + 1 - 2 * core)
    beside = (me_pair, me + 2 - 4 * row)
    near = (me_pair, me + 4 - 8 * low)
    partner = (other, me)
    quarter = me // 4

    def at_quarter(which, pair):
        return (pair, me + 4 * (which - quarter))

    def at_mixed(which, pair):
        return (pair, me + 8 * (which // 2 - high) + 2 * (which % 2 - row))

    used = [0]
    sent = []

    def slot():
        used[0] += 1
        return used[0] - 1

    def copy(src, dst, sem, device):
        return pltpu.make_async_remote_copy(
            src_ref=src,
            dst_ref=dst,
            send_sem=n.send_sem.at[sem],
            recv_sem=n.recv_sem.at[sem],
            device_id=device,
            device_id_type=MESH,
        )

    online = me_pair == 0

    barrier = pltpu.get_barrier_semaphore()
    friends = [partner]
    if inside:
        friends += [sibling, beside]
        for offset in range(1, 4):
            place = (quarter + offset) % 4
            friends += [at_quarter(place, me_pair), at_quarter(place, other)]
        friends += [
            (pair, me + 8 * (1 - 2 * high) + 2 * (1 - 2 * row)) for pair in (me_pair, other)
        ]
        friends += [(other, beside[1])]
    for friend in friends:
        pl.semaphore_signal(barrier, inc=1, device_id=friend, device_id_type=MESH)

    weight_refs = (n.w_qkv, n.w_out, n.w_up, n.w_down, n.w_head)
    if inside:
        theirs = (n.their_qkv, n.their_out, n.their_up, n.their_down, n.their_head)

    def piece_of(ref, half):
        height = ref.shape[0] // data_count
        width = ref.shape[1] // 2
        return (
            pl.ds(pl.multiple_of(me * height, height), height),
            pl.ds(pl.multiple_of(half * width, width), width),
        )

    weight_sems = [slot() for _ in weight_refs]

    def weight_copy(i):
        return copy(weight_refs[i].at[piece_of(weight_refs[i], other)], theirs[i], weight_sems[i], partner)

    gains_sem = slot()

    def gains_copy():
        return copy(n.gains, n.their_gains, gains_sem, partner)

    count_core, count_row = slot(), slot()
    count_far = [slot() for _ in range(3)]

    def count_copy(step, offset=0):
        if step == 0:
            return copy(n.count_out.at[0], n.count_in.at[0], count_core, sibling)
        if step == 1:
            return copy(n.count_out.at[1], n.count_in.at[1], count_row, beside)
        place = (quarter + offset) % 4
        return copy(
            n.count_out.at[2],
            n.count_in.at[1 + offset],
            count_far[offset - 1],
            at_quarter(place, me_pair),
        )

    n.gain_sums[...] = jnp.zeros_like(n.gain_sums)

    @pl.loop(0, seq_count)
    def _(s):
        forward_sequence(n, s, d)

        @pl.when(s == 0)
        def _():
            pl.semaphore_wait(barrier, len(friends))
            if not inside:
                return
            n.count_out[0] = jnp.broadcast_to(
                jnp.sum(n.table[...], axis=0, keepdims=True), (8, 128)
            )
            count_copy(0).start()
            for i in range(len(weight_refs)):
                weight_copy(i).start()
            gains_copy().start()

        if not inside:
            return

        @pl.when(s == 1)
        def _():
            count_copy(0).wait()
            n.count_out[1] = n.count_out[0] + n.count_in[0]
            count_copy(1).start()

        @pl.when(s == 2)
        def _():
            count_copy(1).wait()
            n.count_out[2] = n.count_out[1] + n.count_in[1]
            for offset in range(1, 4):
                count_copy(2, offset).start()

    lane = lax.broadcasted_iota(jnp.int32, (8, LP), 1)
    seq = lax.broadcasted_iota(jnp.int32, (8, LP), 0)
    real = jnp.logical_and(lane < L, seq < seq_count)
    tops = n.tops[...]
    aims_sem = slot()
    q_sem = slot()
    state_sems = [slot() for _ in range(1)]
    state_sems = state_sems + [slot() for _ in range(seq_count - 1)]

    def aims_copy():
        return copy(n.aims_out, n.aims_in, aims_sem, partner)

    def q_copy():
        return copy(n.q_rows.at[:, :, pl.ds(128, 128)], n.q_half, q_sem, partner)

    def state_copy(s):
        return copy(
            n.grad_states.at[s, :, pl.ds(d // 2, d // 2)],
            n.state_half.at[s],
            state_sems[0] + s,
            partner,
        )

    @pl.when(jnp.logical_not(online))
    def _():
        reward = jnp.concatenate([n.aux[s, 1:2, :] for s in range(seq_count)] * 2, axis=0)
        finished = jnp.concatenate([n.aux[s, 2:3, :] for s in range(seq_count)] * 2, axis=0)
        n.aims_out[...] = reward + DISCOUNT * (1.0 - finished) * tops
        aims_copy().start()

    @pl.when(online)
    def _():
        q_copy().start()

    if inside:
        for i in range(len(weight_refs)):
            weight_copy(i).wait()
            mine = weight_refs[i][piece_of(weight_refs[i], me_pair)].astype(F32)
            received = theirs[i][...].astype(F32)
            first = jnp.where(online, mine, received)
            second = jnp.where(online, received, mine)
            (n.new_qkv, n.new_out, n.new_up, n.new_down, n.new_head)[i][...] = second + SOFT_RATE * (
                first - second
            )
        gains_copy().wait()
        first = jnp.where(online, n.gains[...], n.their_gains[...])
        second = jnp.where(online, n.their_gains[...], n.gains[...])
        n.new_gains[...] = second + SOFT_RATE * (first - second)

        for offset in range(1, 4):
            count_copy(2, offset).wait()
        counts = n.count_out[2] + n.count_in[2] + n.count_in[3] + n.count_in[4]
    else:
        counts = n.counts[...]
    seq_weight = (seq_count * data_count) / (
        TASKS * jnp.sum(n.table[...] * counts, axis=1, keepdims=True)
    )

    stat_core, stat_row = slot(), slot()
    stat_far = [slot() for _ in range(7)]
    stat_row_id = lax.broadcasted_iota(jnp.int32, (8, 128), 0)
    stat_lane = lax.broadcasted_iota(jnp.int32, (8, 128), 1)

    def stat_copy(step, k=0):
        if step == 0:
            return copy(n.stat_out.at[0], n.stat_in.at[0], stat_core, sibling)
        if step == 1:
            return copy(n.stat_out.at[1], n.stat_in.at[1], stat_row, beside)
        place = (quarter + (k + 1) % 4) % 4
        pair = me_pair if k < 3 else other
        return copy(n.stat_out.at[2], n.stat_in.at[2 + k], stat_far[k], at_quarter(place, pair))

    def stat_join(a, b):
        return jnp.where(stat_row_id == 1, jnp.maximum(a, b), a + b)

    def stat_first(loss):
        total = jnp.sum(jnp.where(real, tops, 0.0))
        best = jnp.max(jnp.where(real, tops, LOWEST))
        sums = jnp.where(
            stat_lane == 0, loss, jnp.where(stat_lane == 1 + me_pair, total, 0.0)
        )
        bests = jnp.where(stat_lane == me_pair, best, LOWEST)
        n.stat_out[0] = jnp.where(
            stat_row_id == 0, sums, jnp.where(stat_row_id == 1, bests, 0.0)
        )
        if inside:
            stat_copy(0).start()

    def stat_second():
        if not inside:
            return
        stat_copy(0).wait()
        n.stat_out[1] = stat_join(n.stat_out[0], n.stat_in[0])
        stat_copy(1).start()

    def stat_third():
        if not inside:
            return
        stat_copy(1).wait()
        n.stat_out[2] = stat_join(n.stat_out[1], n.stat_in[1])
        for k in range(7):
            stat_copy(2, k).start()

    step_sems = {}
    for name in TENSORS:
        step_sems[name] = (slot(), slot(), [slot() for _ in range(7)])
    along = {"down": "row", "up": "low", "out": "row", "head": "row", "qkv": "row"}
    gain_sems = (slot(), slot(), [slot() for _ in range(7)])

    def core_start(name):
        if inside:
            core_copy(name).start()

    def core_copy(name):
        return copy(
            getattr(n, "g_" + name).at[:, :, :, 1 - core],
            getattr(n, "r1_" + name),
            step_sems[name][0],
            sibling,
        )

    def axis_copy(name):
        r1, r2 = getattr(n, "r1_" + name), getattr(n, "r2_" + name)
        if along[name] == "row":
            return copy(r1.at[:, :, 1 - row], r2, step_sems[name][1], beside)
        return copy(r1.at[:, 1 - low], r2, step_sems[name][1], near)

    def half_of(name, half):
        height, width = getattr(n, "r2_" + name).shape[2:]
        if name == "down":
            return (pl.ds(half * (height // 2), height // 2), slice(None))
        return (slice(None), pl.ds(half * (width // 2), width // 2))

    def far_copy(name, k):
        r2, r3 = getattr(n, "r2_" + name), getattr(n, "r3_" + name)
        offset = (k + 1) % 4
        pair = 0 if k < 3 else 1
        if along[name] == "row":
            place = (quarter + offset) % 4
            device = at_quarter(place, pair)
        else:
            place = (2 * high + row + offset) % 4
            device = at_mixed(place, pair)
        return copy(
            r2.at[(place // 2, place % 2) + half_of(name, pair)],
            r3.at[offset],
            step_sems[name][2][k],
            device,
        )

    def core_done(name):
        if not inside:
            return
        core_copy(name).wait()
        g, r1 = getattr(n, "g_" + name), getattr(n, "r1_" + name)
        for i in range(2):
            for j in range(2):
                for k in range(2):
                    r1[i, j, k] = (g[i, j, k, core].astype(F32) + r1[i, j, k].astype(F32)).astype(
                        BF16
                    )
        axis_copy(name).start()

    def axis_done(name):
        if not inside:
            return
        axis_copy(name).wait()
        r1, r2 = getattr(n, "r1_" + name), getattr(n, "r2_" + name)
        for i in range(2):
            for j in range(2):
                mine = r1[i, j, row] if along[name] == "row" else r1[i, low, j]
                r2[i, j] = (mine.astype(F32) + r2[i, j].astype(F32)).astype(BF16)
        for k in range(7):
            far_copy(name, k).start()

    def owner_online(name):
        if not inside:
            return
        r2, r3 = getattr(n, "r2_" + name), getattr(n, "r3_" + name)
        place = quarter if along[name] == "row" else 2 * high + row
        total = r2[(place // 2, place % 2) + half_of(name, 0)].astype(F32)
        for k in range(3):
            far_copy(name, k).wait_recv()
            total += r3[k + 1].astype(F32)
        getattr(n, "grad_" + name)[...] = total

    def owner_target(name):
        if not inside:
            return
        r3 = getattr(n, "r3_" + name)
        total = None
        for k in range(3, 7):
            far_copy(name, k).wait_recv()
            part = r3[(k + 1) % 4].astype(F32)
            total = part if total is None else total + part
        getattr(n, "grad_" + name)[...] = total

    def gain_copy(step, k=0):
        if step == 0:
            return copy(n.gain_out.at[0], n.gain_in.at[0], gain_sems[0], sibling)
        if step == 1:
            return copy(n.gain_out.at[1], n.gain_in.at[1], gain_sems[1], beside)
        offset = (k + 1) % 4
        pair = 0 if k < 3 else 1
        return copy(
            n.gain_out.at[2],
            n.gain_in.at[2 + offset],
            gain_sems[2][k],
            at_quarter((quarter + offset) % 4, pair),
        )

    @pl.when(online)
    def _():
        aims_copy().wait_recv()
        differ = n.picked[...] - n.aims_in[...]
        weighted = jnp.where(real, seq_weight * differ, 0.0)
        n.coef[...] = weighted
        stat_first(jnp.sum(0.5 * weighted * jnp.where(real, differ, 0.0)))

        @pl.loop(0, seq_count)
        def _(s):
            backward_ffn(n, s)

        stat_second()
        grad_ffn = rows_of(n.grad_ffn, 0, d)

        @pl.loop(0, ff // 256)
        def _(j):
            columns = pl.ds(pl.multiple_of(j * 256, 256), 256)
            value = dot_tn(grad_ffn, n.active[:, :, columns].reshape(seq_count * LP, 256))
            for c in range(2):
                n.g_down[j // 4, (j // 2) % 2, j % 2, c] = value[:, 128 * c : 128 * c + 128].astype(
                    BF16
                )

        core_start("down")
        normed_two = rows_of(n.normed_two, 0, d)

        @pl.loop(0, ff // 256)
        def _(j):
            columns = pl.ds(pl.multiple_of(j * 256, 256), 256)
            value = dot_tn(normed_two, n.slope[:, :, columns].reshape(seq_count * LP, 256))
            n.g_up[:, :, :, :, :, columns] = value.astype(BF16).reshape(2, 2, 2, 2, d // 16, 256)

        core_start("up")
        core_done("down")
        value = dot_tn(rows_of(n.attended, 0, d), rows_of(n.grad_branch, 0, d))
        n.g_out[...] = value.astype(BF16).reshape(n.g_out.shape)
        value = None
        for s in range(seq_count):
            part = dot_nn(n.grad_q[s], n.final_low[s])
            value = part if value is None else value + part
        n.g_head[...] = jnp.transpose(value).astype(BF16).reshape(n.g_head.shape)
        core_start("out")
        core_start("head")
        core_done("up")

        @pl.loop(0, seq_count)
        def _(s):
            backward_attention(n, s, d)
            state_copy(s).start()

            @pl.when(s == 0)
            def _():
                core_done("out")
                core_done("head")
                stat_third()

            @pl.when(s == 2)
            def _():
                axis_done("down")

        n.gain_out[0, 0:1, :] = jnp.sum(n.gain_sums[0], axis=0, keepdims=True)
        n.gain_out[0, 1:2, :] = jnp.sum(n.gain_sums[1], axis=0, keepdims=True)
        n.gain_out[0, 2:8, :] = jnp.zeros((6, d), F32)
        if inside:
            gain_copy(0).start()
        normed_one = rows_of(n.normed_one, 0, d)

        @pl.loop(0, 3 * d // 256)
        def _(j):
            columns = pl.ds(pl.multiple_of(j * 256, 256), 256)
            value = dot_tn(normed_one, n.qkv[:, :, columns].reshape(seq_count * LP, 256))
            n.g_qkv[:, :, :, :, :, columns] = value.astype(BF16).reshape(2, 2, 2, 2, d // 16, 256)

        core_start("qkv")
        axis_done("up")
        core_done("qkv")
        if inside:
            gain_copy(0).wait()
            n.gain_out[1] = n.gain_out[0] + n.gain_in[0]
            gain_copy(1).start()
        axis_done("out")
        axis_done("head")
        owner_online("down")
        if inside:
            gain_copy(1).wait()
            n.gain_out[2] = n.gain_out[1] + n.gain_in[1]
            for k in range(7):
                gain_copy(2, k).start()
        owner_online("up")
        axis_done("qkv")
        for s in range(seq_count):
            n.state_out[s] = n.grad_states[s, :, : d // 2]
        n.q_out[...] = n.q_rows[:, :, :128]
        owner_online("out")
        owner_online("head")
        if inside:
            total = n.gain_out[2]
            for k in range(3):
                gain_copy(2, k).wait_recv()
                total += n.gain_in[3 + k]
            n.grad_gains[...] = total
        else:
            n.grad_gains[...] = n.gain_out[0]
        owner_online("qkv")
        q_copy().wait_send()
        for s in range(seq_count):
            state_copy(s).wait_send()
        if inside:
            for k in range(7):
                for name in TENSORS:
                    far_copy(name, k).wait_send()
                gain_copy(2, k).wait_send()

    @pl.when(jnp.logical_not(online))
    def _():
        stat_first(0.0)
        stat_second()
        stat_third()
        q_copy().wait_recv()
        n.q_out[...] = n.q_half[...]
        for name in TENSORS[:4]:
            owner_target(name)
        for s in range(seq_count):
            state_copy(s).wait_recv()
            n.state_out[s] = n.state_half[s]
        if inside:
            total = None
            for k in range(3, 7):
                gain_copy(2, k).wait_recv()
                part = n.gain_in[2 + (k + 1) % 4]
                total = part if total is None else total + part
            n.grad_gains[...] = total
        owner_target("qkv")
        aims_copy().wait_send()

    if inside:
        for k in range(7):
            stat_copy(2, k).wait()
        joined = n.stat_out[2]
        for k in range(7):
            joined = stat_join(joined, n.stat_in[2 + k])
        n.stats[...] = joined
    else:
        n.stats[...] = n.stat_out[0]
    assert used[0] <= SEMAPHORES


def pad_rows(values, seq_count):
    shaped = values.reshape((seq_count, L) + values.shape[1:])
    return jnp.pad(shaped, ((0, 0), (0, LP - L)) + ((0, 0),) * (shaped.ndim - 2))


def add_outside(out, params, pair_index, data_index, data_count):
    online = pair_index == 0
    other = 1 - pair_index

    def half(matrix, which):
        width = matrix.shape[1] // 2
        return lax.dynamic_slice_in_dim(matrix, which * width, width, 1)

    def piece(matrix, which):
        height = matrix.shape[0] // data_count
        return half(lax.dynamic_slice_in_dim(matrix, data_index * height, height, 0), which)

    def swapped(value):
        return lax.ppermute(value, "pair", [(0, 1), (1, 0)])

    for name in TENSORS:
        grad = out["g_" + name].astype(F32)
        grad = grad.reshape((16,) + grad.shape[4:])
        if name == "down":
            grad = jnp.swapaxes(grad, 1, 2)
        grad = lax.psum_scatter(
            grad.reshape(-1, grad.shape[2]), "dp", scatter_dimension=0, tiled=True
        )
        received = swapped(half(grad, other))
        out["grad_" + name] = jnp.where(online, half(grad, pair_index), received)
    gains = lax.psum(out["grad_gains"], "dp")
    out["grad_gains"] = jnp.where(online, gains, swapped(gains))
    for name, weight in zip(("gains", "qkv", "out", "up", "down", "head"), params):
        if name == "gains":
            weight = jnp.pad(weight.T, ((0, 6), (0, 0)))
            mine, received = weight.astype(F32), swapped(weight).astype(F32)
        else:
            mine = piece(weight, pair_index).astype(F32)
            received = swapped(piece(weight, other)).astype(F32)
        first, second = jnp.where(online, mine, received), jnp.where(online, received, mine)
        out["new_" + name] = second + SOFT_RATE * (first - second)
    sums = lax.psum(out["stats"][0:1], ("pair", "dp"))
    bests = lax.pmax(out["stats"][1:2], ("pair", "dp"))
    out["stats"] = jnp.concatenate([sums, bests])


def local(
    states, norm_gains, w_qkv, w_out, w_up, w_down, w_head, task_ids, chosen, reward, finished
):
    pair_index = lax.axis_index("pair")
    data_index = lax.axis_index("dp")
    data_count = lax.axis_size("dp")
    row_count, d = states.shape[1:]
    ff = w_up.shape[2]
    bin_count = w_head.shape[2]
    seq_count = row_count // L

    x = pad_rows(states[0], seq_count)
    gains = jnp.pad(norm_gains[0].astype(F32).T, ((0, 6), (0, 0)))
    aux = jnp.stack([pad_rows(a, seq_count).astype(F32) for a in (chosen, reward, finished)], axis=1)
    aux = jnp.pad(aux, ((0, 0), (0, 5), (0, 0)))
    table = (task_ids[:, None] == jnp.arange(128, dtype=jnp.int32)[None, :]).astype(F32)
    table = jnp.pad(table, ((0, 8 - seq_count), (0, 0)))

    inside = data_count == 16
    heads = d // HEAD_DIM
    rows = (seq_count, LP, d)
    inputs = dict(
        x=x,
        gains=gains,
        w_qkv=w_qkv[0],
        w_out=w_out[0],
        w_up=w_up[0],
        w_down=w_down[0],
        w_head=w_head[0],
        aux=aux,
        table=table,
    )
    if not inside:
        inputs["counts"] = jnp.broadcast_to(
            lax.psum(jnp.sum(table, axis=0, keepdims=True), "dp"), (8, 128)
        )
    piece = {
        "qkv": (d // 16, 3 * d),
        "out": (d // 16, d),
        "up": (d // 16, ff),
        "head": (d // 16, bin_count),
        "down": (d, ff // 16),
    }
    halves = {
        name: (shape[0] // 2, shape[1]) if name == "down" else (shape[0], shape[1] // 2)
        for name, shape in piece.items()
    }
    new_shapes = dict(halves, down=(ff // 16, d // 2))
    outputs = dict(
        q_out=((seq_count, LP, bin_count // 2), BF16),
        state_out=((seq_count, LP, d // 2), BF16),
        grad_gains=((8, d), F32),
        new_gains=((8, d), F32),
        stats=((8, 128), F32),
    )
    for name in TENSORS:
        if inside:
            outputs["grad_" + name] = (halves[name], F32)
            outputs["new_" + name] = (new_shapes[name], F32)
        else:
            outputs["g_" + name] = ((2, 2, 2, 2) + piece[name], BF16)
    scratch = dict(
        normed_one=(rows, BF16),
        qkv=((seq_count, LP, 3 * d), BF16),
        probs_0=((seq_count, heads) + (BLOCKS[0][1], BLOCKS[0][2]), BF16),
        probs_1=((seq_count, heads) + (BLOCKS[1][1], BLOCKS[1][2]), BF16),
        probs_2=((seq_count, heads) + (BLOCKS[2][1], BLOCKS[2][2]), BF16),
        attended=(rows, BF16),
        middle=(rows, F32),
        normed_two=(rows, BF16),
        active=((seq_count, LP, ff), BF16),
        slope=((seq_count, LP, ff), BF16),
        final_low=(rows, BF16),
        q_rows=((seq_count, LP, bin_count), BF16),
        q_half=((seq_count, LP, bin_count // 2), BF16),
        picked=((8, LP), F32),
        tops=((8, LP), F32),
        coef=((8, LP), F32),
        aims_out=((8, LP), F32),
        aims_in=((8, LP), F32),
        grad_q=((seq_count, bin_count, LP), BF16),
        grad_ffn=(rows, BF16),
        grad_branch=(rows, BF16),
        grad_mixed=(rows, BF16),
        grad_states=(rows, BF16),
        state_half=((seq_count, LP, d // 2), BF16),
        gain_sums=((2, 8, d), F32),
        gain_out=((3, 8, d), F32),
        gain_in=((6, 8, d), F32),
        count_out=((3, 8, 128), F32),
        count_in=((5, 8, 128), F32),
        stat_out=((3, 8, 128), F32),
        stat_in=((9, 8, 128), F32),
        their_gains=((8, d), F32),
    )
    for name in TENSORS if inside else ():
        scratch["g_" + name] = ((2, 2, 2, 2) + piece[name], BF16)
        scratch["r1_" + name] = ((2, 2, 2) + piece[name], BF16)
        scratch["r2_" + name] = ((2, 2) + piece[name], BF16)
        scratch["r3_" + name] = ((4,) + halves[name], BF16)
        scratch["their_" + name] = (new_shapes[name], BF16)
    names = list(inputs) + list(outputs) + list(scratch) + ["send_sem", "recv_sem"]
    in_vmem = pl.BlockSpec(memory_space=pltpu.VMEM)
    raw = pl.pallas_call(
        functools.partial(layer_kernel, names, data_count, inside),
        out_shape=[jax.ShapeDtypeStruct(shape, dtype) for shape, dtype in outputs.values()],
        in_specs=[in_vmem] * len(inputs),
        out_specs=[in_vmem] * len(outputs),
        scratch_shapes=[pltpu.VMEM(shape, dtype) for shape, dtype in scratch.values()]
        + [pltpu.SemaphoreType.DMA((SEMAPHORES,)), pltpu.SemaphoreType.DMA((SEMAPHORES,))],
        compiler_params=pltpu.CompilerParams(
            collective_id=0, has_side_effects=True, vmem_limit_bytes=64 * 1024 * 1024 - 65536
        ),
        name="layer",
    )(*inputs.values())
    out = dict(zip(outputs, raw))
    token_total = row_count * data_count

    def unpad(values):
        return values[:, :L].reshape((row_count,) + values.shape[2:])

    if not inside:
        params = (norm_gains[0], w_qkv[0], w_out[0], w_up[0], w_down[0], w_head[0])
        add_outside(out, params, pair_index, data_index, data_count)
    height = d // data_count

    def gains_piece(values):
        return lax.dynamic_slice(values, (pair_index, data_index * height), (1, height)).reshape(
            height, 1
        )

    stats = jnp.stack(
        [
            out["stats"][0, 0] / token_total,
            out["stats"][0, 1] / token_total,
            out["stats"][1, 0],
            out["stats"][0, 2] / token_total,
            out["stats"][1, 1],
        ]
    )
    return (
        unpad(out["q_out"]),
        unpad(out["state_out"]),
        gains_piece(out["grad_gains"]),
        out["grad_qkv"],
        out["grad_out"],
        out["grad_up"],
        out["grad_down"].T if inside else out["grad_down"],
        out["grad_head"],
        gains_piece(out["new_gains"]),
        out["new_qkv"],
        out["new_out"],
        out["new_up"],
        out["new_down"],
        out["new_head"],
        stats,
    )


def solution(mesh):
    placed = (
        P("pair", "dp", None),
        P("pair", None, None),
        P("pair", None, None),
        P("pair", None, None),
        P("pair", None, None),
        P("pair", None, None),
        P("pair", None, None),
        P("dp"),
        P("dp"),
        P("dp"),
        P("dp"),
    )
    return jax.shard_map(
        local,
        mesh=mesh,
        in_specs=placed,
        out_specs=(P("dp", "pair"),) * 14 + (P(),),
        check_vma=False,
    )
```

```python
import functools

import jax
import jax.numpy as jnp
from jax import lax
from jax.experimental import pallas as pl
from jax.experimental.pallas import tpu as pltpu
from jax.sharding import PartitionSpec as P

F32 = jnp.float32
BF16 = jnp.bfloat16
MESH = pl.DeviceIdType.MESH

HEAD_DIM = 64
L = 296
LP = 304
TASKS = 32
EPSILON = 1e-06
DISCOUNT = 0.98
SOFT_RATE = 0.2
SCORE_SCALE = 0.125
NEG_LARGE = -1000000000.0
LOWEST = -1e30

BLOCKS = ((0, 128, 128), (128, 128, 256), (256, 48, 304))


def dot_nn(a, b):
    return lax.dot_general(a, b, (((1,), (0,)), ((), ())), preferred_element_type=F32)


def dot_nt(a, b):
    return lax.dot_general(a, b, (((1,), (1,)), ((), ())), preferred_element_type=F32)


def dot_tn(a, b):
    return lax.dot_general(a, b, (((0,), (0,)), ((), ())), preferred_element_type=F32)


def dot_tt(a, b):
    return lax.dot_general(a, b, (((0,), (1,)), ((), ())), preferred_element_type=F32)


def inverse_rms(values):
    return lax.rsqrt(jnp.mean(values * values, axis=-1, keepdims=True) + EPSILON)


def gelu_and_slope(u):
    c = 0.7978845608028654
    square = u * u
    t = jnp.tanh(u * (c + (c * 0.044715) * square))
    half = 0.5 * t + 0.5
    slope = half + (u * (0.5 - 0.5 * t * t)) * (c + (3 * c * 0.044715) * square)
    return u * half, slope


def lane_halves(a):
    lane = lax.broadcasted_iota(jnp.int32, (1, 2 * HEAD_DIM), 1)
    zero = jnp.zeros((), a.dtype)
    return jnp.where(lane < HEAD_DIM, a, zero), jnp.where(lane >= HEAD_DIM, a, zero)


def rows_of(ref, first, width):
    value = ref[:, :, first : first + width]
    return value.reshape(value.shape[0] * value.shape[1], width)


def without_pad(ref, s, width):
    rows = [ref[s + i, :, :width].astype(F32)[:L] for i in range(2)]
    return jnp.concatenate(rows, axis=0).astype(BF16)


class Names:
    pass


def in_steps(count, first, second, third):
    for item in range(count + 2):
        if item < count:
            first(item)
        if 0 <= item - 1 < count:
            second(item - 1)
        if item >= 2:
            third(item - 2)


def attend(n, s, d):
    corner = lax.broadcasted_iota(jnp.int32, (128, 128), 0) >= lax.broadcasted_iota(
        jnp.int32, (128, 128), 1
    )
    ones = jnp.ones((LP, 128), BF16)
    marks = lane_halves(ones)
    raw, raised = {}, {}

    def score(pair):
        at = 128 * pair
        queries = lane_halves(n.qkv[s, :, at : at + 128] * jnp.array(SCORE_SCALE, BF16))
        keys = n.qkv[s, :, d + at : d + at + 128]
        for block, (first, rows, seen) in enumerate(BLOCKS):
            both = jnp.concatenate([q[first : first + rows] for q in queries], axis=0)
            raw[pair, block] = dot_nt(both, keys[:seen])

    def raise_scores(pair):
        for block, (first, rows, seen) in enumerate(BLOCKS):
            scores = raw.pop((pair, block))
            visible = jnp.concatenate([corner[:rows, :rows]] * 2, axis=0)
            diagonal = jnp.where(visible, scores[:, first:], NEG_LARGE)
            scores = jnp.concatenate([scores[:, :first], diagonal], axis=1) if first else diagonal
            powers = jnp.exp(scores - jnp.max(scores, axis=-1, keepdims=True)).astype(BF16)
            raised[pair, block] = powers
            n.powers[block][s, pair] = powers

    def mix(pair):
        at = 128 * pair
        values = lane_halves(n.qkv[s, :, 2 * d + at : 2 * d + at + 128])
        wide = [jnp.concatenate(both, axis=1) for both in zip(values, marks)]
        for block, (first, rows, seen) in enumerate(BLOCKS):
            powers = raised.pop((pair, block))
            if seen % 128 == 0:
                mixed = dot_nn(
                    jnp.concatenate([powers[:rows], powers[rows:]], axis=1),
                    jnp.concatenate([w[:seen] for w in wide], axis=0),
                )
            else:
                mixed = dot_nn(powers[:rows], wide[0][:seen]) + dot_nn(powers[rows:], wide[1][:seen])
            inverse = 1.0 / mixed[:, 128:]
            n.inverse_totals[s, first : first + rows, at : at + 128] = inverse
            n.attended[s, first : first + rows, at : at + 128] = (mixed[:, :128] * inverse).astype(
                BF16
            )

    in_steps(d // 128, score, raise_scores, mix)


def lay_out_inputs(n, seq_count):
    d = n.x.shape[2]
    pad = jnp.zeros((LP - L, d), F32)
    for s in range(0, seq_count, 2):
        both = n.states[s * L : (s + 2) * L].astype(F32)
        for i in range(2):
            n.x[s + i] = jnp.concatenate([both[i * L : (i + 1) * L], pad], axis=0).astype(BF16)
    n.flat[...] = jnp.zeros_like(n.flat)
    for i, ref in enumerate((n.chosen, n.reward, n.finished)):
        n.flat[i : i + 1, : seq_count * L] = ref[...].reshape(1, seq_count * L).astype(F32)
    for s in range(seq_count):
        n.aux[s] = n.flat[:, s * L : s * L + LP]
    n.gains[...] = jnp.zeros_like(n.gains)
    n.gains[0:2, :] = n.norm_gains[...].astype(F32)
    seq = lax.broadcasted_iota(jnp.int32, (8, 128), 0)
    task = lax.broadcasted_iota(jnp.int32, (8, 128), 1)
    table = jnp.zeros((8, 128), F32)
    for s in range(seq_count):
        table = jnp.where(jnp.logical_and(seq == s, task == n.task_ids[s]), 1.0, table)
    n.table[...] = table


def forward_sequence(n, s, d):
    x = n.x[s].astype(F32)
    normed = (x * inverse_rms(x) * n.gains[0:1, :]).astype(BF16)
    n.normed_one[s] = normed
    for first in range(0, 3 * d, 256):
        n.qkv[s, :, first : first + 256] = dot_nn(
            normed, n.w_qkv[:, first : first + 256]
        ).astype(BF16)
    attend(n, s, d)
    middle = x + dot_nn(n.attended[s], n.w_out[...])
    n.middle[s] = middle
    normed = (middle * inverse_rms(middle) * n.gains[1:2, :]).astype(BF16)
    n.normed_two[s] = normed
    ff = n.w_up.shape[1]
    for first in range(0, ff, 256):
        active, slope = gelu_and_slope(dot_nn(normed, n.w_up[:, first : first + 256]))
        n.active[s, :, first : first + 256] = active.astype(BF16)
        n.slope[s, :, first : first + 256] = slope.astype(BF16)
    final_low = (n.middle[s] + dot_nn(n.active[s], n.w_down[...])).astype(BF16)
    n.final_low[s] = final_low
    n.q_rows[s] = dot_nn(final_low, n.w_head[...]).astype(BF16)
    q_columns = dot_tt(n.w_head[...], final_low)
    bins = lax.broadcasted_iota(jnp.int32, q_columns.shape, 0)
    chosen = n.aux[s, 0:1, :].astype(jnp.int32)
    n.picked[pl.ds(s, 1), :] = jnp.sum(
        jnp.where(bins == chosen, q_columns, 0.0), axis=0, keepdims=True
    )
    n.tops[pl.ds(s, 1), :] = jnp.max(q_columns, axis=0, keepdims=True)


def backward_ffn(n, s):
    bins = lax.broadcasted_iota(jnp.int32, (n.w_head.shape[1], LP), 0)
    chosen = n.aux[s, 0:1, :].astype(jnp.int32)
    grad_q = jnp.where(bins == chosen, n.coef[pl.ds(s, 1), :], 0.0).astype(BF16)
    n.grad_q[s] = grad_q
    grad_final = dot_tt(grad_q, n.w_head[...])
    grad_ffn = grad_final.astype(BF16)
    n.grad_ffn[s] = grad_ffn
    ff = n.w_up.shape[1]
    for first in range(0, ff, 256):
        grad_active = dot_nt(grad_ffn, n.w_down[first : first + 256, :])
        n.slope[s, :, first : first + 256] = (
            grad_active * n.slope[s, :, first : first + 256].astype(F32)
        ).astype(BF16)
    grad_two = dot_nt(n.slope[s], n.w_up[...])
    middle = n.middle[s]
    inverse = inverse_rms(middle)
    normal = middle * inverse
    n.gain_sums[1] += jnp.sum((grad_two * normal).reshape(LP // 8, 8, -1), axis=0)
    inner = grad_two * n.gains[1:2, :]
    grad_middle = grad_final + inverse * (
        inner - normal * jnp.mean(inner * normal, axis=-1, keepdims=True)
    )
    n.middle[s] = grad_middle
    grad_branch = grad_middle.astype(BF16)
    n.grad_branch[s] = grad_branch
    n.grad_mixed[s] = dot_nt(grad_branch, n.w_out[...]).astype(BF16)


def attend_back(n, s, d):
    side = lax.broadcasted_iota(jnp.int32, (256, 256), 0) % 128 < HEAD_DIM
    head = lax.broadcasted_iota(jnp.int32, (256, 256), 1) < 128
    head_sums = jnp.where(side == head, jnp.ones((), BF16), jnp.zeros((), BF16))
    kept = {}

    def spread(pair):
        at = 128 * pair
        grads = (
            n.grad_mixed[s, :, at : at + 128].astype(F32) * n.inverse_totals[s, :, at : at + 128]
        ).astype(BF16)
        product = n.attended[s, :, at : at + 128].astype(F32) * grads.astype(F32)
        upper = product.astype(BF16)
        lower = (product - upper.astype(F32)).astype(BF16)
        centres = dot_nn(jnp.concatenate([upper, lower], axis=1), head_sums)
        values = n.qkv[s, :, 2 * d + at : 2 * d + at + 128]
        grads = lane_halves(grads)
        found = []
        for first, rows, seen in BLOCKS:
            both = jnp.concatenate([g[first : first + rows] for g in grads], axis=0)
            found.append((both, dot_nt(both, values[:seen])))
        kept[pair] = centres, found

    def centre(pair):
        centres, found = kept[pair]
        done = []
        for block, (first, rows, seen) in enumerate(BLOCKS):
            both, grad_powers = found[block]
            here = centres[first : first + rows]
            here = jnp.concatenate([here[:, :128], here[:, 128:]], axis=0)
            here = jnp.concatenate([here] * ((seen + 127) // 128), axis=1)[:, :seen]
            powers = n.powers[block][s, pair]
            done.append((both, powers, (powers.astype(F32) * (grad_powers - here)).astype(BF16)))
        kept[pair] = done

    def collect(pair):
        at = 128 * pair
        queries = lane_halves(n.qkv[s, :, at : at + 128])
        keys = lane_halves(n.qkv[s, :, d + at : d + at + 128])
        grad_keys = [None] * 3
        grad_values = [None] * 3
        done = kept.pop(pair)
        for block, (first, rows, seen) in enumerate(BLOCKS):
            both, powers, grad_scores = done[block]
            both_queries = jnp.concatenate([q[first : first + rows] for q in queries], axis=0)
            if seen % 128 == 0:
                grad_queries = dot_nn(
                    jnp.concatenate([grad_scores[:rows], grad_scores[rows:]], axis=1),
                    jnp.concatenate([k[:seen] for k in keys], axis=0),
                )
            else:
                grad_queries = dot_nn(grad_scores[:rows], keys[0][:seen]) + dot_nn(
                    grad_scores[rows:], keys[1][:seen]
                )
            of_values = dot_tn(powers, both)
            of_keys = dot_tn(grad_scores, both_queries)
            for i, start in enumerate((0, 128, 256)):
                if start < seen:
                    end = min(start + 128, seen)
                    piece = of_values[start:end]
                    grad_values[i] = piece if grad_values[i] is None else grad_values[i] + piece
                    piece = of_keys[start:end]
                    grad_keys[i] = piece if grad_keys[i] is None else grad_keys[i] + piece
            n.qkv[s, first : first + rows, at : at + 128] = (grad_queries * SCORE_SCALE).astype(
                BF16
            )
        for i, (first, rows, _) in enumerate(BLOCKS):
            n.qkv[s, first : first + rows, d + at : d + at + 128] = (
                grad_keys[i] * SCORE_SCALE
            ).astype(BF16)
            n.qkv[s, first : first + rows, 2 * d + at : 2 * d + at + 128] = grad_values[i].astype(
                BF16
            )

    in_steps(d // 128, spread, centre, collect)


def backward_attention(n, s, d):
    attend_back(n, s, d)
    grad_one = dot_nt(n.qkv[s], n.w_qkv[...])
    x = n.x[s].astype(F32)
    inverse = inverse_rms(x)
    normal = x * inverse
    n.gain_sums[0] += jnp.sum((grad_one * normal).reshape(LP // 8, 8, -1), axis=0)
    inner = grad_one * n.gains[0:1, :]
    n.grad_states[s] = (
        n.middle[s]
        + inverse * (inner - normal * jnp.mean(inner * normal, axis=-1, keepdims=True))
    ).astype(BF16)


TENSORS = ("down", "up", "out", "head", "qkv")
SEMAPHORES = 96


def layer_kernel(names, data_count, inside, *refs):
    n = Names()
    for name, ref in zip(names, refs):
        setattr(n, name, ref)
    n.powers = (n.powers_0, n.powers_1, n.powers_2)
    d = n.x.shape[2]
    ff = n.w_up.shape[1]
    seq_count = n.x.shape[0]

    me_pair = lax.axis_index("pair")
    me = lax.axis_index("dp")
    other = 1 - me_pair
    core = me % 2
    row = (me // 2) % 2
    low = (me // 4) % 2
    high = me // 8
    sibling = (me_pair, me + 1 - 2 * core)
    beside = (me_pair, me + 2 - 4 * row)
    near = (me_pair, me + 4 - 8 * low)
    partner = (other, me)
    quarter = me // 4

    def at_quarter(which, pair):
        return (pair, me + 4 * (which - quarter))

    def at_mixed(which, pair):
        return (pair, me + 8 * (which // 2 - high) + 2 * (which % 2 - row))

    used = [0]
    sent = []

    def slot():
        used[0] += 1
        return used[0] - 1

    def copy(src, dst, sem, device):
        return pltpu.make_async_remote_copy(
            src_ref=src,
            dst_ref=dst,
            send_sem=n.send_sem.at[sem],
            recv_sem=n.recv_sem.at[sem],
            device_id=device,
            device_id_type=MESH,
        )

    online = me_pair == 0

    barrier = pltpu.get_barrier_semaphore()
    friends = [partner]
    if inside:
        friends += [sibling, beside]
        for offset in range(1, 4):
            place = (quarter + offset) % 4
            friends += [at_quarter(place, me_pair), at_quarter(place, other)]
        friends += [
            (pair, me + 8 * (1 - 2 * high) + 2 * (1 - 2 * row)) for pair in (me_pair, other)
        ]
        friends += [(other, beside[1])]
    for friend in friends:
        pl.semaphore_signal(barrier, inc=1, device_id=friend, device_id_type=MESH)

    weight_refs = (n.w_qkv, n.w_out, n.w_up, n.w_down, n.w_head)
    if inside:
        theirs = (n.their_qkv, n.their_out, n.their_up, n.their_down, n.their_head)

    def piece_of(ref, half):
        height = ref.shape[0] // data_count
        width = ref.shape[1] // 2
        return (
            pl.ds(pl.multiple_of(me * height, height), height),
            pl.ds(pl.multiple_of(half * width, width), width),
        )

    weight_sems = [slot() for _ in weight_refs]

    def weight_copy(i):
        return copy(weight_refs[i].at[piece_of(weight_refs[i], other)], theirs[i], weight_sems[i], partner)

    gains_sem = slot()

    def gains_copy():
        return copy(n.gains, n.their_gains, gains_sem, partner)

    count_core, count_row = slot(), slot()
    count_far = [slot() for _ in range(3)]

    def count_copy(step, offset=0):
        if step == 0:
            return copy(n.count_out.at[0], n.count_in.at[0], count_core, sibling)
        if step == 1:
            return copy(n.count_out.at[1], n.count_in.at[1], count_row, beside)
        place = (quarter + offset) % 4
        return copy(
            n.count_out.at[2],
            n.count_in.at[1 + offset],
            count_far[offset - 1],
            at_quarter(place, me_pair),
        )

    n.gain_sums[...] = jnp.zeros_like(n.gain_sums)
    lay_out_inputs(n, seq_count)

    @pl.loop(0, seq_count)
    def _(s):
        forward_sequence(n, s, d)

        @pl.when(s == 0)
        def _():
            pl.semaphore_wait(barrier, len(friends))
            if not inside:
                return
            n.count_out[0] = jnp.broadcast_to(
                jnp.sum(n.table[...], axis=0, keepdims=True), (8, 128)
            )
            count_copy(0).start()
            for i in range(len(weight_refs)):
                weight_copy(i).start()
            gains_copy().start()

        if not inside:
            return

        @pl.when(s == 1)
        def _():
            count_copy(0).wait()
            n.count_out[1] = n.count_out[0] + n.count_in[0]
            count_copy(1).start()

        @pl.when(s == 2)
        def _():
            count_copy(1).wait()
            n.count_out[2] = n.count_out[1] + n.count_in[1]
            for offset in range(1, 4):
                count_copy(2, offset).start()

    lane = lax.broadcasted_iota(jnp.int32, (8, LP), 1)
    seq = lax.broadcasted_iota(jnp.int32, (8, LP), 0)
    real = jnp.logical_and(lane < L, seq < seq_count)
    tops = n.tops[...]
    aims_sem = slot()
    q_sem = slot()
    state_sems = [slot() for _ in range(1)]
    state_sems = state_sems + [slot() for _ in range(seq_count - 1)]

    def aims_copy():
        return copy(n.aims_out, n.aims_in, aims_sem, partner)

    def q_copy():
        return copy(n.q_rows.at[:, :, pl.ds(128, 128)], n.q_half, q_sem, partner)

    def state_copy(s):
        return copy(
            n.grad_states.at[s, :, pl.ds(d // 2, d // 2)],
            n.state_half.at[s],
            state_sems[0] + s,
            partner,
        )

    @pl.when(jnp.logical_not(online))
    def _():
        reward = jnp.concatenate([n.aux[s, 1:2, :] for s in range(seq_count)] * 2, axis=0)
        finished = jnp.concatenate([n.aux[s, 2:3, :] for s in range(seq_count)] * 2, axis=0)
        n.aims_out[...] = reward + DISCOUNT * (1.0 - finished) * tops
        aims_copy().start()

    @pl.when(online)
    def _():
        q_copy().start()

    if inside:
        for i in range(len(weight_refs)):
            weight_copy(i).wait()
            mine = weight_refs[i][piece_of(weight_refs[i], me_pair)].astype(F32)
            received = theirs[i][...].astype(F32)
            first = jnp.where(online, mine, received)
            second = jnp.where(online, received, mine)
            (n.new_qkv, n.new_out, n.new_up, n.new_down, n.new_head)[i][...] = second + SOFT_RATE * (
                first - second
            )
        gains_copy().wait()
        first = jnp.where(online, n.gains[...], n.their_gains[...])
        second = jnp.where(online, n.their_gains[...], n.gains[...])
        n.new_gains[...] = second + SOFT_RATE * (first - second)

        for offset in range(1, 4):
            count_copy(2, offset).wait()
        counts = n.count_out[2] + n.count_in[2] + n.count_in[3] + n.count_in[4]
    else:
        counts = n.counts[...]
    seq_weight = (seq_count * data_count) / (
        TASKS * jnp.sum(n.table[...] * counts, axis=1, keepdims=True)
    )

    stat_core, stat_row = slot(), slot()
    stat_far = [slot() for _ in range(7)]
    stat_row_id = lax.broadcasted_iota(jnp.int32, (8, 128), 0)
    stat_lane = lax.broadcasted_iota(jnp.int32, (8, 128), 1)

    def stat_copy(step, k=0):
        if step == 0:
            return copy(n.stat_out.at[0], n.stat_in.at[0], stat_core, sibling)
        if step == 1:
            return copy(n.stat_out.at[1], n.stat_in.at[1], stat_row, beside)
        place = (quarter + (k + 1) % 4) % 4
        pair = me_pair if k < 3 else other
        return copy(n.stat_out.at[2], n.stat_in.at[2 + k], stat_far[k], at_quarter(place, pair))

    def stat_join(a, b):
        return jnp.where(stat_row_id == 1, jnp.maximum(a, b), a + b)

    def stat_first(loss):
        total = jnp.sum(jnp.where(real, tops, 0.0))
        best = jnp.max(jnp.where(real, tops, LOWEST))
        sums = jnp.where(
            stat_lane == 0, loss, jnp.where(stat_lane == 1 + me_pair, total, 0.0)
        )
        bests = jnp.where(stat_lane == me_pair, best, LOWEST)
        n.stat_out[0] = jnp.where(
            stat_row_id == 0, sums, jnp.where(stat_row_id == 1, bests, 0.0)
        )
        if inside:
            stat_copy(0).start()

    def stat_second():
        if not inside:
            return
        stat_copy(0).wait()
        n.stat_out[1] = stat_join(n.stat_out[0], n.stat_in[0])
        stat_copy(1).start()

    def stat_third():
        if not inside:
            return
        stat_copy(1).wait()
        n.stat_out[2] = stat_join(n.stat_out[1], n.stat_in[1])
        for k in range(7):
            stat_copy(2, k).start()

    step_sems = {}
    for name in TENSORS:
        step_sems[name] = (slot(), slot(), [slot() for _ in range(7)])
    along = {"down": "row", "up": "low", "out": "row", "head": "row", "qkv": "row"}
    gain_sems = (slot(), slot(), [slot() for _ in range(7)])

    def core_start(name):
        if inside:
            core_copy(name).start()

    def core_copy(name):
        return copy(
            getattr(n, "g_" + name).at[:, :, :, 1 - core],
            getattr(n, "r1_" + name),
            step_sems[name][0],
            sibling,
        )

    def axis_copy(name):
        r1, r2 = getattr(n, "r1_" + name), getattr(n, "r2_" + name)
        if along[name] == "row":
            return copy(r1.at[:, :, 1 - row], r2, step_sems[name][1], beside)
        return copy(r1.at[:, 1 - low], r2, step_sems[name][1], near)

    def half_of(name, half):
        height, width = getattr(n, "r2_" + name).shape[2:]
        if name == "down":
            return (pl.ds(half * (height // 2), height // 2), slice(None))
        return (slice(None), pl.ds(half * (width // 2), width // 2))

    def far_copy(name, k):
        r2, r3 = getattr(n, "r2_" + name), getattr(n, "r3_" + name)
        offset = (k + 1) % 4
        pair = 0 if k < 3 else 1
        if along[name] == "row":
            place = (quarter + offset) % 4
            device = at_quarter(place, pair)
        else:
            place = (2 * high + row + offset) % 4
            device = at_mixed(place, pair)
        return copy(
            r2.at[(place // 2, place % 2) + half_of(name, pair)],
            r3.at[offset],
            step_sems[name][2][k],
            device,
        )

    def core_done(name):
        if not inside:
            return
        core_copy(name).wait()
        g, r1 = getattr(n, "g_" + name), getattr(n, "r1_" + name)
        for i in range(2):
            for j in range(2):
                for k in range(2):
                    r1[i, j, k] = (g[i, j, k, core].astype(F32) + r1[i, j, k].astype(F32)).astype(
                        BF16
                    )
        axis_copy(name).start()

    def axis_done(name):
        if not inside:
            return
        axis_copy(name).wait()
        r1, r2 = getattr(n, "r1_" + name), getattr(n, "r2_" + name)
        for i in range(2):
            for j in range(2):
                mine = r1[i, j, row] if along[name] == "row" else r1[i, low, j]
                r2[i, j] = (mine.astype(F32) + r2[i, j].astype(F32)).astype(BF16)
        for k in range(7):
            far_copy(name, k).start()

    def owner_online(name):
        if not inside:
            return
        r2, r3 = getattr(n, "r2_" + name), getattr(n, "r3_" + name)
        place = quarter if along[name] == "row" else 2 * high + row
        total = r2[(place // 2, place % 2) + half_of(name, 0)].astype(F32)
        for k in range(3):
            far_copy(name, k).wait_recv()
            total += r3[k + 1].astype(F32)
        getattr(n, "grad_" + name)[...] = total

    def owner_target(name):
        if not inside:
            return
        r3 = getattr(n, "r3_" + name)
        total = None
        for k in range(3, 7):
            far_copy(name, k).wait_recv()
            part = r3[(k + 1) % 4].astype(F32)
            total = part if total is None else total + part
        getattr(n, "grad_" + name)[...] = total

    def gain_copy(step, k=0):
        if step == 0:
            return copy(n.gain_out.at[0], n.gain_in.at[0], gain_sems[0], sibling)
        if step == 1:
            return copy(n.gain_out.at[1], n.gain_in.at[1], gain_sems[1], beside)
        offset = (k + 1) % 4
        pair = 0 if k < 3 else 1
        return copy(
            n.gain_out.at[2],
            n.gain_in.at[2 + offset],
            gain_sems[2][k],
            at_quarter((quarter + offset) % 4, pair),
        )

    @pl.when(online)
    def _():
        aims_copy().wait_recv()
        differ = n.picked[...] - n.aims_in[...]
        weighted = jnp.where(real, seq_weight * differ, 0.0)
        n.coef[...] = weighted
        stat_first(jnp.sum(0.5 * weighted * jnp.where(real, differ, 0.0)))

        @pl.loop(0, seq_count)
        def _(s):
            backward_ffn(n, s)

        stat_second()
        grad_ffn = rows_of(n.grad_ffn, 0, d)

        @pl.loop(0, ff // 256)
        def _(j):
            columns = pl.ds(pl.multiple_of(j * 256, 256), 256)
            value = dot_tn(grad_ffn, n.active[:, :, columns].reshape(seq_count * LP, 256))
            for c in range(2):
                n.g_down[j // 4, (j // 2) % 2, j % 2, c] = value[:, 128 * c : 128 * c + 128].astype(
                    BF16
                )

        core_start("down")
        normed_two = rows_of(n.normed_two, 0, d)

        @pl.loop(0, ff // 256)
        def _(j):
            columns = pl.ds(pl.multiple_of(j * 256, 256), 256)
            value = dot_tn(normed_two, n.slope[:, :, columns].reshape(seq_count * LP, 256))
            n.g_up[:, :, :, :, :, columns] = value.astype(BF16).reshape(2, 2, 2, 2, d // 16, 256)

        core_start("up")
        core_done("down")
        value = dot_tn(rows_of(n.attended, 0, d), rows_of(n.grad_branch, 0, d))
        n.g_out[...] = value.astype(BF16).reshape(n.g_out.shape)
        value = None
        for s in range(seq_count):
            part = dot_nn(n.grad_q[s], n.final_low[s])
            value = part if value is None else value + part
        n.g_head[...] = jnp.transpose(value).astype(BF16).reshape(n.g_head.shape)
        core_start("out")
        core_start("head")
        core_done("up")

        @pl.loop(0, seq_count)
        def _(s):
            backward_attention(n, s, d)
            state_copy(s).start()

            @pl.when(s == 0)
            def _():
                core_done("out")
                core_done("head")
                stat_third()

            @pl.when(s == 2)
            def _():
                axis_done("down")

        n.gain_out[0, 0:1, :] = jnp.sum(n.gain_sums[0], axis=0, keepdims=True)
        n.gain_out[0, 1:2, :] = jnp.sum(n.gain_sums[1], axis=0, keepdims=True)
        n.gain_out[0, 2:8, :] = jnp.zeros((6, d), F32)
        if inside:
            gain_copy(0).start()
        normed_one = rows_of(n.normed_one, 0, d)

        @pl.loop(0, 3 * d // 256)
        def _(j):
            columns = pl.ds(pl.multiple_of(j * 256, 256), 256)
            value = dot_tn(normed_one, n.qkv[:, :, columns].reshape(seq_count * LP, 256))
            n.g_qkv[:, :, :, :, :, columns] = value.astype(BF16).reshape(2, 2, 2, 2, d // 16, 256)

        core_start("qkv")
        axis_done("up")
        core_done("qkv")
        if inside:
            gain_copy(0).wait()
            n.gain_out[1] = n.gain_out[0] + n.gain_in[0]
            gain_copy(1).start()
        axis_done("out")
        axis_done("head")
        owner_online("down")
        if inside:
            gain_copy(1).wait()
            n.gain_out[2] = n.gain_out[1] + n.gain_in[1]
            for k in range(7):
                gain_copy(2, k).start()
        owner_online("up")
        axis_done("qkv")
        for s in range(0, seq_count, 2):
            n.state_out[s * L : (s + 2) * L] = without_pad(n.grad_states, s, d // 2)
            n.q_out[s * L : (s + 2) * L] = without_pad(n.q_rows, s, 128)
        owner_online("out")
        owner_online("head")
        if inside:
            total = n.gain_out[2]
            for k in range(3):
                gain_copy(2, k).wait_recv()
                total += n.gain_in[3 + k]
            n.grad_gains[...] = total
        else:
            n.grad_gains[...] = n.gain_out[0]
        owner_online("qkv")
        q_copy().wait_send()
        for s in range(seq_count):
            state_copy(s).wait_send()
        if inside:
            for k in range(7):
                for name in TENSORS:
                    far_copy(name, k).wait_send()
                gain_copy(2, k).wait_send()

    @pl.when(jnp.logical_not(online))
    def _():
        stat_first(0.0)
        stat_second()
        stat_third()
        q_copy().wait_recv()
        for s in range(0, seq_count, 2):
            n.q_out[s * L : (s + 2) * L] = without_pad(n.q_half, s, 128)
        for name in TENSORS[:4]:
            owner_target(name)
        for s in range(seq_count):
            state_copy(s).wait_recv()
            if s % 2:
                n.state_out[(s - 1) * L : (s + 1) * L] = without_pad(n.state_half, s - 1, d // 2)
        if inside:
            total = None
            for k in range(3, 7):
                gain_copy(2, k).wait_recv()
                part = n.gain_in[2 + (k + 1) % 4]
                total = part if total is None else total + part
            n.grad_gains[...] = total
        owner_target("qkv")
        aims_copy().wait_send()

    if inside:
        for k in range(7):
            stat_copy(2, k).wait()
        joined = n.stat_out[2]
        for k in range(7):
            joined = stat_join(joined, n.stat_in[2 + k])
        n.stats[...] = joined
    else:
        n.stats[...] = n.stat_out[0]
    assert used[0] <= SEMAPHORES


OUTPUTS = (
    "q_out",
    "state_out",
    "grad_gains",
    "grad_qkv",
    "grad_out",
    "grad_up",
    "grad_down",
    "grad_head",
    "new_gains",
    "new_qkv",
    "new_out",
    "new_up",
    "new_down",
    "new_head",
    "stats",
)


def finish_kernel(moved, worked, token_total, data_count, *refs):
    source = dict(zip(moved + worked, refs))
    result = dict(zip(OUTPUTS, refs[len(source) :]))
    sems = refs[-1]
    copies = [
        pltpu.make_async_copy(source[name], result[name], sems.at[i])
        for i, name in enumerate(moved)
    ]
    for copy in copies:
        copy.start()
    me_pair = lax.axis_index("pair")
    me = lax.axis_index("dp")
    for name in ("grad_gains", "new_gains"):
        height = source[name].shape[1] // data_count
        here = source[name][:, pl.ds(pl.multiple_of(me * height // 128 * 128, 128), 128)]
        value = here[:, :height]
        for at in range(height, 128, height):
            value = jnp.where(me * height % 128 == at, here[:, at : at + height], value)
        result[name][...] = jnp.where(me_pair == 0, value[0:1], value[1:2])
    if "grad_down" in worked:
        result["grad_down"][...] = jnp.transpose(source["grad_down"][...])
    stats = source["stats"]
    result["stats"][0] = stats[0, 0] / token_total
    result["stats"][1] = stats[0, 1] / token_total
    result["stats"][2] = stats[1, 0]
    result["stats"][3] = stats[0, 2] / token_total
    result["stats"][4] = stats[1, 1]
    for copy in copies:
        copy.wait()


def add_outside(out, params, pair_index, data_index, data_count):
    online = pair_index == 0
    other = 1 - pair_index

    def half(matrix, which):
        width = matrix.shape[1] // 2
        return lax.dynamic_slice_in_dim(matrix, which * width, width, 1)

    def piece(matrix, which):
        height = matrix.shape[0] // data_count
        return half(lax.dynamic_slice_in_dim(matrix, data_index * height, height, 0), which)

    def swapped(value):
        return lax.ppermute(value, "pair", [(0, 1), (1, 0)])

    for name in TENSORS:
        grad = out["g_" + name].astype(F32)
        grad = grad.reshape((16,) + grad.shape[4:])
        if name == "down":
            grad = jnp.swapaxes(grad, 1, 2)
        grad = lax.psum_scatter(
            grad.reshape(-1, grad.shape[2]), "dp", scatter_dimension=0, tiled=True
        )
        received = swapped(half(grad, other))
        out["grad_" + name] = jnp.where(online, half(grad, pair_index), received)
    gains = lax.psum(out["grad_gains"], "dp")
    out["grad_gains"] = jnp.where(online, gains, swapped(gains))
    for name, weight in zip(("gains", "qkv", "out", "up", "down", "head"), params):
        if name == "gains":
            weight = jnp.pad(weight.T, ((0, 6), (0, 0)))
            mine, received = weight.astype(F32), swapped(weight).astype(F32)
        else:
            mine = piece(weight, pair_index).astype(F32)
            received = swapped(piece(weight, other)).astype(F32)
        first, second = jnp.where(online, mine, received), jnp.where(online, received, mine)
        out["new_" + name] = second + SOFT_RATE * (first - second)
    sums = lax.psum(out["stats"][0:1], ("pair", "dp"))
    bests = lax.pmax(out["stats"][1:2], ("pair", "dp"))
    out["stats"] = jnp.concatenate([sums, bests])


def local(
    states, norm_gains, w_qkv, w_out, w_up, w_down, w_head, task_ids, chosen, reward, finished
):
    pair_index = lax.axis_index("pair")
    data_index = lax.axis_index("dp")
    data_count = lax.axis_size("dp")
    row_count, d = states.shape[1:]
    ff = w_up.shape[2]
    bin_count = w_head.shape[2]
    seq_count = row_count // L

    inside = data_count == 16
    rows = (seq_count, LP, d)
    inputs = dict(
        states=states[0],
        norm_gains=norm_gains[0].T,
        w_qkv=w_qkv[0],
        w_out=w_out[0],
        w_up=w_up[0],
        w_down=w_down[0],
        w_head=w_head[0],
        task_ids=task_ids,
        chosen=chosen,
        reward=reward,
        finished=finished,
    )
    if not inside:
        table = (task_ids[:, None] == jnp.arange(128, dtype=jnp.int32)[None, :]).astype(F32)
        inputs["counts"] = jnp.broadcast_to(
            lax.psum(jnp.sum(table, axis=0, keepdims=True), "dp"), (8, 128)
        )
    piece = {
        "qkv": (d // 16, 3 * d),
        "out": (d // 16, d),
        "up": (d // 16, ff),
        "head": (d // 16, bin_count),
        "down": (d, ff // 16),
    }
    halves = {
        name: (shape[0] // 2, shape[1]) if name == "down" else (shape[0], shape[1] // 2)
        for name, shape in piece.items()
    }
    new_shapes = dict(halves, down=(ff // 16, d // 2))
    outputs = dict(
        q_out=((row_count, bin_count // 2), BF16),
        state_out=((row_count, d // 2), BF16),
        grad_gains=((8, d), F32),
        new_gains=((8, d), F32),
        stats=((8, 128), F32),
    )
    for name in TENSORS:
        if inside:
            outputs["grad_" + name] = (halves[name], F32)
            outputs["new_" + name] = (new_shapes[name], F32)
        else:
            outputs["g_" + name] = ((2, 2, 2, 2) + piece[name], BF16)
    scratch = dict(
        x=(rows, BF16),
        gains=((8, d), F32),
        flat=((8, -(-(row_count + LP - L) // 128) * 128), F32),
        aux=((seq_count, 8, LP), F32),
        table=((8, 128), F32),
        normed_one=(rows, BF16),
        qkv=((seq_count, LP, 3 * d), BF16),
        powers_0=((seq_count, d // 128) + (2 * BLOCKS[0][1], BLOCKS[0][2]), BF16),
        powers_1=((seq_count, d // 128) + (2 * BLOCKS[1][1], BLOCKS[1][2]), BF16),
        powers_2=((seq_count, d // 128) + (2 * BLOCKS[2][1], BLOCKS[2][2]), BF16),
        inverse_totals=(rows, F32),
        attended=(rows, BF16),
        middle=(rows, F32),
        normed_two=(rows, BF16),
        active=((seq_count, LP, ff), BF16),
        slope=((seq_count, LP, ff), BF16),
        final_low=(rows, BF16),
        q_rows=((seq_count, LP, bin_count), BF16),
        q_half=((seq_count, LP, bin_count // 2), BF16),
        picked=((8, LP), F32),
        tops=((8, LP), F32),
        coef=((8, LP), F32),
        aims_out=((8, LP), F32),
        aims_in=((8, LP), F32),
        grad_q=((seq_count, bin_count, LP), BF16),
        grad_ffn=(rows, BF16),
        grad_branch=(rows, BF16),
        grad_mixed=(rows, BF16),
        grad_states=(rows, BF16),
        state_half=((seq_count, LP, d // 2), BF16),
        gain_sums=((2, 8, d), F32),
        gain_out=((3, 8, d), F32),
        gain_in=((6, 8, d), F32),
        count_out=((3, 8, 128), F32),
        count_in=((5, 8, 128), F32),
        stat_out=((3, 8, 128), F32),
        stat_in=((9, 8, 128), F32),
        their_gains=((8, d), F32),
    )
    for name in TENSORS if inside else ():
        scratch["g_" + name] = ((2, 2, 2, 2) + piece[name], BF16)
        scratch["r1_" + name] = ((2, 2, 2) + piece[name], BF16)
        scratch["r2_" + name] = ((2, 2) + piece[name], BF16)
        scratch["r3_" + name] = ((4,) + halves[name], BF16)
        scratch["their_" + name] = (new_shapes[name], BF16)
    names = list(inputs) + list(outputs) + list(scratch) + ["send_sem", "recv_sem"]
    in_vmem = pl.BlockSpec(memory_space=pltpu.VMEM)
    in_smem = pl.BlockSpec(memory_space=pltpu.SMEM)
    raw = pl.pallas_call(
        functools.partial(layer_kernel, names, data_count, inside),
        out_shape=[jax.ShapeDtypeStruct(shape, dtype) for shape, dtype in outputs.values()],
        in_specs=[in_smem if name == "task_ids" else in_vmem for name in inputs],
        out_specs=[in_vmem] * len(outputs),
        scratch_shapes=[pltpu.VMEM(shape, dtype) for shape, dtype in scratch.values()]
        + [pltpu.SemaphoreType.DMA((SEMAPHORES,)), pltpu.SemaphoreType.DMA((SEMAPHORES,))],
        compiler_params=pltpu.CompilerParams(
            collective_id=0, has_side_effects=True, vmem_limit_bytes=64 * 1024 * 1024 - 65536
        ),
        name="layer",
    )(*inputs.values())
    out = dict(zip(outputs, raw))
    if not inside:
        params = (norm_gains[0], w_qkv[0], w_out[0], w_up[0], w_down[0], w_head[0])
        add_outside(out, params, pair_index, data_index, data_count)
    moved = {name: out[name] for name in OUTPUTS if name not in ("grad_gains", "new_gains", "stats")}
    worked = {name: out[name] for name in ("grad_gains", "new_gains", "stats")}
    results = {name: jax.ShapeDtypeStruct(value.shape, value.dtype) for name, value in moved.items()}
    if inside:
        worked["grad_down"] = moved.pop("grad_down")
        results["grad_down"] = jax.ShapeDtypeStruct((ff // data_count, d // 2), F32)
    results["grad_gains"] = results["new_gains"] = jax.ShapeDtypeStruct((1, d // data_count), F32)
    results["stats"] = jax.ShapeDtypeStruct((5,), F32)
    anywhere = pl.BlockSpec(memory_space=pl.ANY)
    spec_of = {name: anywhere if name in moved else in_vmem for name in OUTPUTS}
    spec_of["stats"] = in_smem
    final = pl.pallas_call(
        functools.partial(
            finish_kernel, list(moved), list(worked), row_count * data_count, data_count
        ),
        out_shape=[results[name] for name in OUTPUTS],
        in_specs=[in_vmem] * (len(moved) + len(worked)),
        out_specs=[spec_of[name] for name in OUTPUTS],
        scratch_shapes=[
            pltpu.SemaphoreType.DMA((len(moved),)),
        ],
        name="finish",
    )(*moved.values(), *worked.values())
    final = dict(zip(OUTPUTS, final))
    for name in ("grad_gains", "new_gains"):
        final[name] = final[name].T
    return tuple(final.values())


def solution(mesh):
    placed = (
        P("pair", "dp", None),
        P("pair", None, None),
        P("pair", None, None),
        P("pair", None, None),
        P("pair", None, None),
        P("pair", None, None),
        P("pair", None, None),
        P("dp"),
        P("dp"),
        P("dp"),
        P("dp"),
    )
    return jax.shard_map(
        local,
        mesh=mesh,
        in_specs=placed,
        out_specs=(P("dp", "pair"),) * 14 + (P(),),
        check_vma=False,
    )
```

```python
import functools

import jax
import jax.numpy as jnp
from jax import lax
from jax.experimental import pallas as pl
from jax.experimental.pallas import tpu as pltpu
from jax.sharding import PartitionSpec as P

F32 = jnp.float32
BF16 = jnp.bfloat16
MESH = pl.DeviceIdType.MESH

DOWN = "down"
PAIR = "pair"
DP = "dp"
STATS = "stats"
ROW = "row"
HEAD = "head"
UP_B = "up_b"
OUT = "out"
UP_A = "up_a"
LOW = "low"
GRAD_GAINS = "grad_gains"
HIGH = "high"
GRAD_DOWN = "grad_down"
NEW_GAINS = "new_gains"
QKV_0 = "qkv_0"
QKV_1 = "qkv_1"
QKV_2 = "qkv_2"
QKV_3 = "qkv_3"
UP = "up"
QKV = "qkv"
GAINS = "gains"

HEAD_DIM = 64
L = 296
LP = 304
TASKS = 32
EPSILON = 1e-06
DISCOUNT = 0.98
SOFT_RATE = 0.2
SCORE_SCALE = 0.125
NEG_LARGE = -1000000000.0
LOWEST = -1e30

BLOCKS = ((0, 128, 128), (128, 128, 256), (256, 48, 304))


def dot_nn(a, b):
    return lax.dot_general(a, b, (((1,), (0,)), ((), ())), preferred_element_type=F32)


def dot_nt(a, b):
    return lax.dot_general(a, b, (((1,), (1,)), ((), ())), preferred_element_type=F32)


def dot_tn(a, b):
    return lax.dot_general(a, b, (((0,), (0,)), ((), ())), preferred_element_type=F32)


def dot_tt(a, b):
    return lax.dot_general(a, b, (((0,), (1,)), ((), ())), preferred_element_type=F32)


def inverse_rms(values):
    return lax.rsqrt(jnp.mean(values * values, axis=-1, keepdims=True) + EPSILON)


def gelu_and_slope(u):
    c = 0.7978845608028654
    square = u * u
    t = jnp.tanh(u * (c + (c * 0.044715) * square))
    half = 0.5 * t + 0.5
    slope = half + (u * (0.5 - 0.5 * t * t)) * (c + (3 * c * 0.044715) * square)
    return u * half, slope


def lane_halves(a):
    lane = lax.broadcasted_iota(jnp.int32, (1, 2 * HEAD_DIM), 1)
    zero = jnp.zeros((), a.dtype)
    return jnp.where(lane < HEAD_DIM, a, zero), jnp.where(lane >= HEAD_DIM, a, zero)


def rows_of(ref, first, width):
    value = ref[:, :, first : first + width]
    return value.reshape(value.shape[0] * value.shape[1], width)


def without_pad(ref, s, width):
    rows = [ref[s + i, :, :width].astype(F32)[:L] for i in range(2)]
    return jnp.concatenate(rows, axis=0).astype(BF16)


class Names:
    pass


def in_steps(count, first, second, third):
    for item in range(count + 2):
        if item < count:
            first(item)
        if 0 <= item - 1 < count:
            second(item - 1)
        if item >= 2:
            third(item - 2)


def attend(n, items, d):
    corner = lax.broadcasted_iota(jnp.int32, (128, 128), 0) >= lax.broadcasted_iota(
        jnp.int32, (128, 128), 1
    )
    ones = jnp.ones((LP, 128), BF16)
    marks = lane_halves(ones)
    raw, raised = {}, {}

    def score(item):
        s, pair = items[item]
        at = 128 * pair
        queries = lane_halves(n.qkv[s, :, at : at + 128] * jnp.array(SCORE_SCALE, BF16))
        keys = n.qkv[s, :, d + at : d + at + 128]
        for block, (first, rows, seen) in enumerate(BLOCKS):
            both = jnp.concatenate([q[first : first + rows] for q in queries], axis=0)
            raw[item, block] = dot_nt(both, keys[:seen])

    def raise_scores(item):
        s, pair = items[item]
        for block, (first, rows, seen) in enumerate(BLOCKS):
            scores = raw.pop((item, block))
            visible = jnp.concatenate([corner[:rows, :rows]] * 2, axis=0)
            diagonal = jnp.where(visible, scores[:, first:], NEG_LARGE)
            scores = jnp.concatenate([scores[:, :first], diagonal], axis=1) if first else diagonal
            powers = jnp.exp(scores - jnp.max(scores, axis=-1, keepdims=True)).astype(BF16)
            raised[item, block] = powers
            n.powers[block][s, pair] = powers

    def mix(item):
        s, pair = items[item]
        at = 128 * pair
        values = lane_halves(n.qkv[s, :, 2 * d + at : 2 * d + at + 128])
        wide = [jnp.concatenate(both, axis=1) for both in zip(values, marks)]
        for block, (first, rows, seen) in enumerate(BLOCKS):
            powers = raised.pop((item, block))
            if seen % 128 == 0:
                mixed = dot_nn(
                    jnp.concatenate([powers[:rows], powers[rows:]], axis=1),
                    jnp.concatenate([w[:seen] for w in wide], axis=0),
                )
            else:
                mixed = dot_nn(powers[:rows], wide[0][:seen]) + dot_nn(powers[rows:], wide[1][:seen])
            inverse = 1.0 / mixed[:, 128:]
            n.inverse_totals[s, first : first + rows, at : at + 128] = inverse
            n.attended[s, first : first + rows, at : at + 128] = (mixed[:, :128] * inverse).astype(
                BF16
            )

    in_steps(len(items), score, raise_scores, mix)


def lay_out_inputs(n, seq_count):
    d = n.x.shape[2]
    pad = jnp.zeros((LP - L, d), F32)
    for s in range(0, seq_count, 2):
        both = n.states[s * L : (s + 2) * L].astype(F32)
        for i in range(2):
            n.x[s + i] = jnp.concatenate([both[i * L : (i + 1) * L], pad], axis=0).astype(BF16)
    n.flat[...] = jnp.zeros_like(n.flat)
    for i, ref in enumerate((n.chosen, n.reward, n.finished)):
        n.flat[i : i + 1, : seq_count * L] = ref[...].reshape(1, seq_count * L).astype(F32)
    for s in range(seq_count):
        n.aux[s] = n.flat[:, s * L : s * L + LP]
    n.gains[...] = jnp.zeros_like(n.gains)
    n.gains[0:2, :] = n.norm_gains[...].astype(F32)
    seq = lax.broadcasted_iota(jnp.int32, (8, 128), 0)
    task = lax.broadcasted_iota(jnp.int32, (8, 128), 1)
    table = jnp.zeros((8, 128), F32)
    for s in range(seq_count):
        table = jnp.where(jnp.logical_and(seq == s, task == n.task_ids[s]), 1.0, table)
    n.table[...] = table


def forward_sequences(n, s, online, loads):
    both = pl.ds(s, 2)
    d = n.x.shape[2]
    ff = n.w_up.shape[1]

    def rows(ref):
        return ref[both].reshape(2 * LP, ref.shape[2])

    def split(value):
        return value.astype(BF16).reshape(2, LP, value.shape[1])

    x = rows(n.x).astype(F32)
    normed = (x * inverse_rms(x) * n.gains[0:1, :]).astype(BF16)
    n.normed_one[both] = split(normed)
    for first in range(0, 3 * d, 256):
        n.qkv[both, :, first : first + 256] = split(
            dot_nn(normed, n.w_qkv[:, first : first + 256])
        )
    attend(n, [(s + i, pair) for i in range(2) for pair in range(d // 128)], d)

    @pl.when(s == 0)
    def _():
        for load in loads:
            load.wait()

    middle = rows(n.x).astype(F32) + dot_nn(rows(n.attended), n.w_out[...])
    n.middle[both] = middle.reshape(2, LP, d)
    normed = (middle * inverse_rms(middle) * n.gains[1:2, :]).astype(BF16)
    n.normed_two[both] = split(normed)

    @pl.when(online)
    def _():
        for first in range(0, ff, 256):
            active, slope = gelu_and_slope(dot_nn(normed, n.w_up[:, first : first + 256]))
            n.active[both, :, first : first + 256] = split(active)
            n.slope[both, :, first : first + 256] = split(slope)

    @pl.when(jnp.logical_not(online))
    def _():
        for first in range(0, ff, 256):
            active, _ = gelu_and_slope(dot_nn(normed, n.w_up[:, first : first + 256]))
            n.active[both, :, first : first + 256] = split(active)

    final_low = (rows(n.middle) + dot_nn(rows(n.active), n.w_down[...])).astype(BF16)
    n.final_low[both] = split(final_low)
    n.q_rows[both] = split(dot_nn(final_low, n.w_head[...]))
    for i in range(2):
        q_columns = dot_tt(n.w_head[...], n.final_low[s + i])
        bins = lax.broadcasted_iota(jnp.int32, q_columns.shape, 0)
        chosen = n.aux[s + i, 0:1, :].astype(jnp.int32)
        n.picked[pl.ds(s + i, 1), :] = jnp.sum(
            jnp.where(bins == chosen, q_columns, 0.0), axis=0, keepdims=True
        )
        n.tops[pl.ds(s + i, 1), :] = jnp.max(q_columns, axis=0, keepdims=True)


def backward_head(n, s):
    bins = lax.broadcasted_iota(jnp.int32, (n.w_head.shape[1], LP), 0)
    chosen = n.aux[s, 0:1, :].astype(jnp.int32)
    grad_q = jnp.where(bins == chosen, n.coef[pl.ds(s, 1), :], 0.0).astype(BF16)
    n.grad_q[s] = grad_q
    n.grad_ffn[s] = dot_tt(grad_q, n.w_head[...]).astype(BF16)


def backward_upper(n, s):
    both = pl.ds(s, 2)
    ff = n.w_up.shape[1]
    grad_ffn = n.grad_ffn[both].reshape(2 * LP, -1)
    for first in range(0, ff, 256):
        grad_active = dot_nt(grad_ffn, n.w_down[first : first + 256, :])
        slope = n.slope[both, :, first : first + 256].astype(F32)
        n.slope[both, :, first : first + 256] = (
            grad_active.reshape(2, LP, 256) * slope
        ).astype(BF16)


def backward_middle(n, s):
    both = pl.ds(s, 2)
    d = n.x.shape[2]
    grad_two = dot_nt(n.slope[both].reshape(2 * LP, -1), n.w_up[...])
    middle = n.middle[both].reshape(2 * LP, d)
    inverse = inverse_rms(middle)
    normal = middle * inverse
    n.gain_sums[1] += jnp.sum((grad_two * normal).reshape(2 * LP // 8, 8, d), axis=0)
    inner = grad_two * n.gains[1:2, :]
    grad_final = jnp.concatenate(
        [dot_tt(n.grad_q[s + i], n.w_head[...]) for i in range(2)], axis=0
    )
    grad_middle = grad_final + inverse * (
        inner - normal * jnp.mean(inner * normal, axis=-1, keepdims=True)
    )
    n.middle[both] = grad_middle.reshape(2, LP, d)
    grad_branch = grad_middle.astype(BF16)
    n.grad_branch[both] = grad_branch.reshape(2, LP, d)
    n.grad_mixed[both] = dot_nt(grad_branch, n.w_out[...]).astype(BF16).reshape(2, LP, d)


def attend_back(n, items, d):
    side = lax.broadcasted_iota(jnp.int32, (256, 256), 0) % 128 < HEAD_DIM
    head = lax.broadcasted_iota(jnp.int32, (256, 256), 1) < 128
    head_sums = jnp.where(side == head, jnp.ones((), BF16), jnp.zeros((), BF16))
    kept = {}

    def spread(item):
        s, pair = items[item]
        at = 128 * pair
        grads = (
            n.grad_mixed[s, :, at : at + 128].astype(F32) * n.inverse_totals[s, :, at : at + 128]
        ).astype(BF16)
        product = n.attended[s, :, at : at + 128].astype(F32) * grads.astype(F32)
        upper = product.astype(BF16)
        lower = (product - upper.astype(F32)).astype(BF16)
        centres = dot_nn(jnp.concatenate([upper, lower], axis=1), head_sums)
        values = n.qkv[s, :, 2 * d + at : 2 * d + at + 128]
        grads = lane_halves(grads)
        found = []
        for first, rows, seen in BLOCKS:
            both = jnp.concatenate([g[first : first + rows] for g in grads], axis=0)
            found.append((both, dot_nt(both, values[:seen])))
        kept[item] = centres, found

    def centre(item):
        s, pair = items[item]
        centres, found = kept[item]
        done = []
        for block, (first, rows, seen) in enumerate(BLOCKS):
            both, grad_powers = found[block]
            here = centres[first : first + rows]
            here = jnp.concatenate([here[:, :128], here[:, 128:]], axis=0)
            here = jnp.concatenate([here] * ((seen + 127) // 128), axis=1)[:, :seen]
            powers = n.powers[block][s, pair]
            done.append((both, powers, (powers.astype(F32) * (grad_powers - here)).astype(BF16)))
        kept[item] = done

    def collect(item):
        s, pair = items[item]
        at = 128 * pair
        queries = lane_halves(n.qkv[s, :, at : at + 128])
        keys = lane_halves(n.qkv[s, :, d + at : d + at + 128])
        grad_keys = [None] * 3
        grad_values = [None] * 3
        done = kept.pop(item)
        for block, (first, rows, seen) in enumerate(BLOCKS):
            both, powers, grad_scores = done[block]
            both_queries = jnp.concatenate([q[first : first + rows] for q in queries], axis=0)
            if seen % 128 == 0:
                grad_queries = dot_nn(
                    jnp.concatenate([grad_scores[:rows], grad_scores[rows:]], axis=1),
                    jnp.concatenate([k[:seen] for k in keys], axis=0),
                )
            else:
                grad_queries = dot_nn(grad_scores[:rows], keys[0][:seen]) + dot_nn(
                    grad_scores[rows:], keys[1][:seen]
                )
            of_values = dot_tn(powers, both)
            of_keys = dot_tn(grad_scores, both_queries)
            for i, start in enumerate((0, 128, 256)):
                if start < seen:
                    end = min(start + 128, seen)
                    piece = of_values[start:end]
                    grad_values[i] = piece if grad_values[i] is None else grad_values[i] + piece
                    piece = of_keys[start:end]
                    grad_keys[i] = piece if grad_keys[i] is None else grad_keys[i] + piece
            n.qkv[s, first : first + rows, at : at + 128] = (grad_queries * SCORE_SCALE).astype(
                BF16
            )
        for i, (first, rows, _) in enumerate(BLOCKS):
            n.qkv[s, first : first + rows, d + at : d + at + 128] = (
                grad_keys[i] * SCORE_SCALE
            ).astype(BF16)
            n.qkv[s, first : first + rows, 2 * d + at : 2 * d + at + 128] = grad_values[i].astype(
                BF16
            )

    in_steps(len(items), spread, centre, collect)


def backward_states(n, s):
    grad_one = dot_nt(n.qkv[s], n.w_qkv[...])
    x = n.x[s].astype(F32)
    inverse = inverse_rms(x)
    normal = x * inverse
    n.gain_sums[0] += jnp.sum((grad_one * normal).reshape(LP // 8, 8, -1), axis=0)
    inner = grad_one * n.gains[0:1, :]
    n.grad_states[s] = (
        n.middle[s]
        + inverse * (inner - normal * jnp.mean(inner * normal, axis=-1, keepdims=True))
    ).astype(BF16)


ROUTES = {
    DOWN: (ROW,),
    HEAD: (ROW,),
    UP_A: (ROW, LOW, HIGH),
    UP_B: (LOW, ROW, HIGH),
    OUT: (ROW,),
    QKV_0: (ROW,),
    QKV_1: (LOW,),
    QKV_2: (ROW,),
    QKV_3: (LOW,),
}
CHUNKS = {
    QKV_0: ((0, 128), (0, 128)),
    QKV_1: ((256, 384), (256, 384)),
    QKV_2: ((512,), (512,)),
    QKV_3: ((640,), (640,)),
}
STRIDES = {HIGH: 8, LOW: 4, ROW: 2}
TENSORS = (DOWN, HEAD, UP, OUT, QKV)
AXES = (HIGH, LOW, ROW)
SEMAPHORES = 128


def layer_kernel(names, data_count, inside, *refs):
    n = Names()
    for name, ref in zip(names, refs):
        setattr(n, name, ref)
    n.powers = (n.powers_0, n.powers_1, n.powers_2)
    n.grad_states, n.grad_branch, n.grad_mixed = n.normed_one, n.normed_two, n.final_low
    d = n.x.shape[2]
    ff = n.w_up.shape[1]
    seq_count = n.x.shape[0]

    me_pair = lax.axis_index(PAIR)
    me = lax.axis_index(DP)
    other = 1 - me_pair
    online = me_pair == 0
    core = me % 2
    row = (me // 2) % 2
    low = (me // 4) % 2
    high = me // 8
    quarter = me // 4
    bits = {ROW: row, LOW: low, HIGH: high}
    sibling = (me_pair, me + 1 - 2 * core)
    partner = (other, me)
    across = {
        "core": sibling,
        ROW: (me_pair, me + 2 - 4 * row),
        LOW: (me_pair, me + 4 - 8 * low),
        HIGH: (me_pair, me + 8 - 16 * high),
        PAIR: partner,
    }

    def at_quarter(which, pair):
        return (pair, me + 4 * (which - quarter))

    used = [0]

    def copy(src, dst, device):
        sem = used[0]
        used[0] += 1
        return pltpu.make_async_remote_copy(
            src_ref=src,
            dst_ref=dst,
            send_sem=n.send_sem.at[sem],
            recv_sem=n.recv_sem.at[sem],
            device_id=device,
            device_id_type=MESH,
        )

    barrier = pltpu.get_barrier_semaphore()
    friends = [partner]
    if inside:
        friends.append(sibling)
        for offset in range(1, 8):
            place = 2 * ((me // 2 + offset) % 8) + core
            friends += [(me_pair, place), (other, place)]
    loads = [
        pltpu.make_async_copy(src, dst, n.load_sem.at[i])
        for i, (src, dst) in enumerate(
            (
                (n.hbm_qkv, n.w_qkv),
                (n.hbm_out, n.w_out),
                (n.hbm_up, n.w_up),
                (n.hbm_down, n.w_down),
                (n.hbm_head, n.w_head),
            )
        )
    ]
    for load in loads:
        load.start()
    for friend in friends:
        pl.semaphore_signal(barrier, inc=1, device_id=friend, device_id_type=MESH)

    weights = {QKV: n.w_qkv, OUT: n.w_out, UP: n.w_up, DOWN: n.w_down, HEAD: n.w_head}

    def piece_of(ref, half):
        height = ref.shape[0] // data_count
        width = ref.shape[1] // 2
        return (
            pl.ds(pl.multiple_of(me * height, height), height),
            pl.ds(pl.multiple_of(half * width, width), width),
        )

    weight_copies = {}
    if inside:
        for name, ref in weights.items():
            weight_copies[name] = copy(
                ref.at[piece_of(ref, other)], getattr(n, "their_" + name), partner
            )
        weight_copies[GAINS] = copy(n.gains, n.their_gains, partner)

    count_copies = []
    if inside:
        count_copies.append(copy(n.count_out.at[0], n.count_in.at[0], sibling))
        for offset in range(1, 8):
            place = (me // 2 + offset) % 8
            count_copies.append(
                copy(n.count_out.at[1], n.count_in.at[offset], (me_pair, 2 * place + core))
            )

    n.gain_sums[...] = jnp.zeros_like(n.gain_sums)
    lay_out_inputs(n, seq_count)
    loads[0].wait()

    @pl.loop(0, seq_count // 2)
    def _(t):
        forward_sequences(n, 2 * t, online, loads[1:])

        @pl.when(t == 0)
        def _():
            pl.semaphore_wait(barrier, len(friends))
            if not inside:
                return
            n.count_out[0] = jnp.broadcast_to(
                jnp.sum(n.table[...], axis=0, keepdims=True), (8, 128)
            )
            count_copies[0].start()
            for each in weight_copies.values():
                each.start()

        @pl.when(t == 1)
        def _():
            if not inside:
                return
            count_copies[0].wait()
            n.count_out[1] = n.count_out[0] + n.count_in[0]
            for each in count_copies[1:]:
                each.start()

    lane = lax.broadcasted_iota(jnp.int32, (8, LP), 1)
    seq = lax.broadcasted_iota(jnp.int32, (8, LP), 0)
    real = jnp.logical_and(lane < L, seq < seq_count)
    tops = n.tops[...]
    aims_copy = copy(n.aims_out, n.aims_in, partner)
    q_copy = copy(n.q_rows.at[:, :, pl.ds(128, 128)], n.q_half, partner)
    state_sem = used[0]
    used[0] += seq_count

    def state_copy(s):
        return pltpu.make_async_remote_copy(
            src_ref=n.grad_states.at[s, :, pl.ds(d // 2, d // 2)],
            dst_ref=n.state_half.at[s],
            send_sem=n.send_sem.at[state_sem + s],
            recv_sem=n.recv_sem.at[state_sem + s],
            device_id=partner,
            device_id_type=MESH,
        )

    @pl.when(jnp.logical_not(online))
    def _():
        reward = jnp.concatenate([n.aux[s, 1:2, :] for s in range(seq_count)] * 2, axis=0)
        finished = jnp.concatenate([n.aux[s, 2:3, :] for s in range(seq_count)] * 2, axis=0)
        n.aims_out[...] = reward + DISCOUNT * (1.0 - finished) * tops
        aims_copy.start()

    @pl.when(online)
    def _():
        q_copy.start()

    if inside:
        for name, each in weight_copies.items():
            each.wait()
            if name == GAINS:
                mine, received = n.gains[...], n.their_gains[...]
            else:
                mine = weights[name][piece_of(weights[name], me_pair)].astype(F32)
                received = getattr(n, "their_" + name)[...].astype(F32)
            first = jnp.where(online, mine, received)
            second = jnp.where(online, received, mine)
            getattr(n, "new_" + name)[...] = second + SOFT_RATE * (first - second)
        counts = n.count_out[1]
        for i in range(1, 8):
            count_copies[i].wait()
            counts += n.count_in[i]
    else:
        counts = n.counts[...]
    seq_weight = (seq_count * data_count) / (
        TASKS * jnp.sum(n.table[...] * counts, axis=1, keepdims=True)
    )

    stat_row_id = lax.broadcasted_iota(jnp.int32, (8, 128), 0)
    stat_lane = lax.broadcasted_iota(jnp.int32, (8, 128), 1)
    stat_axes = ("core", ROW, LOW, HIGH, PAIR)
    stat_copies = [] if not inside else [
        copy(n.stat_out.at[i], n.stat_in.at[i], across[axis]) for i, axis in enumerate(stat_axes)
    ]

    def stat_first(loss):
        total = jnp.sum(jnp.where(real, tops, 0.0))
        best = jnp.max(jnp.where(real, tops, LOWEST))
        sums = jnp.where(stat_lane == 0, loss, jnp.where(stat_lane == 1 + me_pair, total, 0.0))
        bests = jnp.where(stat_lane == me_pair, best, LOWEST)
        n.stat_out[0] = jnp.where(stat_row_id == 0, sums, jnp.where(stat_row_id == 1, bests, 0.0))
        if inside:
            stat_copies[0].start()

    def stat_next(i):
        if not inside:
            return
        stat_copies[i].wait()
        mine, received = n.stat_out[i], n.stat_in[i]
        joined = jnp.where(stat_row_id == 1, jnp.maximum(mine, received), mine + received)
        n.stat_out[i + 1] = joined
        if i + 1 < len(stat_copies):
            stat_copies[i + 1].start()

    def half_of(name, half):
        if name in CHUNKS:
            first, second = (128 * len(at) for at in CHUNKS[name])
            return (slice(None), pl.ds(first * half, second if half else first))
        ref = getattr(n, "r1_" + name)
        height, width = (size // 2 for size in ref.shape[-2:])
        if name == DOWN:
            return (pl.ds(half * height, height), slice(None))
        return (slice(None), pl.ds(half * width, width))

    def put(name, total, pair=0):
        if name in CHUNKS:
            for i, at in enumerate(CHUNKS[name][pair]):
                n.grad_qkv[:, at : at + 128] = total[:, 128 * i : 128 * i + 128]
        elif name in (UP_A, UP_B):
            width = total.shape[1]
            n.grad_up[:, pl.ds(width * (name == UP_B), width)] = total
        else:
            getattr(n, "grad_" + name)[...] = total

    def places(count):
        if count == 0:
            return [()]
        return [(i,) + rest for i in range(2) for rest in places(count - 1)]

    def index_at(left, axis, value, place=None):
        place = iter(place or (slice(None),) * 2)
        return tuple(value if each == axis else next(place) for each in left)

    def left_after(name, count):
        return tuple(each for each in AXES if each not in ROUTES[name][:count])

    def n_far(name):
        return getattr(n, "far_" + name)

    core_copies, axis_copies, far_copies, pair_copies = {}, {}, {}, {}
    for name in ROUTES if inside else ():
        r1 = getattr(n, "r1_" + name)
        core_copies[name] = copy(getattr(n, "g_" + name).at[:, :, :, 1 - core], r1, sibling)
        if name == DOWN:
            whole = (slice(None),) * 3
            pair_copies[name] = copy(r1.at[whole + half_of(name, 1)], n.half_down, partner)
            r1 = n.half_down
        axis_copies[name] = []
        for i, axis in enumerate(ROUTES[name]):
            src = r1 if i == 0 else getattr(n, f"r{i + 1}_{name}")
            view = src.at[index_at(left_after(name, i), axis, 1 - bits[axis])]
            axis_copies[name].append(copy(view, getattr(n, f"r{i + 2}_{name}"), across[axis]))
        if len(ROUTES[name]) == 1:
            rest = left_after(name, 1)
            mine = 2 * bits[rest[0]] + bits[rest[1]]
            far_copies[name] = []
            for k in range(7 if name in CHUNKS else 3):
                offset, pair = (k + 1) % 4, 0 if k < 3 else 1
                place = (mine + offset) % 4
                target = me
                for each, bit in zip(rest, (place // 2, place % 2)):
                    target = target + STRIDES[each] * (bit - bits[each])
                view, landing = (place // 2, place % 2), (offset,)
                if name in CHUNKS:
                    view += half_of(name, pair)
                    landing += (slice(None), pl.ds(0, 128 * len(CHUNKS[name][pair])))
                else:
                    pair = me_pair
                far_copies[name].append(
                    copy(getattr(n, "r2_" + name).at[view], n_far(name).at[landing], (pair, target))
                )
        if name != DOWN and name not in CHUNKS:
            pair_copies[name] = copy(getattr(n, "to_" + name), getattr(n, "from_" + name), partner)

    def core_start(name):
        if inside:
            core_copies[name].start()

    def core_done(name):
        if not inside:
            return
        core_copies[name].wait()
        g, r1 = getattr(n, "g_" + name), getattr(n, "r1_" + name)
        for place in places(3):
            total = (g[place + (core,)].astype(F32) + r1[place].astype(F32)).astype(BF16)
            if name == DOWN:
                height = total.shape[0] // 2
                n.half_down[place] = total[:height]
                r1[place + half_of(name, 1)] = total[height:]
            else:
                r1[place] = total
        if name == DOWN:
            pair_copies[name].start()
        axis_copies[name][0].start()

    def axis_done(name, i=0):
        if not inside:
            return
        axis = ROUTES[name][i]
        left = left_after(name, i)
        axis_copies[name][i].wait()
        src = n.half_down if name == DOWN else getattr(n, f"r{i + 1}_{name}")
        dst = getattr(n, f"r{i + 2}_{name}")
        for place in places(len(left) - 1):
            mine = src[index_at(left, axis, bits[axis], place)].astype(F32)
            at = place or (slice(None),) * 2
            total = mine + dst[at].astype(F32)
            if place:
                dst[at] = total.astype(BF16)
        if i + 1 < len(ROUTES[name]):
            axis_copies[name][i + 1].start()
        elif len(left) == 1:
            to_pair(name, total)
        else:
            for each in far_copies[name]:
                each.start()

    def to_pair(name, total):
        width = total.shape[1] // 2
        getattr(n, "to_" + name)[...] = total[:, width:].astype(BF16)
        pair_copies[name].start()
        put(name, total[:, :width])

    def far_total(name, pair):
        r2, far = getattr(n, "r2_" + name), n_far(name)
        total = None
        if pair == 0 or name == DOWN:
            first, second = left_after(name, 1)
            view = (bits[first], bits[second])
            total = r2[view + half_of(name, 0) if name in CHUNKS else view].astype(F32)
        for k in range(3) if pair == 0 or name == DOWN else range(3, 7):
            far_copies[name][k].wait_recv()
            part = far[(k + 1) % 4]
            if name in CHUNKS:
                part = part[:, : 128 * len(CHUNKS[name][pair])]
            part = part.astype(F32)
            total = part if total is None else total + part
        return total

    def far_done(name):
        if not inside:
            return
        total = far_total(name, 0)
        if name in pair_copies and name != DOWN:
            to_pair(name, total)
        else:
            put(name, total)

    def far_done_target(name):
        if not inside:
            return
        if name in CHUNKS:
            total = far_total(name, 1)
        elif name == DOWN:
            pair_copies[name].wait_recv()
            axis_copies[name][0].start()
            axis_done(name)
            total = far_total(name, 1)
        else:
            pair_copies[name].wait_recv()
            total = getattr(n, "from_" + name)[...].astype(F32)
        put(name, total, 1)

    gain_copies = []
    if inside:
        gain_copies = [
            copy(n.gain_out.at[0], n.gain_in.at[0], sibling),
            copy(n.gain_out.at[1], n.gain_in.at[1], across[ROW]),
        ]
        for k in range(7):
            offset, pair = (k + 1) % 4, 0 if k < 3 else 1
            gain_copies.append(
                copy(
                    n.gain_out.at[2],
                    n.gain_in.at[2 + offset],
                    at_quarter((quarter + offset) % 4, pair),
                )
            )

    def gain_step(i):
        if not inside:
            return
        gain_copies[i].wait()
        n.gain_out[i + 1] = n.gain_out[i] + n.gain_in[i]
        for each in gain_copies[1:2] if i == 0 else gain_copies[2:]:
            each.start()

    def gain_owner(pair):
        if not inside:
            n.grad_gains[...] = n.gain_out[0]
            return
        total = n.gain_out[2] if pair == 0 else None
        for k in range(3) if pair == 0 else range(3, 7):
            gain_copies[2 + k].wait_recv()
            part = n.gain_in[2 + (k + 1) % 4]
            total = part if total is None else total + part
        n.grad_gains[...] = total

    def turned(ref):
        return jnp.transpose(rows_of(ref, 0, d))

    def product(left, right):
        return dot_nn(left[...], right.reshape(seq_count * LP, right.shape[2]))

    def blocks(value):
        return value.astype(BF16).reshape(2, 2, 2, 2, d // 16, value.shape[1])

    @pl.when(online)
    def _():
        n.turned_one[...] = turned(n.normed_one)
        n.turned_two[...] = turned(n.normed_two)
        n.turned_mixed[...] = turned(n.attended)
        aims_copy.wait_recv()
        differ = n.picked[...] - n.aims_in[...]
        weighted = jnp.where(real, seq_weight * differ, 0.0)
        n.coef[...] = weighted
        stat_first(jnp.sum(0.5 * weighted * jnp.where(real, differ, 0.0)))

        @pl.loop(0, seq_count)
        def _(s):
            backward_head(n, s)

        n.turned_ffn[...] = turned(n.grad_ffn)

        @pl.loop(0, ff // 512)
        def _(j):
            columns = pl.ds(pl.multiple_of(j * 512, 512), 512)
            value = product(n.turned_ffn, n.active[:, :, columns]).astype(BF16)
            for c in range(4):
                n.g_down[j // 2, j % 2, c // 2, c % 2] = value[:, 128 * c : 128 * c + 128]

        core_start(DOWN)
        value = None
        for s in range(seq_count):
            part = dot_nn(n.grad_q[s], n.final_low[s])
            value = part if value is None else value + part
        n.g_head[...] = blocks(jnp.transpose(value))
        core_start(HEAD)
        stat_next(0)

        @pl.loop(0, seq_count // 2)
        def _(t):
            backward_upper(n, 2 * t)

        core_done(DOWN)
        core_done(HEAD)

        def up_product(ref, tiles, first):
            @pl.loop(0, 2 * tiles)
            def _(j):
                columns = pl.ds(
                    pl.multiple_of((j // tiles) * (ff // 2) + first + (j % tiles) * 512, 512), 512
                )
                here = pl.ds(pl.multiple_of(j * 512, 512), 512)
                ref[:, :, :, :, :, here] = blocks(product(n.turned_two, n.slope[:, :, columns]))

        if inside:
            up_product(n.g_up_a, ff // 4 // 512, 0)
            core_start(UP_A)
            up_product(n.g_up_b, ff // 4 // 512, ff // 4)
            core_start(UP_B)
        else:
            up_product(n.g_up, ff // 2 // 512, 0)
        stat_next(1)

        @pl.loop(0, seq_count // 2)
        def _(t):
            backward_middle(n, 2 * t)

            @pl.when(t == 0)
            def _():
                core_done(UP_A)

            @pl.when(t == 1)
            def _():
                core_done(UP_B)

        n.g_out[...] = blocks(product(n.turned_mixed, n.grad_branch[...]))
        core_start(OUT)
        stat_next(2)

        @pl.loop(0, seq_count)
        def _(s):
            attend_back(n, [(s, pair) for pair in range(d // 128)], d)
            backward_states(n, s)
            state_copy(s).start()

            @pl.when(s == 0)
            def _():
                axis_done(DOWN)
                axis_done(HEAD)
                core_done(OUT)

            @pl.when(s == 1)
            def _():
                stat_next(3)
                axis_done(UP_A)

            @pl.when(s == 2)
            def _():
                axis_done(UP_B)

            @pl.when(s == 3)
            def _():
                axis_done(OUT)
                far_done(HEAD)
                axis_done(UP_A, 1)

        n.gain_out[0, 0:1, :] = jnp.sum(n.gain_sums[0], axis=0, keepdims=True)
        n.gain_out[0, 1:2, :] = jnp.sum(n.gain_sums[1], axis=0, keepdims=True)
        n.gain_out[0, 2:8, :] = jnp.zeros((6, d), F32)

        def qkv_product(first, *names):
            width = 256 // len(names)
            for half in range(2):
                at = half * (3 * d // 2) + first
                value = blocks(product(n.turned_one, n.qkv[:, :, at : at + 256]))
                for i, name in enumerate(names):
                    getattr(n, "g_" + name)[..., half * width : (half + 1) * width] = value[
                        ..., i * width : (i + 1) * width
                    ]
            for name in names:
                core_start(name)

        if inside:
            gain_copies[0].start()
            qkv_product(0, QKV_0)
            axis_done(UP_B, 1)
            qkv_product(256, QKV_1)
            core_done(QKV_0)
            qkv_product(512, QKV_2, QKV_3)
            core_done(QKV_1)
            core_done(QKV_2)
            core_done(QKV_3)
            gain_step(0)
            far_done(DOWN)
            axis_done(UP_A, 2)
        else:
            for first in range(0, 3 * d, 256):
                n.g_qkv[..., first : first + 256] = blocks(
                    product(n.turned_one, n.qkv[:, :, first : first + 256])
                )
        for s in range(0, seq_count, 2):
            n.state_out[s * L : (s + 2) * L] = without_pad(n.grad_states, s, d // 2)
            n.q_out[s * L : (s + 2) * L] = without_pad(n.q_rows, s, 128)
        axis_done(QKV_0)
        if inside:
            gain_step(1)
        axis_done(QKV_1)
        axis_done(QKV_2)
        axis_done(QKV_3)
        far_done(OUT)
        axis_done(UP_B, 2)
        gain_owner(0)
        for name in CHUNKS:
            far_done(name)
        q_copy.wait_send()
        for s in range(seq_count):
            state_copy(s).wait_send()
        for each in pair_copies.values():
            each.wait_send()
        for each in gain_copies[2:] + [each for sent in far_copies.values() for each in sent]:
            each.wait_send()

    @pl.when(jnp.logical_not(online))
    def _():
        stat_first(0.0)
        for i in range(4):
            stat_next(i)
        far_done_target(DOWN)
        q_copy.wait_recv()
        for s in range(0, seq_count, 2):
            n.q_out[s * L : (s + 2) * L] = without_pad(n.q_half, s, 128)
        for s in range(seq_count):
            state_copy(s).wait_recv()
            if s % 2:
                n.state_out[(s - 1) * L : (s + 1) * L] = without_pad(n.state_half, s - 1, d // 2)
        for name in (HEAD, UP_A, UP_B, OUT):
            far_done_target(name)
        if inside:
            gain_owner(1)
        for name in CHUNKS:
            far_done_target(name)
        aims_copy.wait_send()
        if inside:
            for each in far_copies[DOWN]:
                each.wait_send()

    if inside:
        stat_next(4)
        n.stats[...] = n.stat_out[5]
    else:
        n.stats[...] = n.stat_out[0]
    assert used[0] <= SEMAPHORES


OUTPUTS = (
    "q_out",
    "state_out",
    GRAD_GAINS,
    "grad_qkv",
    "grad_out",
    "grad_up",
    GRAD_DOWN,
    "grad_head",
    NEW_GAINS,
    "new_qkv",
    "new_out",
    "new_up",
    "new_down",
    "new_head",
    STATS,
)


def finish_kernel(moved, worked, token_total, data_count, *refs):
    source = dict(zip(moved + worked, refs))
    result = dict(zip(OUTPUTS, refs[len(source) :]))
    sems = refs[-1]
    copies = [
        pltpu.make_async_copy(source[name], result[name], sems.at[i])
        for i, name in enumerate(moved)
    ]
    for copy in copies:
        copy.start()
    me_pair = lax.axis_index(PAIR)
    me = lax.axis_index(DP)
    for name in (GRAD_GAINS, NEW_GAINS):
        height = source[name].shape[1] // data_count
        here = source[name][:, pl.ds(pl.multiple_of(me * height // 128 * 128, 128), 128)]
        value = here[:, :height]
        for at in range(height, 128, height):
            value = jnp.where(me * height % 128 == at, here[:, at : at + height], value)
        result[name][...] = jnp.where(me_pair == 0, value[0:1], value[1:2])
    if GRAD_DOWN in worked:
        result[GRAD_DOWN][...] = jnp.transpose(source[GRAD_DOWN][...])
    stats = source[STATS]
    result[STATS][0] = stats[0, 0] / token_total
    result[STATS][1] = stats[0, 1] / token_total
    result[STATS][2] = stats[1, 0]
    result[STATS][3] = stats[0, 2] / token_total
    result[STATS][4] = stats[1, 1]
    for copy in copies:
        copy.wait()


def add_outside(out, params, pair_index, data_index, data_count):
    online = pair_index == 0
    other = 1 - pair_index

    def half(matrix, which):
        width = matrix.shape[1] // 2
        return lax.dynamic_slice_in_dim(matrix, which * width, width, 1)

    def piece(matrix, which):
        height = matrix.shape[0] // data_count
        return half(lax.dynamic_slice_in_dim(matrix, data_index * height, height, 0), which)

    def swapped(value):
        return lax.ppermute(value, PAIR, [(0, 1), (1, 0)])

    for name in TENSORS:
        grad = out["g_" + name].astype(F32)
        grad = grad.reshape((16,) + grad.shape[4:])
        if name == DOWN:
            grad = jnp.swapaxes(grad, 1, 2)
        grad = lax.psum_scatter(
            grad.reshape(-1, grad.shape[2]), DP, scatter_dimension=0, tiled=True
        )
        received = swapped(half(grad, other))
        out["grad_" + name] = jnp.where(online, half(grad, pair_index), received)
    gains = lax.psum(out[GRAD_GAINS], DP)
    out[GRAD_GAINS] = jnp.where(online, gains, swapped(gains))
    for name, weight in zip((GAINS, QKV, OUT, UP, DOWN, HEAD), params):
        if name == GAINS:
            weight = jnp.pad(weight.T, ((0, 6), (0, 0)))
            mine, received = weight.astype(F32), swapped(weight).astype(F32)
        else:
            mine = piece(weight, pair_index).astype(F32)
            received = swapped(piece(weight, other)).astype(F32)
        first, second = jnp.where(online, mine, received), jnp.where(online, received, mine)
        out["new_" + name] = second + SOFT_RATE * (first - second)
    sums = lax.psum(out[STATS][0:1], (PAIR, DP))
    bests = lax.pmax(out[STATS][1:2], (PAIR, DP))
    out[STATS] = jnp.concatenate([sums, bests])


def local(
    states, norm_gains, w_qkv, w_out, w_up, w_down, w_head, task_ids, chosen, reward, finished
):
    pair_index = lax.axis_index(PAIR)
    data_index = lax.axis_index(DP)
    data_count = lax.axis_size(DP)
    row_count, d = states.shape[1:]
    ff = w_up.shape[2]
    bin_count = w_head.shape[2]
    seq_count = row_count // L

    inside = data_count == 16
    rows = (seq_count, LP, d)
    inputs = dict(
        states=states[0],
        norm_gains=norm_gains[0].T,
        hbm_qkv=w_qkv[0],
        hbm_out=w_out[0],
        hbm_up=w_up[0],
        hbm_down=w_down[0],
        hbm_head=w_head[0],
        task_ids=task_ids,
        chosen=chosen,
        reward=reward,
        finished=finished,
    )
    if not inside:
        table = (task_ids[:, None] == jnp.arange(128, dtype=jnp.int32)[None, :]).astype(F32)
        inputs["counts"] = jnp.broadcast_to(
            lax.psum(jnp.sum(table, axis=0, keepdims=True), DP), (8, 128)
        )
    piece = {
        QKV: (d // 16, 3 * d),
        OUT: (d // 16, d),
        UP: (d // 16, ff),
        HEAD: (d // 16, bin_count),
        DOWN: (d, ff // 16),
    }
    halves = {
        name: (shape[0] // 2, shape[1]) if name == DOWN else (shape[0], shape[1] // 2)
        for name, shape in piece.items()
    }
    new_shapes = dict(halves, down=(ff // 16, d // 2))
    outputs = dict(
        q_out=((row_count, bin_count // 2), BF16),
        state_out=((row_count, d // 2), BF16),
        grad_gains=((8, d), F32),
        new_gains=((8, d), F32),
        stats=((8, 128), F32),
    )
    for name in TENSORS:
        if inside:
            outputs["grad_" + name] = (halves[name], F32)
            outputs["new_" + name] = (new_shapes[name], F32)
        else:
            outputs["g_" + name] = ((2, 2, 2, 2) + piece[name], BF16)
    scratch = dict(
        w_qkv=((d, 3 * d), BF16),
        w_out=((d, d), BF16),
        w_up=((d, ff), BF16),
        w_down=((ff, d), BF16),
        w_head=((d, bin_count), BF16),
        x=(rows, BF16),
        gains=((8, d), F32),
        flat=((8, -(-(row_count + LP - L) // 128) * 128), F32),
        aux=((seq_count, 8, LP), F32),
        table=((8, 128), F32),
        normed_one=(rows, BF16),
        qkv=((seq_count, LP, 3 * d), BF16),
        powers_0=((seq_count, d // 128) + (2 * BLOCKS[0][1], BLOCKS[0][2]), BF16),
        powers_1=((seq_count, d // 128) + (2 * BLOCKS[1][1], BLOCKS[1][2]), BF16),
        powers_2=((seq_count, d // 128) + (2 * BLOCKS[2][1], BLOCKS[2][2]), BF16),
        inverse_totals=(rows, F32),
        attended=(rows, BF16),
        middle=(rows, F32),
        normed_two=(rows, BF16),
        active=((seq_count, LP, ff), BF16),
        slope=((seq_count, LP, ff), BF16),
        final_low=(rows, BF16),
        q_rows=((seq_count, LP, bin_count), BF16),
        q_half=((seq_count, LP, bin_count // 2), BF16),
        picked=((8, LP), F32),
        tops=((8, LP), F32),
        coef=((8, LP), F32),
        aims_out=((8, LP), F32),
        aims_in=((8, LP), F32),
        grad_q=((seq_count, bin_count, LP), BF16),
        grad_ffn=(rows, BF16),
        turned_one=((d, seq_count * LP), BF16),
        turned_two=((d, seq_count * LP), BF16),
        turned_mixed=((d, seq_count * LP), BF16),
        turned_ffn=((d, seq_count * LP), BF16),
        state_half=((seq_count, LP, d // 2), BF16),
        gain_sums=((2, 8, d), F32),
        gain_out=((3, 8, d), F32),
        gain_in=((6, 8, d), F32),
        count_out=((2, 8, 128), F32),
        count_in=((8, 8, 128), F32),
        stat_out=((6, 8, 128), F32),
        stat_in=((5, 8, 128), F32),
        their_gains=((8, d), F32),
    )
    if inside:
        for name in TENSORS:
            scratch["their_" + name] = (new_shapes[name], BF16)
        scratch["half_down"] = ((2, 2, 2) + halves[DOWN], BF16)
        for name, route in ROUTES.items():
            if name in CHUNKS:
                far = (d // 16, 128 * len(CHUNKS[name][0]))
                shape = (far[0], 2 * far[1])
            elif name == DOWN:
                shape, far = piece[DOWN], halves[DOWN]
            else:
                shape = far = (d // 16, ff // 2) if name in (UP_A, UP_B) else piece[name]
                scratch["to_" + name] = (shape[0], shape[1] // 2), BF16
                scratch["from_" + name] = (shape[0], shape[1] // 2), BF16
            scratch["g_" + name] = ((2, 2, 2, 2) + shape, BF16)
            scratch["r1_" + name] = ((2, 2, 2) + shape, BF16)
            for i in range(len(route)):
                scratch[f"r{i + 2}_{name}"] = ((2,) * (2 - i) + (far if name == DOWN else shape), BF16)
            if len(route) == 1:
                scratch["far_" + name] = ((4,) + far, BF16)
    names = list(inputs) + list(outputs) + list(scratch) + ["send_sem", "recv_sem", "load_sem"]
    in_vmem = pl.BlockSpec(memory_space=pltpu.VMEM)
    in_smem = pl.BlockSpec(memory_space=pltpu.SMEM)
    anywhere = pl.BlockSpec(memory_space=pl.ANY)
    raw = pl.pallas_call(
        functools.partial(layer_kernel, names, data_count, inside),
        out_shape=[jax.ShapeDtypeStruct(shape, dtype) for shape, dtype in outputs.values()],
        in_specs=[
            in_smem if name == "task_ids" else anywhere if name[:3] == "hbm" else in_vmem
            for name in inputs
        ],
        out_specs=[in_vmem] * len(outputs),
        scratch_shapes=[pltpu.VMEM(shape, dtype) for shape, dtype in scratch.values()]
        + [pltpu.SemaphoreType.DMA((SEMAPHORES,)), pltpu.SemaphoreType.DMA((SEMAPHORES,))]
        + [pltpu.SemaphoreType.DMA((5,))],
        compiler_params=pltpu.CompilerParams(
            collective_id=0, has_side_effects=True, vmem_limit_bytes=64 * 1024 * 1024 - 65536
        ),
        name="layer",
    )(*inputs.values())
    out = dict(zip(outputs, raw))
    if not inside:
        params = (norm_gains[0], w_qkv[0], w_out[0], w_up[0], w_down[0], w_head[0])
        add_outside(out, params, pair_index, data_index, data_count)
    moved = {name: out[name] for name in OUTPUTS if name not in (GRAD_GAINS, NEW_GAINS, STATS)}
    worked = {name: out[name] for name in (GRAD_GAINS, NEW_GAINS, STATS)}
    results = {name: jax.ShapeDtypeStruct(value.shape, value.dtype) for name, value in moved.items()}
    if inside:
        worked[GRAD_DOWN] = moved.pop(GRAD_DOWN)
        results[GRAD_DOWN] = jax.ShapeDtypeStruct((ff // data_count, d // 2), F32)
    results[GRAD_GAINS] = results[NEW_GAINS] = jax.ShapeDtypeStruct((1, d // data_count), F32)
    results[STATS] = jax.ShapeDtypeStruct((5,), F32)
    spec_of = {name: anywhere if name in moved else in_vmem for name in OUTPUTS}
    spec_of[STATS] = in_smem
    final = pl.pallas_call(
        functools.partial(
            finish_kernel, list(moved), list(worked), row_count * data_count, data_count
        ),
        out_shape=[results[name] for name in OUTPUTS],
        in_specs=[in_vmem] * (len(moved) + len(worked)),
        out_specs=[spec_of[name] for name in OUTPUTS],
        scratch_shapes=[
            pltpu.SemaphoreType.DMA((len(moved),)),
        ],
        name="finish",
    )(*moved.values(), *worked.values())
    final = dict(zip(OUTPUTS, final))
    for name in (GRAD_GAINS, NEW_GAINS):
        final[name] = final[name].T
    return tuple(final.values())


def solution(mesh):
    placed = (
        P(PAIR, DP, None),
        P(PAIR, None, None),
        P(PAIR, None, None),
        P(PAIR, None, None),
        P(PAIR, None, None),
        P(PAIR, None, None),
        P(PAIR, None, None),
        P(DP),
        P(DP),
        P(DP),
        P(DP),
    )
    return jax.shard_map(
        local,
        mesh=mesh,
        in_specs=placed,
        out_specs=(P(DP, PAIR),) * 14 + (P(),),
        check_vma=False,
    )
```

```python
import functools

import jax
import jax.numpy as jnp
from jax import lax
from jax.experimental import pallas as pl
from jax.experimental.pallas import tpu as pltpu
from jax.sharding import PartitionSpec as P

F32 = jnp.float32
BF16 = jnp.bfloat16
MESH = pl.DeviceIdType.MESH

DOWN = "down"
PAIR = "pair"
DP = "dp"
STATS = "stats"
ROW = "row"
HEAD = "head"
UP_B = "up_b"
OUT = "out"
UP_A = "up_a"
LOW = "low"
GRAD_GAINS = "grad_gains"
HIGH = "high"
GRAD_DOWN = "grad_down"
NEW_GAINS = "new_gains"
QKV_0 = "qkv_0"
QKV_1 = "qkv_1"
QKV_2 = "qkv_2"
QKV_3 = "qkv_3"
UP = "up"
QKV = "qkv"
GAINS = "gains"

HEAD_DIM = 64
L = 296
LP = 304
TASKS = 32
EPSILON = 1e-06
DISCOUNT = 0.98
SOFT_RATE = 0.2
SCORE_SCALE = 0.125
NEG_LARGE = -1000000000.0
LOWEST = -1e30

BLOCKS = ((0, 128, 128), (128, 128, 256), (256, 48, 304))


def dot_nn(a, b):
    return lax.dot_general(a, b, (((1,), (0,)), ((), ())), preferred_element_type=F32)


def dot_nt(a, b):
    return lax.dot_general(a, b, (((1,), (1,)), ((), ())), preferred_element_type=F32)


def dot_tn(a, b):
    return lax.dot_general(a, b, (((0,), (0,)), ((), ())), preferred_element_type=F32)


def dot_tt(a, b):
    return lax.dot_general(a, b, (((0,), (1,)), ((), ())), preferred_element_type=F32)


def inverse_rms(values):
    return lax.rsqrt(jnp.mean(values * values, axis=-1, keepdims=True) + EPSILON)


def gelu_and_slope(u):
    c = 0.7978845608028654
    square = u * u
    t = jnp.tanh(u * (c + (c * 0.044715) * square))
    half = 0.5 * t + 0.5
    slope = half + (u * (0.5 - 0.5 * t * t)) * (c + (3 * c * 0.044715) * square)
    return u * half, slope


def lane_halves(a):
    lane = lax.broadcasted_iota(jnp.int32, (1, 2 * HEAD_DIM), 1)
    zero = jnp.zeros((), a.dtype)
    return jnp.where(lane < HEAD_DIM, a, zero), jnp.where(lane >= HEAD_DIM, a, zero)


def rows_of(ref, first, width):
    value = ref[:, :, first : first + width]
    return value.reshape(value.shape[0] * value.shape[1], width)


def without_pad(ref, s, width):
    rows = [ref[s + i, :, :width].astype(F32)[:L] for i in range(2)]
    return jnp.concatenate(rows, axis=0).astype(BF16)


class Names:
    pass


def in_steps(count, first, second, third):
    for item in range(count + 2):
        if item < count:
            first(item)
        if 0 <= item - 1 < count:
            second(item - 1)
        if item >= 2:
            third(item - 2)


def attend(n, items, d):
    corner = lax.broadcasted_iota(jnp.int32, (128, 128), 0) >= lax.broadcasted_iota(
        jnp.int32, (128, 128), 1
    )
    ones = jnp.ones((LP, 128), BF16)
    marks = lane_halves(ones)
    raw, raised = {}, {}

    def score(item):
        s, pair = items[item]
        at = 128 * pair
        queries = lane_halves(n.qkv[s, :, at : at + 128] * jnp.array(SCORE_SCALE, BF16))
        keys = n.qkv[s, :, d + at : d + at + 128]
        for block, (first, rows, seen) in enumerate(BLOCKS):
            both = jnp.concatenate([q[first : first + rows] for q in queries], axis=0)
            raw[item, block] = dot_nt(both, keys[:seen])

    def raise_scores(item):
        s, pair = items[item]
        for block, (first, rows, seen) in enumerate(BLOCKS):
            scores = raw.pop((item, block))
            visible = jnp.concatenate([corner[:rows, :rows]] * 2, axis=0)
            diagonal = jnp.where(visible, scores[:, first:], NEG_LARGE)
            scores = jnp.concatenate([scores[:, :first], diagonal], axis=1) if first else diagonal
            powers = jnp.exp(scores - jnp.max(scores, axis=-1, keepdims=True)).astype(BF16)
            raised[item, block] = powers
            n.powers[block][s, pair] = powers

    def mix(item):
        s, pair = items[item]
        at = 128 * pair
        values = lane_halves(n.qkv[s, :, 2 * d + at : 2 * d + at + 128])
        wide = [jnp.concatenate(both, axis=1) for both in zip(values, marks)]
        for block, (first, rows, seen) in enumerate(BLOCKS):
            powers = raised.pop((item, block))
            if seen % 128 == 0:
                mixed = dot_nn(
                    jnp.concatenate([powers[:rows], powers[rows:]], axis=1),
                    jnp.concatenate([w[:seen] for w in wide], axis=0),
                )
            else:
                mixed = dot_nn(powers[:rows], wide[0][:seen]) + dot_nn(powers[rows:], wide[1][:seen])
            inverse = 1.0 / mixed[:, 128:]
            n.inverse_totals[s, first : first + rows, at : at + 128] = inverse
            n.attended[s, first : first + rows, at : at + 128] = (mixed[:, :128] * inverse).astype(
                BF16
            )

    in_steps(len(items), score, raise_scores, mix)


def lay_out_inputs(n, seq_count):
    d = n.x.shape[2]
    pad = jnp.zeros((LP - L, d), F32)
    for s in range(0, seq_count, 2):
        both = n.states[s * L : (s + 2) * L].astype(F32)
        for i in range(2):
            n.x[s + i] = jnp.concatenate([both[i * L : (i + 1) * L], pad], axis=0).astype(BF16)
    n.flat[...] = jnp.zeros_like(n.flat)
    for i, ref in enumerate((n.chosen, n.reward, n.finished)):
        n.flat[i : i + 1, : seq_count * L] = ref[...].reshape(1, seq_count * L).astype(F32)
    for s in range(seq_count):
        n.aux[s] = n.flat[:, s * L : s * L + LP]
    n.gains[...] = jnp.zeros_like(n.gains)
    n.gains[0:2, :] = n.norm_gains[...].astype(F32)
    seq = lax.broadcasted_iota(jnp.int32, (8, 128), 0)
    task = lax.broadcasted_iota(jnp.int32, (8, 128), 1)
    table = jnp.zeros((8, 128), F32)
    for s in range(seq_count):
        table = jnp.where(jnp.logical_and(seq == s, task == n.task_ids[s]), 1.0, table)
    n.table[...] = table


def forward_sequences(n, s, online, loads):
    both = pl.ds(s, 2)
    d = n.x.shape[2]
    ff = n.w_up.shape[1]

    def rows(ref):
        return ref[both].reshape(2 * LP, ref.shape[2])

    def split(value):
        return value.astype(BF16).reshape(2, LP, value.shape[1])

    x = rows(n.x).astype(F32)
    normed = (x * inverse_rms(x) * n.gains[0:1, :]).astype(BF16)
    n.normed_one[both] = split(normed)
    for first in range(0, 3 * d, 256):
        n.qkv[both, :, first : first + 256] = split(
            dot_nn(normed, n.w_qkv[:, first : first + 256])
        )
    attend(n, [(s + i, pair) for i in range(2) for pair in range(d // 128)], d)

    @pl.when(s == 0)
    def _():
        for load in loads:
            load.wait()

    middle = rows(n.x).astype(F32) + dot_nn(rows(n.attended), n.w_out[...])
    n.middle[both] = middle.reshape(2, LP, d)
    normed = (middle * inverse_rms(middle) * n.gains[1:2, :]).astype(BF16)
    n.normed_two[both] = split(normed)

    @pl.when(online)
    def _():
        for first in range(0, ff, 256):
            active, slope = gelu_and_slope(dot_nn(normed, n.w_up[:, first : first + 256]))
            n.active[both, :, first : first + 256] = split(active)
            n.slope[both, :, first : first + 256] = split(slope)

    @pl.when(jnp.logical_not(online))
    def _():
        for first in range(0, ff, 256):
            active, _ = gelu_and_slope(dot_nn(normed, n.w_up[:, first : first + 256]))
            n.active[both, :, first : first + 256] = split(active)

    final_low = (rows(n.middle) + dot_nn(rows(n.active), n.w_down[...])).astype(BF16)
    n.final_low[both] = split(final_low)
    n.q_rows[both] = split(dot_nn(final_low, n.w_head[...]))
    for i in range(2):
        q_columns = dot_tt(n.w_head[...], n.final_low[s + i])
        bins = lax.broadcasted_iota(jnp.int32, q_columns.shape, 0)
        chosen = n.aux[s + i, 0:1, :].astype(jnp.int32)
        n.picked[pl.ds(s + i, 1), :] = jnp.sum(
            jnp.where(bins == chosen, q_columns, 0.0), axis=0, keepdims=True
        )
        n.tops[pl.ds(s + i, 1), :] = jnp.max(q_columns, axis=0, keepdims=True)


def backward_head(n, s):
    bins = lax.broadcasted_iota(jnp.int32, (n.w_head.shape[1], LP), 0)
    chosen = n.aux[s, 0:1, :].astype(jnp.int32)
    grad_q = jnp.where(bins == chosen, n.coef[pl.ds(s, 1), :], 0.0).astype(BF16)
    n.grad_q[s] = grad_q
    n.grad_ffn[s] = dot_tt(grad_q, n.w_head[...]).astype(BF16)


def backward_upper(n, s):
    both = pl.ds(s, 2)
    ff = n.w_up.shape[1]
    grad_ffn = n.grad_ffn[both].reshape(2 * LP, -1)
    for first in range(0, ff, 256):
        grad_active = dot_nt(grad_ffn, n.w_down[first : first + 256, :])
        slope = n.slope[both, :, first : first + 256].astype(F32)
        n.slope[both, :, first : first + 256] = (
            grad_active.reshape(2, LP, 256) * slope
        ).astype(BF16)


def backward_middle(n, s):
    both = pl.ds(s, 2)
    d = n.x.shape[2]
    grad_two = dot_nt(n.slope[both].reshape(2 * LP, -1), n.w_up[...])
    middle = n.middle[both].reshape(2 * LP, d)
    inverse = inverse_rms(middle)
    normal = middle * inverse
    n.gain_sums[1] += jnp.sum((grad_two * normal).reshape(2 * LP // 8, 8, d), axis=0)
    inner = grad_two * n.gains[1:2, :]
    grad_final = jnp.concatenate(
        [dot_tt(n.grad_q[s + i], n.w_head[...]) for i in range(2)], axis=0
    )
    grad_middle = grad_final + inverse * (
        inner - normal * jnp.mean(inner * normal, axis=-1, keepdims=True)
    )
    n.middle[both] = grad_middle.reshape(2, LP, d)
    grad_branch = grad_middle.astype(BF16)
    n.grad_branch[both] = grad_branch.reshape(2, LP, d)
    n.grad_mixed[both] = dot_nt(grad_branch, n.w_out[...]).astype(BF16).reshape(2, LP, d)


def attend_back(n, items, d):
    side = lax.broadcasted_iota(jnp.int32, (256, 256), 0) % 128 < HEAD_DIM
    head = lax.broadcasted_iota(jnp.int32, (256, 256), 1) < 128
    head_sums = jnp.where(side == head, jnp.ones((), BF16), jnp.zeros((), BF16))
    kept = {}

    def spread(item):
        s, pair = items[item]
        at = 128 * pair
        grads = (
            n.grad_mixed[s, :, at : at + 128].astype(F32) * n.inverse_totals[s, :, at : at + 128]
        ).astype(BF16)
        product = n.attended[s, :, at : at + 128].astype(F32) * grads.astype(F32)
        upper = product.astype(BF16)
        lower = (product - upper.astype(F32)).astype(BF16)
        centres = dot_nn(jnp.concatenate([upper, lower], axis=1), head_sums)
        values = n.qkv[s, :, 2 * d + at : 2 * d + at + 128]
        grads = lane_halves(grads)
        found = []
        for first, rows, seen in BLOCKS:
            both = jnp.concatenate([g[first : first + rows] for g in grads], axis=0)
            found.append((both, dot_nt(both, values[:seen])))
        kept[item] = centres, found

    def centre(item):
        s, pair = items[item]
        centres, found = kept[item]
        done = []
        for block, (first, rows, seen) in enumerate(BLOCKS):
            both, grad_powers = found[block]
            here = centres[first : first + rows]
            here = jnp.concatenate([here[:, :128], here[:, 128:]], axis=0)
            here = jnp.concatenate([here] * ((seen + 127) // 128), axis=1)[:, :seen]
            powers = n.powers[block][s, pair]
            done.append((both, powers, (powers.astype(F32) * (grad_powers - here)).astype(BF16)))
        kept[item] = done

    def collect(item):
        s, pair = items[item]
        at = 128 * pair
        queries = lane_halves(n.qkv[s, :, at : at + 128])
        keys = lane_halves(n.qkv[s, :, d + at : d + at + 128])
        grad_keys = [None] * 3
        grad_values = [None] * 3
        done = kept.pop(item)
        for block, (first, rows, seen) in enumerate(BLOCKS):
            both, powers, grad_scores = done[block]
            both_queries = jnp.concatenate([q[first : first + rows] for q in queries], axis=0)
            if seen % 128 == 0:
                grad_queries = dot_nn(
                    jnp.concatenate([grad_scores[:rows], grad_scores[rows:]], axis=1),
                    jnp.concatenate([k[:seen] for k in keys], axis=0),
                )
            else:
                grad_queries = dot_nn(grad_scores[:rows], keys[0][:seen]) + dot_nn(
                    grad_scores[rows:], keys[1][:seen]
                )
            of_values = dot_tn(powers, both)
            of_keys = dot_tn(grad_scores, both_queries)
            for i, start in enumerate((0, 128, 256)):
                if start < seen:
                    end = min(start + 128, seen)
                    piece = of_values[start:end]
                    grad_values[i] = piece if grad_values[i] is None else grad_values[i] + piece
                    piece = of_keys[start:end]
                    grad_keys[i] = piece if grad_keys[i] is None else grad_keys[i] + piece
            n.qkv[s, first : first + rows, at : at + 128] = (grad_queries * SCORE_SCALE).astype(
                BF16
            )
        for i, (first, rows, _) in enumerate(BLOCKS):
            n.qkv[s, first : first + rows, d + at : d + at + 128] = (
                grad_keys[i] * SCORE_SCALE
            ).astype(BF16)
            n.qkv[s, first : first + rows, 2 * d + at : 2 * d + at + 128] = grad_values[i].astype(
                BF16
            )

    in_steps(len(items), spread, centre, collect)


def backward_states(n, s):
    grad_one = dot_nt(n.qkv[s], n.w_qkv[...])
    x = n.x[s].astype(F32)
    inverse = inverse_rms(x)
    normal = x * inverse
    n.gain_sums[0] += jnp.sum((grad_one * normal).reshape(LP // 8, 8, -1), axis=0)
    inner = grad_one * n.gains[0:1, :]
    n.grad_states[s] = (
        n.middle[s]
        + inverse * (inner - normal * jnp.mean(inner * normal, axis=-1, keepdims=True))
    ).astype(BF16)


ROUTES = {
    DOWN: ((), (ROW,)),
    HEAD: ((ROW,), ()),
    UP_A: ((ROW, LOW), (HIGH,)),
    UP_B: ((LOW, ROW), (HIGH,)),
    OUT: ((ROW,), ()),
    QKV_0: ((ROW,), ()),
    QKV_1: ((LOW,), ()),
    QKV_2: ((ROW,), ()),
    QKV_3: ((LOW,), ()),
}
CHUNKS = {QKV_0: (0, 256), QKV_1: (256, 512), QKV_2: (512, 640), QKV_3: (640, 768)}
STRIDES = {HIGH: 8, LOW: 4, ROW: 2}
TENSORS = (DOWN, HEAD, UP, OUT, QKV)
AXES = (HIGH, LOW, ROW)
SEMAPHORES = 160


def layer_kernel(names, data_count, inside, *refs):
    n = Names()
    for name, ref in zip(names, refs):
        setattr(n, name, ref)
    n.powers = (n.powers_0, n.powers_1, n.powers_2)
    n.grad_states, n.grad_branch, n.grad_mixed = n.normed_one, n.normed_two, n.final_low
    d = n.x.shape[2]
    ff = n.w_up.shape[1]
    seq_count = n.x.shape[0]

    me_pair = lax.axis_index(PAIR)
    me = lax.axis_index(DP)
    other = 1 - me_pair
    online = me_pair == 0
    core = me % 2
    row = (me // 2) % 2
    low = (me // 4) % 2
    high = me // 8
    quarter = me // 4
    bits = {ROW: row, LOW: low, HIGH: high}
    sibling = (me_pair, me + 1 - 2 * core)
    partner = (other, me)
    across = {
        "core": sibling,
        ROW: (me_pair, me + 2 - 4 * row),
        LOW: (me_pair, me + 4 - 8 * low),
        HIGH: (me_pair, me + 8 - 16 * high),
        PAIR: partner,
    }

    def at_quarter(which, pair):
        return (pair, me + 4 * (which - quarter))

    used = [0]

    def copy(src, dst, device):
        sem = used[0]
        used[0] += 1
        return pltpu.make_async_remote_copy(
            src_ref=src,
            dst_ref=dst,
            send_sem=n.send_sem.at[sem],
            recv_sem=n.recv_sem.at[sem],
            device_id=device,
            device_id_type=MESH,
        )

    barrier = pltpu.get_barrier_semaphore()
    friends = [partner]
    if inside:
        friends.append(sibling)
        for offset in range(1, 8):
            place = 2 * ((me // 2 + offset) % 8) + core
            friends += [(me_pair, place), (other, place)]
    loads = [
        pltpu.make_async_copy(src, dst, n.load_sem.at[i])
        for i, (src, dst) in enumerate(
            (
                (n.hbm_qkv, n.w_qkv),
                (n.hbm_out, n.w_out),
                (n.hbm_up, n.w_up),
                (n.hbm_down, n.w_down),
                (n.hbm_head, n.w_head),
            )
        )
    ]
    for load in loads:
        load.start()
    for friend in friends:
        pl.semaphore_signal(barrier, inc=1, device_id=friend, device_id_type=MESH)

    weights = {QKV: n.w_qkv, OUT: n.w_out, UP: n.w_up, DOWN: n.w_down, HEAD: n.w_head}

    def piece_of(ref, half):
        height = ref.shape[0] // data_count
        width = ref.shape[1] // 2
        return (
            pl.ds(pl.multiple_of(me * height, height), height),
            pl.ds(pl.multiple_of(half * width, width), width),
        )

    weight_copies = {}
    if inside:
        for name, ref in weights.items():
            weight_copies[name] = copy(
                ref.at[piece_of(ref, other)], getattr(n, "their_" + name), partner
            )
        weight_copies[GAINS] = copy(n.gains, n.their_gains, partner)

    count_copies = []
    if inside:
        count_copies.append(copy(n.count_out.at[0], n.count_in.at[0], sibling))
        for offset in range(1, 8):
            place = (me // 2 + offset) % 8
            count_copies.append(
                copy(n.count_out.at[1], n.count_in.at[offset], (me_pair, 2 * place + core))
            )

    n.gain_sums[...] = jnp.zeros_like(n.gain_sums)
    lay_out_inputs(n, seq_count)
    loads[0].wait()

    @pl.loop(0, seq_count // 2)
    def _(t):
        forward_sequences(n, 2 * t, online, loads[1:])

        @pl.when(t == 0)
        def _():
            pl.semaphore_wait(barrier, len(friends))
            if not inside:
                return
            n.count_out[0] = jnp.broadcast_to(
                jnp.sum(n.table[...], axis=0, keepdims=True), (8, 128)
            )
            count_copies[0].start()
            for each in weight_copies.values():
                each.start()

        @pl.when(t == 1)
        def _():
            if not inside:
                return
            count_copies[0].wait()
            n.count_out[1] = n.count_out[0] + n.count_in[0]
            for each in count_copies[1:]:
                each.start()

    lane = lax.broadcasted_iota(jnp.int32, (8, LP), 1)
    seq = lax.broadcasted_iota(jnp.int32, (8, LP), 0)
    real = jnp.logical_and(lane < L, seq < seq_count)
    tops = n.tops[...]
    aims_copy = copy(n.aims_out, n.aims_in, partner)
    q_copy = copy(n.q_rows.at[:, :, pl.ds(128, 128)], n.q_half, partner)
    state_sem = used[0]
    used[0] += seq_count

    def state_copy(s):
        return pltpu.make_async_remote_copy(
            src_ref=n.grad_states.at[s, :, pl.ds(d // 2, d // 2)],
            dst_ref=n.state_half.at[s],
            send_sem=n.send_sem.at[state_sem + s],
            recv_sem=n.recv_sem.at[state_sem + s],
            device_id=partner,
            device_id_type=MESH,
        )

    @pl.when(jnp.logical_not(online))
    def _():
        reward = jnp.concatenate([n.aux[s, 1:2, :] for s in range(seq_count)] * 2, axis=0)
        finished = jnp.concatenate([n.aux[s, 2:3, :] for s in range(seq_count)] * 2, axis=0)
        n.aims_out[...] = reward + DISCOUNT * (1.0 - finished) * tops
        aims_copy.start()

    @pl.when(online)
    def _():
        q_copy.start()

    if inside:
        for name, each in weight_copies.items():
            each.wait()
            if name == GAINS:
                mine, received = n.gains[...], n.their_gains[...]
            else:
                mine = weights[name][piece_of(weights[name], me_pair)].astype(F32)
                received = getattr(n, "their_" + name)[...].astype(F32)
            first = jnp.where(online, mine, received)
            second = jnp.where(online, received, mine)
            getattr(n, "new_" + name)[...] = second + SOFT_RATE * (first - second)
        counts = n.count_out[1]
        for i in range(1, 8):
            count_copies[i].wait()
            counts += n.count_in[i]
    else:
        counts = n.counts[...]
    seq_weight = (seq_count * data_count) / (
        TASKS * jnp.sum(n.table[...] * counts, axis=1, keepdims=True)
    )

    stat_row_id = lax.broadcasted_iota(jnp.int32, (8, 128), 0)
    stat_lane = lax.broadcasted_iota(jnp.int32, (8, 128), 1)
    stat_axes = ("core", ROW, LOW, HIGH, PAIR)
    stat_copies = [] if not inside else [
        copy(n.stat_out.at[i], n.stat_in.at[i], across[axis]) for i, axis in enumerate(stat_axes)
    ]

    def stat_first(loss):
        total = jnp.sum(jnp.where(real, tops, 0.0))
        best = jnp.max(jnp.where(real, tops, LOWEST))
        sums = jnp.where(stat_lane == 0, loss, jnp.where(stat_lane == 1 + me_pair, total, 0.0))
        bests = jnp.where(stat_lane == me_pair, best, LOWEST)
        n.stat_out[0] = jnp.where(stat_row_id == 0, sums, jnp.where(stat_row_id == 1, bests, 0.0))
        if inside:
            stat_copies[0].start()

    def stat_next(i):
        if not inside:
            return
        stat_copies[i].wait()
        mine, received = n.stat_out[i], n.stat_in[i]
        joined = jnp.where(stat_row_id == 1, jnp.maximum(mine, received), mine + received)
        n.stat_out[i + 1] = joined
        if i + 1 < len(stat_copies):
            stat_copies[i + 1].start()

    def half_of(name, half):
        height, width = (size // 2 for size in getattr(n, "r1_" + name).shape[-2:])
        if name == DOWN:
            return (pl.ds(half * height, height), slice(None))
        return (slice(None), pl.ds(half * width, width))

    def put(name, total):
        if name in CHUNKS:
            first, last = CHUNKS[name]
            n.grad_qkv[:, first:last] = total
        elif name in (UP_A, UP_B):
            width = total.shape[1]
            n.grad_up[:, pl.ds(width * (name == UP_B), width)] = total
        else:
            getattr(n, "grad_" + name)[...] = total

    def places(count):
        if count == 0:
            return [()]
        return [(i,) + rest for i in range(2) for rest in places(count - 1)]

    def index_at(left, axis, value, place=None):
        place = iter(place or (slice(None),) * 2)
        return tuple(value if each == axis else next(place) for each in left)

    def left_after(done):
        return tuple(each for each in AXES if each not in done)

    def exchange(src, dst, left, axis):
        view = src.at[index_at(left, axis, 1 - bits[axis])]
        return copy(view, dst, across[axis])

    core_copies, before, pair_copies, after, straight = {}, {}, {}, {}, {}
    for name, (first_axes, then_axes) in ROUTES.items() if inside else ():
        ref = getattr(n, "r1_" + name)
        core_copies[name] = copy(getattr(n, "g_" + name).at[:, :, :, 1 - core], ref, sibling)
        left = AXES
        before[name] = []
        for i, axis in enumerate(first_axes):
            dst = getattr(n, f"r{i + 2}_{name}")
            before[name].append((ref, dst, left, axis, exchange(ref, dst, left, axis)))
            ref, left = dst, left_after(first_axes[: i + 1])
        whole = (slice(None),) * len(left)
        half = getattr(n, "half_" + name)
        pair_copies[name] = copy(ref.at[whole + half_of(name, 1)], half, partner)
        after[name] = []
        ref = half
        for i, axis in enumerate(then_axes):
            dst = getattr(n, "then_" + name)
            after[name].append((ref, dst, left, axis, exchange(ref, dst, left, axis)))
            ref, left = dst, left_after(first_axes + then_axes)
        straight[name] = []
        if left:
            first, second = left
            mine = 2 * bits[first] + bits[second]
            for offset in range(1, 4):
                place = (mine + offset) % 4
                target = me + STRIDES[first] * (place // 2 - bits[first])
                target = target + STRIDES[second] * (place % 2 - bits[second])
                straight[name].append(
                    copy(
                        ref.at[place // 2, place % 2],
                        getattr(n, "far_" + name).at[offset],
                        (me_pair, target),
                    )
                )

    def added(step):
        src, dst, left, axis, each = step
        each.wait()
        for place in places(len(left) - 1):
            mine = src[index_at(left, axis, bits[axis], place)].astype(F32)
            at = place or (slice(None),) * 2
            yield at, mine + dst[at].astype(F32)

    def core_start(name):
        if inside:
            core_copies[name].start()

    def hand_over(name, ref, sums):
        half = getattr(n, "half_" + name)
        for at, total in sums:
            total = total.astype(BF16)
            if name == DOWN:
                height = total.shape[0] // 2
                own, others = total[:height], total[height:]
            else:
                width = total.shape[1] // 2
                own, others = total[:, :width], total[:, width:]
            half[at] = own
            ref[at + half_of(name, 1)] = others
        go_on(name)
        pair_copies[name].start()

    def go_on(name):
        if after[name]:
            after[name][0][-1].start()
        else:
            for each in straight[name]:
                each.start()

    def core_done(name):
        if not inside:
            return
        core_copies[name].wait()
        g, r1 = getattr(n, "g_" + name), getattr(n, "r1_" + name)
        sums = (
            (place, g[place + (core,)].astype(F32) + r1[place].astype(F32)) for place in places(3)
        )
        if not before[name]:
            hand_over(name, r1, sums)
            return
        for at, total in sums:
            r1[at] = total.astype(BF16)
        before[name][0][-1].start()

    def axis_done(name, i=0):
        if not inside:
            return
        step = before[name][i]
        if i + 1 == len(before[name]):
            hand_over(name, step[1], added(step))
            return
        for at, total in added(step):
            step[1][at] = total.astype(BF16)
        before[name][i + 1][-1].start()

    def then_done(name):
        if not inside:
            return
        step = after[name][0]
        for at, total in added(step):
            if straight[name]:
                step[1][at] = total.astype(BF16)
            else:
                put(name, total)
        for each in straight[name]:
            each.start()

    def far_done(name):
        if not inside:
            return
        ref = after[name][0][1] if after[name] else getattr(n, "half_" + name)
        first, second = straight_axes(name)
        total = ref[bits[first], bits[second]].astype(F32)
        for offset in range(1, 4):
            straight[name][offset - 1].wait_recv()
            total += getattr(n, "far_" + name)[offset].astype(F32)
        put(name, total)

    def straight_axes(name):
        first_axes, then_axes = ROUTES[name]
        return left_after(first_axes + then_axes)

    gain_copies = []
    if inside:
        gain_copies.append(copy(n.gain_out.at[0], n.gain_in.at[0], sibling))
        for k in range(15):
            offset, pair = (k + 1) % 8, 0 if k < 7 else 1
            gain_copies.append(
                copy(
                    n.gain_out.at[1],
                    n.gain_in.at[1 + offset],
                    (pair, 2 * ((me // 2 + offset) % 8) + core),
                )
            )

    def gain_step():
        if not inside:
            return
        gain_copies[0].wait()
        n.gain_out[1] = n.gain_out[0] + n.gain_in[0]
        for each in gain_copies[1:]:
            each.start()

    def gain_owner(pair):
        if not inside:
            n.grad_gains[...] = n.gain_out[0]
            return
        total = n.gain_out[1] if pair == 0 else None
        for k in range(7) if pair == 0 else range(7, 15):
            gain_copies[1 + k].wait_recv()
            part = n.gain_in[1 + (k + 1) % 8]
            total = part if total is None else total + part
        n.grad_gains[...] = total

    def turned(ref):
        return jnp.transpose(rows_of(ref, 0, d))

    def product(left, right):
        return dot_nn(left[...], right.reshape(seq_count * LP, right.shape[2]))

    def blocks(value):
        return value.astype(BF16).reshape(2, 2, 2, 2, d // 16, value.shape[1])

    @pl.when(online)
    def _():
        n.turned_one[...] = turned(n.normed_one)
        n.turned_two[...] = turned(n.normed_two)
        n.turned_mixed[...] = turned(n.attended)
        aims_copy.wait_recv()
        differ = n.picked[...] - n.aims_in[...]
        weighted = jnp.where(real, seq_weight * differ, 0.0)
        n.coef[...] = weighted
        stat_first(jnp.sum(0.5 * weighted * jnp.where(real, differ, 0.0)))

        @pl.loop(0, seq_count)
        def _(s):
            backward_head(n, s)

        n.turned_ffn[...] = turned(n.grad_ffn)

        @pl.loop(0, ff // 512)
        def _(j):
            columns = pl.ds(pl.multiple_of(j * 512, 512), 512)
            value = product(n.turned_ffn, n.active[:, :, columns]).astype(BF16)
            for c in range(4):
                n.g_down[j // 2, j % 2, c // 2, c % 2] = value[:, 128 * c : 128 * c + 128]

        core_start(DOWN)
        value = None
        for s in range(seq_count):
            part = dot_nn(n.grad_q[s], n.final_low[s])
            value = part if value is None else value + part
        n.g_head[...] = blocks(jnp.transpose(value))
        core_start(HEAD)
        stat_next(0)

        @pl.loop(0, seq_count // 2)
        def _(t):
            backward_upper(n, 2 * t)

        core_done(DOWN)
        core_done(HEAD)

        def up_product(ref, tiles, first):
            @pl.loop(0, 2 * tiles)
            def _(j):
                columns = pl.ds(
                    pl.multiple_of((j // tiles) * (ff // 2) + first + (j % tiles) * 512, 512), 512
                )
                here = pl.ds(pl.multiple_of(j * 512, 512), 512)
                ref[:, :, :, :, :, here] = blocks(product(n.turned_two, n.slope[:, :, columns]))

        if inside:
            up_product(n.g_up_a, ff // 4 // 512, 0)
            core_start(UP_A)
            up_product(n.g_up_b, ff // 4 // 512, ff // 4)
            core_start(UP_B)
        else:
            up_product(n.g_up, ff // 2 // 512, 0)
        stat_next(1)

        @pl.loop(0, seq_count // 2)
        def _(t):
            backward_middle(n, 2 * t)

            @pl.when(t == 0)
            def _():
                core_done(UP_A)

            @pl.when(t == 1)
            def _():
                core_done(UP_B)

        n.g_out[...] = blocks(product(n.turned_mixed, n.grad_branch[...]))
        core_start(OUT)
        stat_next(2)

        @pl.loop(0, seq_count)
        def _(s):
            attend_back(n, [(s, pair) for pair in range(d // 128)], d)
            backward_states(n, s)
            state_copy(s).start()

            @pl.when(s == 0)
            def _():
                then_done(DOWN)
                axis_done(HEAD)
                core_done(OUT)

            @pl.when(s == 1)
            def _():
                stat_next(3)
                axis_done(UP_A)

            @pl.when(s == 2)
            def _():
                axis_done(UP_B)

            @pl.when(s == 3)
            def _():
                axis_done(OUT)

        n.gain_out[0, 0:1, :] = jnp.sum(n.gain_sums[0], axis=0, keepdims=True)
        n.gain_out[0, 1:2, :] = jnp.sum(n.gain_sums[1], axis=0, keepdims=True)
        n.gain_out[0, 2:8, :] = jnp.zeros((6, d), F32)

        def qkv_product(first, *names):
            width = 256 // len(names)
            for half in range(2):
                at = half * (3 * d // 2) + first
                value = blocks(product(n.turned_one, n.qkv[:, :, at : at + 256]))
                for i, name in enumerate(names):
                    getattr(n, "g_" + name)[..., half * width : (half + 1) * width] = value[
                        ..., i * width : (i + 1) * width
                    ]
            for name in names:
                core_start(name)

        if inside:
            gain_copies[0].start()
            qkv_product(0, QKV_0)
            qkv_product(256, QKV_1)
            core_done(QKV_0)
            qkv_product(512, QKV_2, QKV_3)
            core_done(QKV_1)
            axis_done(UP_A, 1)
            axis_done(UP_B, 1)
            core_done(QKV_2)
            core_done(QKV_3)
            gain_step()
            far_done(HEAD)
            far_done(DOWN)
            axis_done(QKV_0)
            axis_done(QKV_1)
            axis_done(QKV_2)
            axis_done(QKV_3)
            far_done(OUT)
            then_done(UP_A)
            then_done(UP_B)
        else:
            for first in range(0, 3 * d, 256):
                n.g_qkv[..., first : first + 256] = blocks(
                    product(n.turned_one, n.qkv[:, :, first : first + 256])
                )
        for s in range(0, seq_count, 2):
            n.state_out[s * L : (s + 2) * L] = without_pad(n.grad_states, s, d // 2)
            n.q_out[s * L : (s + 2) * L] = without_pad(n.q_rows, s, 128)
        gain_owner(0)
        for name in CHUNKS:
            far_done(name)
        q_copy.wait_send()
        for s in range(seq_count):
            state_copy(s).wait_send()
        for each in tuple(pair_copies.values()) + tuple(gain_copies[1:]):
            each.wait_send()

    @pl.when(jnp.logical_not(online))
    def _():
        stat_first(0.0)
        for i in range(4):
            stat_next(i)
        received = (DOWN, HEAD, UP_A, UP_B, OUT) + tuple(CHUNKS)

        def receive(name):
            if inside:
                pair_copies[name].wait_recv()
                go_on(name)

        receive(DOWN)
        q_copy.wait_recv()
        for s in range(0, seq_count, 2):
            n.q_out[s * L : (s + 2) * L] = without_pad(n.q_half, s, 128)
        then_done(DOWN)
        for name in received[1:]:
            receive(name)
            if name == UP_B:
                far_done(DOWN)
        for s in range(seq_count):
            state_copy(s).wait_recv()
            if s % 2:
                n.state_out[(s - 1) * L : (s + 1) * L] = without_pad(n.state_half, s - 1, d // 2)
        far_done(HEAD)
        far_done(OUT)
        then_done(UP_A)
        then_done(UP_B)
        gain_owner(1)
        for name in CHUNKS:
            far_done(name)
        aims_copy.wait_send()

    for sent in straight.values():
        for each in sent:
            each.wait_send()
    if inside:
        stat_next(4)
        n.stats[...] = n.stat_out[5]
    else:
        n.stats[...] = n.stat_out[0]
    assert used[0] <= SEMAPHORES


OUTPUTS = (
    "q_out",
    "state_out",
    GRAD_GAINS,
    "grad_qkv",
    "grad_out",
    "grad_up",
    GRAD_DOWN,
    "grad_head",
    NEW_GAINS,
    "new_qkv",
    "new_out",
    "new_up",
    "new_down",
    "new_head",
    STATS,
)


def finish_kernel(moved, worked, token_total, data_count, *refs):
    source = dict(zip(moved + worked, refs))
    result = dict(zip(OUTPUTS, refs[len(source) :]))
    sems = refs[-1]
    copies = [
        pltpu.make_async_copy(source[name], result[name], sems.at[i])
        for i, name in enumerate(moved)
    ]
    for copy in copies:
        copy.start()
    me_pair = lax.axis_index(PAIR)
    me = lax.axis_index(DP)
    for name in (GRAD_GAINS, NEW_GAINS):
        height = source[name].shape[1] // data_count
        here = source[name][:, pl.ds(pl.multiple_of(me * height // 128 * 128, 128), 128)]
        value = here[:, :height]
        for at in range(height, 128, height):
            value = jnp.where(me * height % 128 == at, here[:, at : at + height], value)
        result[name][...] = jnp.where(me_pair == 0, value[0:1], value[1:2])
    if GRAD_DOWN in worked:
        result[GRAD_DOWN][...] = jnp.transpose(source[GRAD_DOWN][...])
    stats = source[STATS]
    result[STATS][0] = stats[0, 0] / token_total
    result[STATS][1] = stats[0, 1] / token_total
    result[STATS][2] = stats[1, 0]
    result[STATS][3] = stats[0, 2] / token_total
    result[STATS][4] = stats[1, 1]
    for copy in copies:
        copy.wait()


def add_outside(out, params, pair_index, data_index, data_count):
    online = pair_index == 0
    other = 1 - pair_index

    def half(matrix, which):
        width = matrix.shape[1] // 2
        return lax.dynamic_slice_in_dim(matrix, which * width, width, 1)

    def piece(matrix, which):
        height = matrix.shape[0] // data_count
        return half(lax.dynamic_slice_in_dim(matrix, data_index * height, height, 0), which)

    def swapped(value):
        return lax.ppermute(value, PAIR, [(0, 1), (1, 0)])

    for name in TENSORS:
        grad = out["g_" + name].astype(F32)
        grad = grad.reshape((16,) + grad.shape[4:])
        if name == DOWN:
            grad = jnp.swapaxes(grad, 1, 2)
        grad = lax.psum_scatter(
            grad.reshape(-1, grad.shape[2]), DP, scatter_dimension=0, tiled=True
        )
        received = swapped(half(grad, other))
        out["grad_" + name] = jnp.where(online, half(grad, pair_index), received)
    gains = lax.psum(out[GRAD_GAINS], DP)
    out[GRAD_GAINS] = jnp.where(online, gains, swapped(gains))
    for name, weight in zip((GAINS, QKV, OUT, UP, DOWN, HEAD), params):
        if name == GAINS:
            weight = jnp.pad(weight.T, ((0, 6), (0, 0)))
            mine, received = weight.astype(F32), swapped(weight).astype(F32)
        else:
            mine = piece(weight, pair_index).astype(F32)
            received = swapped(piece(weight, other)).astype(F32)
        first, second = jnp.where(online, mine, received), jnp.where(online, received, mine)
        out["new_" + name] = second + SOFT_RATE * (first - second)
    sums = lax.psum(out[STATS][0:1], (PAIR, DP))
    bests = lax.pmax(out[STATS][1:2], (PAIR, DP))
    out[STATS] = jnp.concatenate([sums, bests])


def local(
    states, norm_gains, w_qkv, w_out, w_up, w_down, w_head, task_ids, chosen, reward, finished
):
    pair_index = lax.axis_index(PAIR)
    data_index = lax.axis_index(DP)
    data_count = lax.axis_size(DP)
    row_count, d = states.shape[1:]
    ff = w_up.shape[2]
    bin_count = w_head.shape[2]
    seq_count = row_count // L

    inside = data_count == 16
    rows = (seq_count, LP, d)
    inputs = dict(
        states=states[0],
        norm_gains=norm_gains[0].T,
        hbm_qkv=w_qkv[0],
        hbm_out=w_out[0],
        hbm_up=w_up[0],
        hbm_down=w_down[0],
        hbm_head=w_head[0],
        task_ids=task_ids,
        chosen=chosen,
        reward=reward,
        finished=finished,
    )
    if not inside:
        table = (task_ids[:, None] == jnp.arange(128, dtype=jnp.int32)[None, :]).astype(F32)
        inputs["counts"] = jnp.broadcast_to(
            lax.psum(jnp.sum(table, axis=0, keepdims=True), DP), (8, 128)
        )
    piece = {
        QKV: (d // 16, 3 * d),
        OUT: (d // 16, d),
        UP: (d // 16, ff),
        HEAD: (d // 16, bin_count),
        DOWN: (d, ff // 16),
    }
    halves = {
        name: (shape[0] // 2, shape[1]) if name == DOWN else (shape[0], shape[1] // 2)
        for name, shape in piece.items()
    }
    new_shapes = dict(halves, down=(ff // 16, d // 2))
    outputs = dict(
        q_out=((row_count, bin_count // 2), BF16),
        state_out=((row_count, d // 2), BF16),
        grad_gains=((8, d), F32),
        new_gains=((8, d), F32),
        stats=((8, 128), F32),
    )
    for name in TENSORS:
        if inside:
            outputs["grad_" + name] = (halves[name], F32)
            outputs["new_" + name] = (new_shapes[name], F32)
        else:
            outputs["g_" + name] = ((2, 2, 2, 2) + piece[name], BF16)
    scratch = dict(
        w_qkv=((d, 3 * d), BF16),
        w_out=((d, d), BF16),
        w_up=((d, ff), BF16),
        w_down=((ff, d), BF16),
        w_head=((d, bin_count), BF16),
        x=(rows, BF16),
        gains=((8, d), F32),
        flat=((8, -(-(row_count + LP - L) // 128) * 128), F32),
        aux=((seq_count, 8, LP), F32),
        table=((8, 128), F32),
        normed_one=(rows, BF16),
        qkv=((seq_count, LP, 3 * d), BF16),
        powers_0=((seq_count, d // 128) + (2 * BLOCKS[0][1], BLOCKS[0][2]), BF16),
        powers_1=((seq_count, d // 128) + (2 * BLOCKS[1][1], BLOCKS[1][2]), BF16),
        powers_2=((seq_count, d // 128) + (2 * BLOCKS[2][1], BLOCKS[2][2]), BF16),
        inverse_totals=(rows, F32),
        attended=(rows, BF16),
        middle=(rows, F32),
        normed_two=(rows, BF16),
        active=((seq_count, LP, ff), BF16),
        slope=((seq_count, LP, ff), BF16),
        final_low=(rows, BF16),
        q_rows=((seq_count, LP, bin_count), BF16),
        q_half=((seq_count, LP, bin_count // 2), BF16),
        picked=((8, LP), F32),
        tops=((8, LP), F32),
        coef=((8, LP), F32),
        aims_out=((8, LP), F32),
        aims_in=((8, LP), F32),
        grad_q=((seq_count, bin_count, LP), BF16),
        grad_ffn=(rows, BF16),
        turned_one=((d, seq_count * LP), BF16),
        turned_two=((d, seq_count * LP), BF16),
        turned_mixed=((d, seq_count * LP), BF16),
        turned_ffn=((d, seq_count * LP), BF16),
        state_half=((seq_count, LP, d // 2), BF16),
        gain_sums=((2, 8, d), F32),
        gain_out=((2, 8, d), F32),
        gain_in=((9, 8, d), F32),
        count_out=((2, 8, 128), F32),
        count_in=((8, 8, 128), F32),
        stat_out=((6, 8, 128), F32),
        stat_in=((5, 8, 128), F32),
        their_gains=((8, d), F32),
    )
    if inside:
        for name in TENSORS:
            scratch["their_" + name] = (new_shapes[name], BF16)
        for name, (first_axes, then_axes) in ROUTES.items():
            if name in CHUNKS:
                shape = (d // 16, 2 * (CHUNKS[name][1] - CHUNKS[name][0]))
            else:
                shape = (d // 16, ff // 2) if name in (UP_A, UP_B) else piece[name]
            half = halves[DOWN] if name == DOWN else (shape[0], shape[1] // 2)
            scratch["g_" + name] = (2, 2, 2, 2) + shape, BF16
            for i in range(len(first_axes) + 1):
                scratch[f"r{i + 1}_{name}"] = (2,) * (3 - i) + shape, BF16
            left = 3 - len(first_axes)
            scratch["half_" + name] = (2,) * left + half, BF16
            if then_axes:
                scratch["then_" + name] = (2,) * (left - 1) + half, BF16
            if left - len(then_axes) == 2:
                scratch["far_" + name] = (4,) + half, BF16
    names = list(inputs) + list(outputs) + list(scratch) + ["send_sem", "recv_sem", "load_sem"]
    in_vmem = pl.BlockSpec(memory_space=pltpu.VMEM)
    in_smem = pl.BlockSpec(memory_space=pltpu.SMEM)
    anywhere = pl.BlockSpec(memory_space=pl.ANY)
    raw = pl.pallas_call(
        functools.partial(layer_kernel, names, data_count, inside),
        out_shape=[jax.ShapeDtypeStruct(shape, dtype) for shape, dtype in outputs.values()],
        in_specs=[
            in_smem if name == "task_ids" else anywhere if name[:3] == "hbm" else in_vmem
            for name in inputs
        ],
        out_specs=[in_vmem] * len(outputs),
        scratch_shapes=[pltpu.VMEM(shape, dtype) for shape, dtype in scratch.values()]
        + [pltpu.SemaphoreType.DMA((SEMAPHORES,)), pltpu.SemaphoreType.DMA((SEMAPHORES,))]
        + [pltpu.SemaphoreType.DMA((5,))],
        compiler_params=pltpu.CompilerParams(
            collective_id=0, has_side_effects=True, vmem_limit_bytes=64 * 1024 * 1024 - 65536
        ),
        name="layer",
    )(*inputs.values())
    out = dict(zip(outputs, raw))
    if not inside:
        params = (norm_gains[0], w_qkv[0], w_out[0], w_up[0], w_down[0], w_head[0])
        add_outside(out, params, pair_index, data_index, data_count)
    moved = {name: out[name] for name in OUTPUTS if name not in (GRAD_GAINS, NEW_GAINS, STATS)}
    worked = {name: out[name] for name in (GRAD_GAINS, NEW_GAINS, STATS)}
    results = {name: jax.ShapeDtypeStruct(value.shape, value.dtype) for name, value in moved.items()}
    if inside:
        worked[GRAD_DOWN] = moved.pop(GRAD_DOWN)
        results[GRAD_DOWN] = jax.ShapeDtypeStruct((ff // data_count, d // 2), F32)
    results[GRAD_GAINS] = results[NEW_GAINS] = jax.ShapeDtypeStruct((1, d // data_count), F32)
    results[STATS] = jax.ShapeDtypeStruct((5,), F32)
    spec_of = {name: anywhere if name in moved else in_vmem for name in OUTPUTS}
    spec_of[STATS] = in_smem
    final = pl.pallas_call(
        functools.partial(
            finish_kernel, list(moved), list(worked), row_count * data_count, data_count
        ),
        out_shape=[results[name] for name in OUTPUTS],
        in_specs=[in_vmem] * (len(moved) + len(worked)),
        out_specs=[spec_of[name] for name in OUTPUTS],
        scratch_shapes=[
            pltpu.SemaphoreType.DMA((len(moved),)),
        ],
        name="finish",
    )(*moved.values(), *worked.values())
    final = dict(zip(OUTPUTS, final))
    for name in (GRAD_GAINS, NEW_GAINS):
        final[name] = final[name].T
    return tuple(final.values())


def solution(mesh):
    placed = (
        P(PAIR, DP, None),
        P(PAIR, None, None),
        P(PAIR, None, None),
        P(PAIR, None, None),
        P(PAIR, None, None),
        P(PAIR, None, None),
        P(PAIR, None, None),
        P(DP),
        P(DP),
        P(DP),
        P(DP),
    )
    return jax.shard_map(
        local,
        mesh=mesh,
        in_specs=placed,
        out_specs=(P(DP, PAIR),) * 14 + (P(),),
        check_vma=False,
    )
```

```python
import functools

import jax
import jax.numpy as jnp
from jax import lax
from jax.experimental import pallas as pl
from jax.experimental.pallas import tpu as pltpu
from jax.sharding import PartitionSpec as P

F32 = jnp.float32
BF16 = jnp.bfloat16
MESH = pl.DeviceIdType.MESH

DOWN = "down"
PAIR = "pair"
DP = "dp"
STATS = "stats"
ROW = "row"
HEAD = "head"
UP_B = "up_b"
OUT = "out"
UP_A = "up_a"
LOW = "low"
GRAD_GAINS = "grad_gains"
HIGH = "high"
GRAD_DOWN = "grad_down"
NEW_GAINS = "new_gains"
QKV_0 = "qkv_0"
QKV_1 = "qkv_1"
QKV_2 = "qkv_2"
QKV_3 = "qkv_3"
UP = "up"
QKV = "qkv"
GAINS = "gains"

HEAD_DIM = 64
L = 296
LP = 304
TASKS = 32
EPSILON = 1e-06
DISCOUNT = 0.98
SOFT_RATE = 0.2
SCORE_SCALE = 0.125
NEG_LARGE = -1000000000.0
LOWEST = -1e30

BLOCKS = ((0, 128, 128), (128, 128, 256), (256, 48, 304))


def dot_nn(a, b):
    return lax.dot_general(a, b, (((1,), (0,)), ((), ())), preferred_element_type=F32)


def dot_nt(a, b):
    return lax.dot_general(a, b, (((1,), (1,)), ((), ())), preferred_element_type=F32)


def dot_tn(a, b):
    return lax.dot_general(a, b, (((0,), (0,)), ((), ())), preferred_element_type=F32)


def dot_tt(a, b):
    return lax.dot_general(a, b, (((0,), (1,)), ((), ())), preferred_element_type=F32)


def inverse_rms(values):
    return lax.rsqrt(jnp.mean(values * values, axis=-1, keepdims=True) + EPSILON)


def gelu_and_slope(u):
    c = 0.7978845608028654
    square = u * u
    t = jnp.tanh(u * (c + (c * 0.044715) * square))
    half = 0.5 * t + 0.5
    slope = half + (u * (0.5 - 0.5 * t * t)) * (c + (3 * c * 0.044715) * square)
    return u * half, slope


def lane_halves(a):
    lane = lax.broadcasted_iota(jnp.int32, (1, 2 * HEAD_DIM), 1)
    zero = jnp.zeros((), a.dtype)
    return jnp.where(lane < HEAD_DIM, a, zero), jnp.where(lane >= HEAD_DIM, a, zero)


def rows_of(ref, first, width):
    value = ref[:, :, first : first + width]
    return value.reshape(value.shape[0] * value.shape[1], width)


def without_pad(ref, s, width):
    rows = [ref[s + i, :, :width].astype(F32)[:L] for i in range(2)]
    return jnp.concatenate(rows, axis=0).astype(BF16)


class Names:
    pass


def in_steps(count, first, second, third):
    for item in range(count + 2):
        if item < count:
            first(item)
        if 0 <= item - 1 < count:
            second(item - 1)
        if item >= 2:
            third(item - 2)


def attend(n, items, d):
    corner = lax.broadcasted_iota(jnp.int32, (128, 128), 0) >= lax.broadcasted_iota(
        jnp.int32, (128, 128), 1
    )
    ones = jnp.ones((LP, 128), BF16)
    marks = lane_halves(ones)
    raw, raised = {}, {}

    def score(item):
        s, pair = items[item]
        at = 128 * pair
        queries = lane_halves(n.qkv[s, :, at : at + 128] * jnp.array(SCORE_SCALE, BF16))
        keys = n.qkv[s, :, d + at : d + at + 128]
        for block, (first, rows, seen) in enumerate(BLOCKS):
            both = jnp.concatenate([q[first : first + rows] for q in queries], axis=0)
            raw[item, block] = dot_nt(both, keys[:seen])

    def raise_scores(item):
        s, pair = items[item]
        for block, (first, rows, seen) in enumerate(BLOCKS):
            scores = raw.pop((item, block))
            visible = jnp.concatenate([corner[:rows, :rows]] * 2, axis=0)
            diagonal = jnp.where(visible, scores[:, first:], NEG_LARGE)
            scores = jnp.concatenate([scores[:, :first], diagonal], axis=1) if first else diagonal
            powers = jnp.exp(scores - jnp.max(scores, axis=-1, keepdims=True)).astype(BF16)
            raised[item, block] = powers
            n.powers[block][s, pair] = powers

    def mix(item):
        s, pair = items[item]
        at = 128 * pair
        values = lane_halves(n.qkv[s, :, 2 * d + at : 2 * d + at + 128])
        wide = [jnp.concatenate(both, axis=1) for both in zip(values, marks)]
        for block, (first, rows, seen) in enumerate(BLOCKS):
            powers = raised.pop((item, block))
            if seen % 128 == 0:
                mixed = dot_nn(
                    jnp.concatenate([powers[:rows], powers[rows:]], axis=1),
                    jnp.concatenate([w[:seen] for w in wide], axis=0),
                )
            else:
                mixed = dot_nn(powers[:rows], wide[0][:seen]) + dot_nn(powers[rows:], wide[1][:seen])
            inverse = 1.0 / mixed[:, 128:]
            n.inverse_totals[s, first : first + rows, at : at + 128] = inverse
            n.attended[s, first : first + rows, at : at + 128] = (mixed[:, :128] * inverse).astype(
                BF16
            )

    in_steps(len(items), score, raise_scores, mix)


def lay_out_inputs(n, seq_count):
    d = n.x.shape[2]
    pad = jnp.zeros((LP - L, d), F32)
    for s in range(0, seq_count, 2):
        both = n.states[s * L : (s + 2) * L].astype(F32)
        for i in range(2):
            n.x[s + i] = jnp.concatenate([both[i * L : (i + 1) * L], pad], axis=0).astype(BF16)
    n.flat[...] = jnp.zeros_like(n.flat)
    for i, ref in enumerate((n.chosen, n.reward, n.finished)):
        n.flat[i : i + 1, : seq_count * L] = ref[...].reshape(1, seq_count * L).astype(F32)
    for s in range(seq_count):
        n.aux[s] = n.flat[:, s * L : s * L + LP]
    n.gains[...] = jnp.zeros_like(n.gains)
    n.gains[0:2, :] = n.norm_gains[...].astype(F32)
    seq = lax.broadcasted_iota(jnp.int32, (8, 128), 0)
    task = lax.broadcasted_iota(jnp.int32, (8, 128), 1)
    table = jnp.zeros((8, 128), F32)
    for s in range(seq_count):
        table = jnp.where(jnp.logical_and(seq == s, task == n.task_ids[s]), 1.0, table)
    n.table[...] = table


def forward_sequences(n, s, online, loads):
    both = pl.ds(s, 2)
    d = n.x.shape[2]
    ff = n.w_up.shape[1]

    def rows(ref):
        return ref[both].reshape(2 * LP, ref.shape[2])

    def split(value):
        return value.astype(BF16).reshape(2, LP, value.shape[1])

    x = rows(n.x).astype(F32)
    normed = (x * inverse_rms(x) * n.gains[0:1, :]).astype(BF16)
    n.normed_one[both] = split(normed)
    for first in range(0, 3 * d, 512):
        n.qkv[both, :, first : first + 512] = split(
            dot_nn(normed, n.w_qkv[:, first : first + 512])
        )
    attend(n, [(s + i, pair) for i in range(2) for pair in range(d // 128)], d)

    @pl.when(s == 0)
    def _():
        for load in loads:
            load.wait()

    middle = rows(n.x).astype(F32) + dot_nn(rows(n.attended), n.w_out[...])
    n.middle[both] = middle.reshape(2, LP, d)
    normed = (middle * inverse_rms(middle) * n.gains[1:2, :]).astype(BF16)
    n.normed_two[both] = split(normed)

    @pl.when(online)
    def _():
        for first in range(0, ff, 256):
            active, slope = gelu_and_slope(dot_nn(normed, n.w_up[:, first : first + 256]))
            n.active[both, :, first : first + 256] = split(active)
            n.slope[both, :, first : first + 256] = split(slope)

    @pl.when(jnp.logical_not(online))
    def _():
        for first in range(0, ff, 256):
            active, _ = gelu_and_slope(dot_nn(normed, n.w_up[:, first : first + 256]))
            n.active[both, :, first : first + 256] = split(active)

    final_low = (rows(n.middle) + dot_nn(rows(n.active), n.w_down[...])).astype(BF16)
    n.final_low[both] = split(final_low)
    n.q_rows[both] = split(dot_nn(final_low, n.w_head[...]))
    for i in range(2):
        q_columns = dot_tt(n.w_head[...], n.final_low[s + i])
        bins = lax.broadcasted_iota(jnp.int32, q_columns.shape, 0)
        chosen = n.aux[s + i, 0:1, :].astype(jnp.int32)
        n.picked[pl.ds(s + i, 1), :] = jnp.sum(
            jnp.where(bins == chosen, q_columns, 0.0), axis=0, keepdims=True
        )
        n.tops[pl.ds(s + i, 1), :] = jnp.max(q_columns, axis=0, keepdims=True)


def backward_head(n, s):
    bins = lax.broadcasted_iota(jnp.int32, (n.w_head.shape[1], LP), 0)
    chosen = n.aux[s, 0:1, :].astype(jnp.int32)
    grad_q = jnp.where(bins == chosen, n.coef[pl.ds(s, 1), :], 0.0).astype(BF16)
    n.grad_q[s] = grad_q
    n.grad_ffn[s] = dot_tt(grad_q, n.w_head[...]).astype(BF16)


def backward_upper(n, s):
    both = pl.ds(s, 2)
    ff = n.w_up.shape[1]
    grad_ffn = n.grad_ffn[both].reshape(2 * LP, -1)
    for first in range(0, ff, 512):
        grad_active = dot_nt(grad_ffn, n.w_down[first : first + 512, :])
        slope = n.slope[both, :, first : first + 512].astype(F32)
        n.slope[both, :, first : first + 512] = (
            grad_active.reshape(2, LP, 512) * slope
        ).astype(BF16)


def backward_middle(n, s):
    both = pl.ds(s, 2)
    d = n.x.shape[2]
    grad_two = dot_nt(n.slope[both].reshape(2 * LP, -1), n.w_up[...])
    middle = n.middle[both].reshape(2 * LP, d)
    inverse = inverse_rms(middle)
    normal = middle * inverse
    n.gain_sums[1] += jnp.sum((grad_two * normal).reshape(2 * LP // 8, 8, d), axis=0)
    inner = grad_two * n.gains[1:2, :]
    grad_final = jnp.concatenate(
        [dot_tt(n.grad_q[s + i], n.w_head[...]) for i in range(2)], axis=0
    )
    grad_middle = grad_final + inverse * (
        inner - normal * jnp.mean(inner * normal, axis=-1, keepdims=True)
    )
    n.middle[both] = grad_middle.reshape(2, LP, d)
    grad_branch = grad_middle.astype(BF16)
    n.grad_branch[both] = grad_branch.reshape(2, LP, d)
    n.grad_mixed[both] = dot_nt(grad_branch, n.w_out[...]).astype(BF16).reshape(2, LP, d)


def attend_back(n, items, d):
    side = lax.broadcasted_iota(jnp.int32, (256, 256), 0) % 128 < HEAD_DIM
    head = lax.broadcasted_iota(jnp.int32, (256, 256), 1) < 128
    head_sums = jnp.where(side == head, jnp.ones((), BF16), jnp.zeros((), BF16))
    kept = {}

    def spread(item):
        s, pair = items[item]
        at = 128 * pair
        grads = (
            n.grad_mixed[s, :, at : at + 128].astype(F32) * n.inverse_totals[s, :, at : at + 128]
        ).astype(BF16)
        product = n.attended[s, :, at : at + 128].astype(F32) * grads.astype(F32)
        upper = product.astype(BF16)
        lower = (product - upper.astype(F32)).astype(BF16)
        centres = dot_nn(jnp.concatenate([upper, lower], axis=1), head_sums)
        values = n.qkv[s, :, 2 * d + at : 2 * d + at + 128]
        grads = lane_halves(grads)
        found = []
        for first, rows, seen in BLOCKS:
            both = jnp.concatenate([g[first : first + rows] for g in grads], axis=0)
            found.append((both, dot_nt(both, values[:seen])))
        kept[item] = centres, found

    def centre(item):
        s, pair = items[item]
        centres, found = kept[item]
        done = []
        for block, (first, rows, seen) in enumerate(BLOCKS):
            both, grad_powers = found[block]
            here = centres[first : first + rows]
            here = jnp.concatenate([here[:, :128], here[:, 128:]], axis=0)
            here = jnp.concatenate([here] * ((seen + 127) // 128), axis=1)[:, :seen]
            powers = n.powers[block][s, pair]
            done.append((both, powers, (powers.astype(F32) * (grad_powers - here)).astype(BF16)))
        kept[item] = done

    def collect(item):
        s, pair = items[item]
        at = 128 * pair
        queries = lane_halves(n.qkv[s, :, at : at + 128])
        keys = lane_halves(n.qkv[s, :, d + at : d + at + 128])
        grad_keys = [None] * 3
        grad_values = [None] * 3
        done = kept.pop(item)
        for block, (first, rows, seen) in enumerate(BLOCKS):
            both, powers, grad_scores = done[block]
            both_queries = jnp.concatenate([q[first : first + rows] for q in queries], axis=0)
            if seen % 128 == 0:
                grad_queries = dot_nn(
                    jnp.concatenate([grad_scores[:rows], grad_scores[rows:]], axis=1),
                    jnp.concatenate([k[:seen] for k in keys], axis=0),
                )
            else:
                grad_queries = dot_nn(grad_scores[:rows], keys[0][:seen]) + dot_nn(
                    grad_scores[rows:], keys[1][:seen]
                )
            of_values = dot_tn(powers, both)
            of_keys = dot_tn(grad_scores, both_queries)
            for i, start in enumerate((0, 128, 256)):
                if start < seen:
                    end = min(start + 128, seen)
                    piece = of_values[start:end]
                    grad_values[i] = piece if grad_values[i] is None else grad_values[i] + piece
                    piece = of_keys[start:end]
                    grad_keys[i] = piece if grad_keys[i] is None else grad_keys[i] + piece
            n.qkv[s, first : first + rows, at : at + 128] = (grad_queries * SCORE_SCALE).astype(
                BF16
            )
        for i, (first, rows, _) in enumerate(BLOCKS):
            n.qkv[s, first : first + rows, d + at : d + at + 128] = (
                grad_keys[i] * SCORE_SCALE
            ).astype(BF16)
            n.qkv[s, first : first + rows, 2 * d + at : 2 * d + at + 128] = grad_values[i].astype(
                BF16
            )

    in_steps(len(items), spread, centre, collect)


def backward_states(n, s):
    grad_one = dot_nt(n.qkv[s], n.w_qkv[...])
    x = n.x[s].astype(F32)
    inverse = inverse_rms(x)
    normal = x * inverse
    n.gain_sums[0] += jnp.sum((grad_one * normal).reshape(LP // 8, 8, -1), axis=0)
    inner = grad_one * n.gains[0:1, :]
    n.grad_states[s] = (
        n.middle[s]
        + inverse * (inner - normal * jnp.mean(inner * normal, axis=-1, keepdims=True))
    ).astype(BF16)


ROUTES = {
    DOWN: ((), (ROW,)),
    HEAD: ((ROW,), ()),
    UP_A: ((ROW, LOW), (HIGH,)),
    UP_B: ((LOW, ROW), (HIGH,)),
    OUT: ((ROW,), ()),
    QKV_0: ((ROW,), ()),
    QKV_1: ((LOW,), ()),
    QKV_2: ((ROW,), ()),
    QKV_3: ((LOW,), ()),
}
CHUNKS = {QKV_0: (0, 256), QKV_1: (256, 512), QKV_2: (512, 640), QKV_3: (640, 768)}
STRIDES = {HIGH: 8, LOW: 4, ROW: 2}
TENSORS = (DOWN, HEAD, UP, OUT, QKV)
AXES = (HIGH, LOW, ROW)
SEMAPHORES = 160


def layer_kernel(names, data_count, inside, *refs):
    n = Names()
    for name, ref in zip(names, refs):
        setattr(n, name, ref)
    n.powers = (n.powers_0, n.powers_1, n.powers_2)
    n.grad_states, n.grad_branch, n.grad_mixed = n.normed_one, n.normed_two, n.final_low
    d = n.x.shape[2]
    ff = n.w_up.shape[1]
    seq_count = n.x.shape[0]

    me_pair = lax.axis_index(PAIR)
    me = lax.axis_index(DP)
    other = 1 - me_pair
    online = me_pair == 0
    core = me % 2
    row = (me // 2) % 2
    low = (me // 4) % 2
    high = me // 8
    quarter = me // 4
    bits = {ROW: row, LOW: low, HIGH: high}
    sibling = (me_pair, me + 1 - 2 * core)
    partner = (other, me)
    across = {
        "core": sibling,
        ROW: (me_pair, me + 2 - 4 * row),
        LOW: (me_pair, me + 4 - 8 * low),
        HIGH: (me_pair, me + 8 - 16 * high),
        PAIR: partner,
    }

    def at_quarter(which, pair):
        return (pair, me + 4 * (which - quarter))

    used = [0]

    def copy(src, dst, device):
        sem = used[0]
        used[0] += 1
        return pltpu.make_async_remote_copy(
            src_ref=src,
            dst_ref=dst,
            send_sem=n.send_sem.at[sem],
            recv_sem=n.recv_sem.at[sem],
            device_id=device,
            device_id_type=MESH,
        )

    barrier = pltpu.get_barrier_semaphore()
    friends = [partner]
    if inside:
        friends.append(sibling)
        for offset in range(1, 8):
            place = 2 * ((me // 2 + offset) % 8) + core
            friends += [(me_pair, place), (other, place)]
    loads = [
        pltpu.make_async_copy(src, dst, n.load_sem.at[i])
        for i, (src, dst) in enumerate(
            (
                (n.hbm_qkv, n.w_qkv),
                (n.hbm_out, n.w_out),
                (n.hbm_up, n.w_up),
                (n.hbm_down, n.w_down),
                (n.hbm_head, n.w_head),
            )
        )
    ]
    for load in loads:
        load.start()
    for friend in friends:
        pl.semaphore_signal(barrier, inc=1, device_id=friend, device_id_type=MESH)

    weights = {QKV: n.w_qkv, OUT: n.w_out, UP: n.w_up, DOWN: n.w_down, HEAD: n.w_head}

    def piece_of(ref, half):
        height = ref.shape[0] // data_count
        width = ref.shape[1] // 2
        return (
            pl.ds(pl.multiple_of(me * height, height), height),
            pl.ds(pl.multiple_of(half * width, width), width),
        )

    weight_copies = {}
    if inside:
        for name, ref in weights.items():
            weight_copies[name] = copy(
                ref.at[piece_of(ref, other)], getattr(n, "their_" + name), partner
            )
        weight_copies[GAINS] = copy(n.gains, n.their_gains, partner)

    count_copies = []
    if inside:
        count_copies.append(copy(n.count_out.at[0], n.count_in.at[0], sibling))
        for offset in range(1, 8):
            place = (me // 2 + offset) % 8
            count_copies.append(
                copy(n.count_out.at[1], n.count_in.at[offset], (me_pair, 2 * place + core))
            )

    n.gain_sums[...] = jnp.zeros_like(n.gain_sums)
    lay_out_inputs(n, seq_count)
    loads[0].wait()

    @pl.loop(0, seq_count // 2)
    def _(t):
        forward_sequences(n, 2 * t, online, loads[1:])

        @pl.when(t == 0)
        def _():
            pl.semaphore_wait(barrier, len(friends))
            if not inside:
                return
            n.count_out[0] = jnp.broadcast_to(
                jnp.sum(n.table[...], axis=0, keepdims=True), (8, 128)
            )
            count_copies[0].start()
            for each in weight_copies.values():
                each.start()

        @pl.when(t == 1)
        def _():
            if not inside:
                return
            count_copies[0].wait()
            n.count_out[1] = n.count_out[0] + n.count_in[0]
            for each in count_copies[1:]:
                each.start()

    lane = lax.broadcasted_iota(jnp.int32, (8, LP), 1)
    seq = lax.broadcasted_iota(jnp.int32, (8, LP), 0)
    real = jnp.logical_and(lane < L, seq < seq_count)
    tops = n.tops[...]
    aims_copy = copy(n.aims_out, n.aims_in, partner)
    q_copy = copy(n.q_rows.at[:, :, pl.ds(128, 128)], n.q_half, partner)
    state_sem = used[0]
    used[0] += seq_count

    def state_copy(s):
        return pltpu.make_async_remote_copy(
            src_ref=n.grad_states.at[s, :, pl.ds(d // 2, d // 2)],
            dst_ref=n.state_half.at[s],
            send_sem=n.send_sem.at[state_sem + s],
            recv_sem=n.recv_sem.at[state_sem + s],
            device_id=partner,
            device_id_type=MESH,
        )

    @pl.when(jnp.logical_not(online))
    def _():
        reward = jnp.concatenate([n.aux[s, 1:2, :] for s in range(seq_count)] * 2, axis=0)
        finished = jnp.concatenate([n.aux[s, 2:3, :] for s in range(seq_count)] * 2, axis=0)
        n.aims_out[...] = reward + DISCOUNT * (1.0 - finished) * tops
        aims_copy.start()

    @pl.when(online)
    def _():
        q_copy.start()

    if inside:
        for name, each in weight_copies.items():
            each.wait()
            if name == GAINS:
                mine, received = n.gains[...], n.their_gains[...]
            else:
                mine = weights[name][piece_of(weights[name], me_pair)].astype(F32)
                received = getattr(n, "their_" + name)[...].astype(F32)
            first = jnp.where(online, mine, received)
            second = jnp.where(online, received, mine)
            getattr(n, "new_" + name)[...] = second + SOFT_RATE * (first - second)
        counts = n.count_out[1]
        for i in range(1, 8):
            count_copies[i].wait()
            counts += n.count_in[i]
    else:
        counts = n.counts[...]
    seq_weight = (seq_count * data_count) / (
        TASKS * jnp.sum(n.table[...] * counts, axis=1, keepdims=True)
    )

    stat_row_id = lax.broadcasted_iota(jnp.int32, (8, 128), 0)
    stat_lane = lax.broadcasted_iota(jnp.int32, (8, 128), 1)
    stat_axes = ("core", ROW, LOW, HIGH, PAIR)
    stat_copies = [] if not inside else [
        copy(n.stat_out.at[i], n.stat_in.at[i], across[axis]) for i, axis in enumerate(stat_axes)
    ]

    def stat_first(loss):
        total = jnp.sum(jnp.where(real, tops, 0.0))
        best = jnp.max(jnp.where(real, tops, LOWEST))
        sums = jnp.where(stat_lane == 0, loss, jnp.where(stat_lane == 1 + me_pair, total, 0.0))
        bests = jnp.where(stat_lane == me_pair, best, LOWEST)
        n.stat_out[0] = jnp.where(stat_row_id == 0, sums, jnp.where(stat_row_id == 1, bests, 0.0))
        if inside:
            stat_copies[0].start()

    def stat_next(i):
        if not inside:
            return
        stat_copies[i].wait()
        mine, received = n.stat_out[i], n.stat_in[i]
        joined = jnp.where(stat_row_id == 1, jnp.maximum(mine, received), mine + received)
        n.stat_out[i + 1] = joined
        if i + 1 < len(stat_copies):
            stat_copies[i + 1].start()

    def half_of(name, half):
        height, width = (size // 2 for size in getattr(n, "r1_" + name).shape[-2:])
        if name == DOWN:
            return (pl.ds(half * height, height), slice(None))
        return (slice(None), pl.ds(half * width, width))

    def put(name, total):
        if name in CHUNKS:
            first, last = CHUNKS[name]
            n.grad_qkv[:, first:last] = total
        elif name in (UP_A, UP_B):
            width = total.shape[1]
            n.grad_up[:, pl.ds(width * (name == UP_B), width)] = total
        else:
            getattr(n, "grad_" + name)[...] = total

    def places(count):
        if count == 0:
            return [()]
        return [(i,) + rest for i in range(2) for rest in places(count - 1)]

    def index_at(left, axis, value, place=None):
        place = iter(place or (slice(None),) * 2)
        return tuple(value if each == axis else next(place) for each in left)

    def left_after(done):
        return tuple(each for each in AXES if each not in done)

    def exchange(src, dst, left, axis):
        view = src.at[index_at(left, axis, 1 - bits[axis])]
        return copy(view, dst, across[axis])

    core_copies, before, pair_copies, after, straight = {}, {}, {}, {}, {}
    for name, (first_axes, then_axes) in ROUTES.items() if inside else ():
        ref = getattr(n, "r1_" + name)
        core_copies[name] = copy(getattr(n, "g_" + name).at[:, :, :, 1 - core], ref, sibling)
        left = AXES
        before[name] = []
        for i, axis in enumerate(first_axes):
            dst = getattr(n, f"r{i + 2}_{name}")
            before[name].append((ref, dst, left, axis, exchange(ref, dst, left, axis)))
            ref, left = dst, left_after(first_axes[: i + 1])
        whole = (slice(None),) * len(left)
        half = getattr(n, "half_" + name)
        pair_copies[name] = copy(ref.at[whole + half_of(name, 1)], half, partner)
        after[name] = []
        ref = half
        for i, axis in enumerate(then_axes):
            dst = getattr(n, "then_" + name)
            after[name].append((ref, dst, left, axis, exchange(ref, dst, left, axis)))
            ref, left = dst, left_after(first_axes + then_axes)
        straight[name] = []
        if left:
            first, second = left
            mine = 2 * bits[first] + bits[second]
            for offset in range(1, 4):
                place = (mine + offset) % 4
                target = me + STRIDES[first] * (place // 2 - bits[first])
                target = target + STRIDES[second] * (place % 2 - bits[second])
                straight[name].append(
                    copy(
                        ref.at[place // 2, place % 2],
                        getattr(n, "far_" + name).at[offset],
                        (me_pair, target),
                    )
                )

    def added(step):
        src, dst, left, axis, each = step
        each.wait()
        for place in places(len(left) - 1):
            mine = src[index_at(left, axis, bits[axis], place)].astype(F32)
            at = place or (slice(None),) * 2
            yield at, mine + dst[at].astype(F32)

    def core_start(name):
        if inside:
            core_copies[name].start()

    def hand_over(name, ref, sums):
        half = getattr(n, "half_" + name)
        for at, total in sums:
            total = total.astype(BF16)
            if name == DOWN:
                height = total.shape[0] // 2
                own, others = total[:height], total[height:]
            else:
                width = total.shape[1] // 2
                own, others = total[:, :width], total[:, width:]
            half[at] = own
            ref[at + half_of(name, 1)] = others
        go_on(name)
        pair_copies[name].start()

    def go_on(name):
        if after[name]:
            after[name][0][-1].start()
        else:
            for each in straight[name]:
                each.start()

    def core_done(name):
        if not inside:
            return
        core_copies[name].wait()
        g, r1 = getattr(n, "g_" + name), getattr(n, "r1_" + name)
        sums = (
            (place, g[place + (core,)].astype(F32) + r1[place].astype(F32)) for place in places(3)
        )
        if not before[name]:
            hand_over(name, r1, sums)
            return
        for at, total in sums:
            r1[at] = total.astype(BF16)
        before[name][0][-1].start()

    def axis_done(name, i=0):
        if not inside:
            return
        step = before[name][i]
        if i + 1 == len(before[name]):
            hand_over(name, step[1], added(step))
            return
        for at, total in added(step):
            step[1][at] = total.astype(BF16)
        before[name][i + 1][-1].start()

    def then_done(name):
        if not inside:
            return
        step = after[name][0]
        for at, total in added(step):
            if straight[name]:
                step[1][at] = total.astype(BF16)
            else:
                put(name, total)
        for each in straight[name]:
            each.start()

    def far_done(name):
        if not inside:
            return
        ref = after[name][0][1] if after[name] else getattr(n, "half_" + name)
        first, second = straight_axes(name)
        total = ref[bits[first], bits[second]].astype(F32)
        for offset in range(1, 4):
            straight[name][offset - 1].wait_recv()
            total += getattr(n, "far_" + name)[offset].astype(F32)
        put(name, total)

    def straight_axes(name):
        first_axes, then_axes = ROUTES[name]
        return left_after(first_axes + then_axes)

    gain_copies = []
    if inside:
        gain_copies.append(copy(n.gain_out.at[0], n.gain_in.at[0], sibling))
        for k in range(15):
            offset, pair = (k + 1) % 8, 0 if k < 7 else 1
            gain_copies.append(
                copy(
                    n.gain_out.at[1],
                    n.gain_in.at[1 + offset],
                    (pair, 2 * ((me // 2 + offset) % 8) + core),
                )
            )

    def gain_step():
        if not inside:
            return
        gain_copies[0].wait()
        n.gain_out[1] = n.gain_out[0] + n.gain_in[0]
        for each in gain_copies[1:]:
            each.start()

    def gain_owner(pair):
        if not inside:
            n.grad_gains[...] = n.gain_out[0]
            return
        total = n.gain_out[1] if pair == 0 else None
        for k in range(7) if pair == 0 else range(7, 15):
            gain_copies[1 + k].wait_recv()
            part = n.gain_in[1 + (k + 1) % 8]
            total = part if total is None else total + part
        n.grad_gains[...] = total

    def turned(ref):
        return jnp.transpose(rows_of(ref, 0, d))

    def product(left, right):
        return dot_nn(left[...], right.reshape(seq_count * LP, right.shape[2]))

    def blocks(value):
        return value.astype(BF16).reshape(2, 2, 2, 2, d // 16, value.shape[1])

    @pl.when(online)
    def _():
        n.turned_one[...] = turned(n.normed_one)
        n.turned_two[...] = turned(n.normed_two)
        n.turned_mixed[...] = turned(n.attended)
        aims_copy.wait_recv()
        differ = n.picked[...] - n.aims_in[...]
        weighted = jnp.where(real, seq_weight * differ, 0.0)
        n.coef[...] = weighted
        stat_first(jnp.sum(0.5 * weighted * jnp.where(real, differ, 0.0)))

        @pl.loop(0, seq_count)
        def _(s):
            backward_head(n, s)

        n.turned_ffn[...] = turned(n.grad_ffn)

        @pl.loop(0, ff // 512)
        def _(j):
            columns = pl.ds(pl.multiple_of(j * 512, 512), 512)
            value = product(n.turned_ffn, n.active[:, :, columns]).astype(BF16)
            for c in range(4):
                n.g_down[j // 2, j % 2, c // 2, c % 2] = value[:, 128 * c : 128 * c + 128]

        core_start(DOWN)
        value = None
        for s in range(seq_count):
            part = dot_nn(n.grad_q[s], n.final_low[s])
            value = part if value is None else value + part
        n.g_head[...] = blocks(jnp.transpose(value))
        core_start(HEAD)
        stat_next(0)

        @pl.loop(0, seq_count // 2)
        def _(t):
            backward_upper(n, 2 * t)

        core_done(DOWN)
        core_done(HEAD)

        def up_product(ref, tiles, first):
            @pl.loop(0, 2 * tiles)
            def _(j):
                columns = pl.ds(
                    pl.multiple_of((j // tiles) * (ff // 2) + first + (j % tiles) * 512, 512), 512
                )
                here = pl.ds(pl.multiple_of(j * 512, 512), 512)
                ref[:, :, :, :, :, here] = blocks(product(n.turned_two, n.slope[:, :, columns]))

        if inside:
            up_product(n.g_up_a, ff // 4 // 512, 0)
            core_start(UP_A)
            up_product(n.g_up_b, ff // 4 // 512, ff // 4)
            core_start(UP_B)
        else:
            up_product(n.g_up, ff // 2 // 512, 0)
        stat_next(1)

        @pl.loop(0, seq_count // 2)
        def _(t):
            backward_middle(n, 2 * t)

            @pl.when(t == 0)
            def _():
                core_done(UP_A)

            @pl.when(t == 1)
            def _():
                core_done(UP_B)

        n.g_out[...] = blocks(product(n.turned_mixed, n.grad_branch[...]))
        core_start(OUT)
        stat_next(2)

        @pl.loop(0, seq_count)
        def _(s):
            attend_back(n, [(s, pair) for pair in range(d // 128)], d)
            backward_states(n, s)
            state_copy(s).start()

            @pl.when(s == 0)
            def _():
                then_done(DOWN)
                axis_done(HEAD)
                core_done(OUT)

            @pl.when(s == 1)
            def _():
                stat_next(3)
                axis_done(UP_A)

            @pl.when(s == 2)
            def _():
                axis_done(UP_B)

            @pl.when(s == 3)
            def _():
                axis_done(OUT)

        n.gain_out[0, 0:1, :] = jnp.sum(n.gain_sums[0], axis=0, keepdims=True)
        n.gain_out[0, 1:2, :] = jnp.sum(n.gain_sums[1], axis=0, keepdims=True)
        n.gain_out[0, 2:8, :] = jnp.zeros((6, d), F32)

        def qkv_product(first, *names):
            width = 256 // len(names)
            for half in range(2):
                at = half * (3 * d // 2) + first
                value = blocks(product(n.turned_one, n.qkv[:, :, at : at + 256]))
                for i, name in enumerate(names):
                    getattr(n, "g_" + name)[..., half * width : (half + 1) * width] = value[
                        ..., i * width : (i + 1) * width
                    ]
            for name in names:
                core_start(name)

        if inside:
            gain_copies[0].start()
            qkv_product(0, QKV_0)
            qkv_product(256, QKV_1)
            core_done(QKV_0)
            qkv_product(512, QKV_2, QKV_3)
            core_done(QKV_1)
            axis_done(UP_A, 1)
            axis_done(UP_B, 1)
            core_done(QKV_2)
            core_done(QKV_3)
            gain_step()
            far_done(HEAD)
            far_done(DOWN)
            axis_done(QKV_0)
            axis_done(QKV_1)
            axis_done(QKV_2)
            axis_done(QKV_3)
            far_done(OUT)
            then_done(UP_A)
            then_done(UP_B)
        else:
            for first in range(0, 3 * d, 256):
                n.g_qkv[..., first : first + 256] = blocks(
                    product(n.turned_one, n.qkv[:, :, first : first + 256])
                )
        for s in range(0, seq_count, 2):
            n.state_out[s * L : (s + 2) * L] = without_pad(n.grad_states, s, d // 2)
            n.q_out[s * L : (s + 2) * L] = without_pad(n.q_rows, s, 128)
        gain_owner(0)
        for name in CHUNKS:
            far_done(name)
        q_copy.wait_send()
        for s in range(seq_count):
            state_copy(s).wait_send()
        for each in tuple(pair_copies.values()) + tuple(gain_copies[1:]):
            each.wait_send()

    @pl.when(jnp.logical_not(online))
    def _():
        stat_first(0.0)
        for i in range(4):
            stat_next(i)
        received = (DOWN, HEAD, UP_A, UP_B, OUT) + tuple(CHUNKS)

        def receive(name):
            if inside:
                pair_copies[name].wait_recv()
                go_on(name)

        receive(DOWN)
        q_copy.wait_recv()
        for s in range(0, seq_count, 2):
            n.q_out[s * L : (s + 2) * L] = without_pad(n.q_half, s, 128)
        then_done(DOWN)
        for name in received[1:]:
            receive(name)
            if name == UP_B:
                far_done(DOWN)
        for s in range(seq_count):
            state_copy(s).wait_recv()
            if s % 2:
                n.state_out[(s - 1) * L : (s + 1) * L] = without_pad(n.state_half, s - 1, d // 2)
        far_done(HEAD)
        far_done(OUT)
        then_done(UP_A)
        then_done(UP_B)
        gain_owner(1)
        for name in CHUNKS:
            far_done(name)
        aims_copy.wait_send()

    for sent in straight.values():
        for each in sent:
            each.wait_send()
    if inside:
        stat_next(4)
        n.stats[...] = n.stat_out[5]
    else:
        n.stats[...] = n.stat_out[0]
    assert used[0] <= SEMAPHORES


OUTPUTS = (
    "q_out",
    "state_out",
    GRAD_GAINS,
    "grad_qkv",
    "grad_out",
    "grad_up",
    GRAD_DOWN,
    "grad_head",
    NEW_GAINS,
    "new_qkv",
    "new_out",
    "new_up",
    "new_down",
    "new_head",
    STATS,
)


def finish_kernel(moved, worked, token_total, data_count, *refs):
    source = dict(zip(moved + worked, refs))
    result = dict(zip(OUTPUTS, refs[len(source) :]))
    sems = refs[-1]
    copies = [
        pltpu.make_async_copy(source[name], result[name], sems.at[i])
        for i, name in enumerate(moved)
    ]
    for copy in copies:
        copy.start()
    me_pair = lax.axis_index(PAIR)
    me = lax.axis_index(DP)
    for name in (GRAD_GAINS, NEW_GAINS):
        height = source[name].shape[1] // data_count
        here = source[name][:, pl.ds(pl.multiple_of(me * height // 128 * 128, 128), 128)]
        value = here[:, :height]
        for at in range(height, 128, height):
            value = jnp.where(me * height % 128 == at, here[:, at : at + height], value)
        result[name][...] = jnp.where(me_pair == 0, value[0:1], value[1:2])
    if GRAD_DOWN in worked:
        result[GRAD_DOWN][...] = jnp.transpose(source[GRAD_DOWN][...])
    stats = source[STATS]
    result[STATS][0] = stats[0, 0] / token_total
    result[STATS][1] = stats[0, 1] / token_total
    result[STATS][2] = stats[1, 0]
    result[STATS][3] = stats[0, 2] / token_total
    result[STATS][4] = stats[1, 1]
    for copy in copies:
        copy.wait()


def add_outside(out, params, pair_index, data_index, data_count):
    online = pair_index == 0
    other = 1 - pair_index

    def half(matrix, which):
        width = matrix.shape[1] // 2
        return lax.dynamic_slice_in_dim(matrix, which * width, width, 1)

    def piece(matrix, which):
        height = matrix.shape[0] // data_count
        return half(lax.dynamic_slice_in_dim(matrix, data_index * height, height, 0), which)

    def swapped(value):
        return lax.ppermute(value, PAIR, [(0, 1), (1, 0)])

    for name in TENSORS:
        grad = out["g_" + name].astype(F32)
        grad = grad.reshape((16,) + grad.shape[4:])
        if name == DOWN:
            grad = jnp.swapaxes(grad, 1, 2)
        grad = lax.psum_scatter(
            grad.reshape(-1, grad.shape[2]), DP, scatter_dimension=0, tiled=True
        )
        received = swapped(half(grad, other))
        out["grad_" + name] = jnp.where(online, half(grad, pair_index), received)
    gains = lax.psum(out[GRAD_GAINS], DP)
    out[GRAD_GAINS] = jnp.where(online, gains, swapped(gains))
    for name, weight in zip((GAINS, QKV, OUT, UP, DOWN, HEAD), params):
        if name == GAINS:
            weight = jnp.pad(weight.T, ((0, 6), (0, 0)))
            mine, received = weight.astype(F32), swapped(weight).astype(F32)
        else:
            mine = piece(weight, pair_index).astype(F32)
            received = swapped(piece(weight, other)).astype(F32)
        first, second = jnp.where(online, mine, received), jnp.where(online, received, mine)
        out["new_" + name] = second + SOFT_RATE * (first - second)
    sums = lax.psum(out[STATS][0:1], (PAIR, DP))
    bests = lax.pmax(out[STATS][1:2], (PAIR, DP))
    out[STATS] = jnp.concatenate([sums, bests])


def local(
    states, norm_gains, w_qkv, w_out, w_up, w_down, w_head, task_ids, chosen, reward, finished
):
    pair_index = lax.axis_index(PAIR)
    data_index = lax.axis_index(DP)
    data_count = lax.axis_size(DP)
    row_count, d = states.shape[1:]
    ff = w_up.shape[2]
    bin_count = w_head.shape[2]
    seq_count = row_count // L

    inside = data_count == 16
    rows = (seq_count, LP, d)
    inputs = dict(
        states=states[0],
        norm_gains=norm_gains[0].T,
        hbm_qkv=w_qkv[0],
        hbm_out=w_out[0],
        hbm_up=w_up[0],
        hbm_down=w_down[0],
        hbm_head=w_head[0],
        task_ids=task_ids,
        chosen=chosen,
        reward=reward,
        finished=finished,
    )
    if not inside:
        table = (task_ids[:, None] == jnp.arange(128, dtype=jnp.int32)[None, :]).astype(F32)
        inputs["counts"] = jnp.broadcast_to(
            lax.psum(jnp.sum(table, axis=0, keepdims=True), DP), (8, 128)
        )
    piece = {
        QKV: (d // 16, 3 * d),
        OUT: (d // 16, d),
        UP: (d // 16, ff),
        HEAD: (d // 16, bin_count),
        DOWN: (d, ff // 16),
    }
    halves = {
        name: (shape[0] // 2, shape[1]) if name == DOWN else (shape[0], shape[1] // 2)
        for name, shape in piece.items()
    }
    new_shapes = dict(halves, down=(ff // 16, d // 2))
    outputs = dict(
        q_out=((row_count, bin_count // 2), BF16),
        state_out=((row_count, d // 2), BF16),
        grad_gains=((8, d), F32),
        new_gains=((8, d), F32),
        stats=((8, 128), F32),
    )
    for name in TENSORS:
        if inside:
            outputs["grad_" + name] = (halves[name], F32)
            outputs["new_" + name] = (new_shapes[name], F32)
        else:
            outputs["g_" + name] = ((2, 2, 2, 2) + piece[name], BF16)
    scratch = dict(
        w_qkv=((d, 3 * d), BF16),
        w_out=((d, d), BF16),
        w_up=((d, ff), BF16),
        w_down=((ff, d), BF16),
        w_head=((d, bin_count), BF16),
        x=(rows, BF16),
        gains=((8, d), F32),
        flat=((8, -(-(row_count + LP - L) // 128) * 128), F32),
        aux=((seq_count, 8, LP), F32),
        table=((8, 128), F32),
        normed_one=(rows, BF16),
        qkv=((seq_count, LP, 3 * d), BF16),
        powers_0=((seq_count, d // 128) + (2 * BLOCKS[0][1], BLOCKS[0][2]), BF16),
        powers_1=((seq_count, d // 128) + (2 * BLOCKS[1][1], BLOCKS[1][2]), BF16),
        powers_2=((seq_count, d // 128) + (2 * BLOCKS[2][1], BLOCKS[2][2]), BF16),
        inverse_totals=(rows, F32),
        attended=(rows, BF16),
        middle=(rows, F32),
        normed_two=(rows, BF16),
        active=((seq_count, LP, ff), BF16),
        slope=((seq_count, LP, ff), BF16),
        final_low=(rows, BF16),
        q_rows=((seq_count, LP, bin_count), BF16),
        q_half=((seq_count, LP, bin_count // 2), BF16),
        picked=((8, LP), F32),
        tops=((8, LP), F32),
        coef=((8, LP), F32),
        aims_out=((8, LP), F32),
        aims_in=((8, LP), F32),
        grad_q=((seq_count, bin_count, LP), BF16),
        grad_ffn=(rows, BF16),
        turned_one=((d, seq_count * LP), BF16),
        turned_two=((d, seq_count * LP), BF16),
        turned_mixed=((d, seq_count * LP), BF16),
        turned_ffn=((d, seq_count * LP), BF16),
        state_half=((seq_count, LP, d // 2), BF16),
        gain_sums=((2, 8, d), F32),
        gain_out=((2, 8, d), F32),
        gain_in=((9, 8, d), F32),
        count_out=((2, 8, 128), F32),
        count_in=((8, 8, 128), F32),
        stat_out=((6, 8, 128), F32),
        stat_in=((5, 8, 128), F32),
        their_gains=((8, d), F32),
    )
    if inside:
        for name in TENSORS:
            scratch["their_" + name] = (new_shapes[name], BF16)
        for name, (first_axes, then_axes) in ROUTES.items():
            if name in CHUNKS:
                shape = (d // 16, 2 * (CHUNKS[name][1] - CHUNKS[name][0]))
            else:
                shape = (d // 16, ff // 2) if name in (UP_A, UP_B) else piece[name]
            half = halves[DOWN] if name == DOWN else (shape[0], shape[1] // 2)
            scratch["g_" + name] = (2, 2, 2, 2) + shape, BF16
            for i in range(len(first_axes) + 1):
                scratch[f"r{i + 1}_{name}"] = (2,) * (3 - i) + shape, BF16
            left = 3 - len(first_axes)
            scratch["half_" + name] = (2,) * left + half, BF16
            if then_axes:
                scratch["then_" + name] = (2,) * (left - 1) + half, BF16
            if left - len(then_axes) == 2:
                scratch["far_" + name] = (4,) + half, BF16
    names = list(inputs) + list(outputs) + list(scratch) + ["send_sem", "recv_sem", "load_sem"]
    in_vmem = pl.BlockSpec(memory_space=pltpu.VMEM)
    in_smem = pl.BlockSpec(memory_space=pltpu.SMEM)
    anywhere = pl.BlockSpec(memory_space=pl.ANY)
    raw = pl.pallas_call(
        functools.partial(layer_kernel, names, data_count, inside),
        out_shape=[jax.ShapeDtypeStruct(shape, dtype) for shape, dtype in outputs.values()],
        in_specs=[
            in_smem if name == "task_ids" else anywhere if name[:3] == "hbm" else in_vmem
            for name in inputs
        ],
        out_specs=[in_vmem] * len(outputs),
        scratch_shapes=[pltpu.VMEM(shape, dtype) for shape, dtype in scratch.values()]
        + [pltpu.SemaphoreType.DMA((SEMAPHORES,)), pltpu.SemaphoreType.DMA((SEMAPHORES,))]
        + [pltpu.SemaphoreType.DMA((5,))],
        compiler_params=pltpu.CompilerParams(
            collective_id=0, has_side_effects=True, vmem_limit_bytes=64 * 1024 * 1024 - 65536
        ),
        name="layer",
    )(*inputs.values())
    out = dict(zip(outputs, raw))
    if not inside:
        params = (norm_gains[0], w_qkv[0], w_out[0], w_up[0], w_down[0], w_head[0])
        add_outside(out, params, pair_index, data_index, data_count)
    moved = {name: out[name] for name in OUTPUTS if name not in (GRAD_GAINS, NEW_GAINS, STATS)}
    worked = {name: out[name] for name in (GRAD_GAINS, NEW_GAINS, STATS)}
    results = {name: jax.ShapeDtypeStruct(value.shape, value.dtype) for name, value in moved.items()}
    if inside:
        worked[GRAD_DOWN] = moved.pop(GRAD_DOWN)
        results[GRAD_DOWN] = jax.ShapeDtypeStruct((ff // data_count, d // 2), F32)
    results[GRAD_GAINS] = results[NEW_GAINS] = jax.ShapeDtypeStruct((1, d // data_count), F32)
    results[STATS] = jax.ShapeDtypeStruct((5,), F32)
    spec_of = {name: anywhere if name in moved else in_vmem for name in OUTPUTS}
    spec_of[STATS] = in_smem
    final = pl.pallas_call(
        functools.partial(
            finish_kernel, list(moved), list(worked), row_count * data_count, data_count
        ),
        out_shape=[results[name] for name in OUTPUTS],
        in_specs=[in_vmem] * (len(moved) + len(worked)),
        out_specs=[spec_of[name] for name in OUTPUTS],
        scratch_shapes=[
            pltpu.SemaphoreType.DMA((len(moved),)),
        ],
        name="finish",
    )(*moved.values(), *worked.values())
    final = dict(zip(OUTPUTS, final))
    for name in (GRAD_GAINS, NEW_GAINS):
        final[name] = final[name].T
    return tuple(final.values())


def solution(mesh):
    placed = (
        P(PAIR, DP, None),
        P(PAIR, None, None),
        P(PAIR, None, None),
        P(PAIR, None, None),
        P(PAIR, None, None),
        P(PAIR, None, None),
        P(PAIR, None, None),
        P(DP),
        P(DP),
        P(DP),
        P(DP),
    )
    return jax.shard_map(
        local,
        mesh=mesh,
        in_specs=placed,
        out_specs=(P(DP, PAIR),) * 14 + (P(),),
        check_vma=False,
    )
```
